32 devices in a mesh: dp: 32 (over z, y, x, core).
Axes of the slice: x: 2, y: 2, z: 4, core: 2. Of those that a mesh axis runs over, the one named last changes fastest.
Arguments:
- log_mels: bfloat16 [64, 3000, 80], P('dp'), may hold values from -6 to 6
- mask_spans: int32 [64, 4], P('dp'), may hold values from 0 to 2900, as said below
- live_slots: int32 [32], P('dp'), may hold values from 1 to 2, as said below
- first_conv: bfloat16 [3, 80, 512], P(None, None, 'dp'), may hold values from -0.375 to 0.375
- second_conv: bfloat16 [3, 512, 512], P(None, 'dp'), may hold values from -0.15625 to 0.15625
- biases: bfloat16 [8, 512], P(None, 'dp'), may hold values from -2 to 2
- norm_gains: bfloat16 [2, 512], P(None, 'dp'), may hold values from 0.099609375 to 1.8984375
- qkv_weight: bfloat16 [512, 3, 512], P('dp'), may hold values from -0.25 to 0.25
- out_weight: bfloat16 [512, 512], P('dp'), may hold values from -6 to 6
- up_weight: bfloat16 [512, 2048], P('dp'), may hold values from -0.25 to 0.25
- up_bias: bfloat16 [2048], P('dp'), may hold values from -2 to 2
- down_weight: bfloat16 [2048, 512], P('dp'), may hold values from -0.125 to 0.125
- cotangent: bfloat16 [64, 1500, 512], P('dp'), may hold values from -6 to 6
Outputs:
- encoded: bfloat16 [64, 1500, 512], P('dp')
- mel_grad: float32 [64, 3000, 80], P('dp')
- first_conv_grad: float32 [3, 80, 512], P(None, None, 'dp')
- second_conv_grad: float32 [3, 512, 512], P(None, 'dp')
- biases_grad: float32 [8, 512], P(None, 'dp')
- norm_gains_grad: float32 [2, 512], P(None, 'dp')
- qkv_weight_grad: float32 [512, 3, 512], P('dp')
- out_weight_grad: float32 [512, 512], P('dp')
- up_weight_grad: float32 [512, 2048], P('dp')
- up_bias_grad: float32 [2048], P('dp')
- down_weight_grad: float32 [2048, 512], P('dp')
- second_shift_grad: float32 [512], P('dp')
The draws below stay inside these ranges and needn't reach their ends.
Inputs may be any that keep to these rules, and one draw needn't show every extreme that they name: `mask_spans`: time width 1 to 100 with start plus width at most 3000; frequency width 1 to 27 with start plus width at most 80. `live_slots`: a device's live slots are its first ones; in every draw some device has 2 and some has 1.
All inputs are finite; a program needn't handle non-finite values.
Results may differ from the reference program's by a relative error of at most 0.014.
Values may be sent and summed in bfloat16 or wider, within the bound.
No kernel may reach another device: no remote copies, remote signals or barrier semaphores. Data moves between devices by JAX's collectives and lax.ppermute only.
A program may use at most 320 MiB of HBM per device.

```python
import math
import jax
import jax.numpy as jnp
from jax import lax

D = 512
FF = 2048
HEADS = 8
HEAD_DIM = 64
NMEL = 80
MELF = 3000
CLIP_DEV = 2
T_MASK = 100
F_MASK = 27
FR = 1500
CLIPS = 64
N_DP = 32


def draw_mask_spans(key, part):
    key = jax.random.fold_in(key, 1)
    keys = jax.random.split(key, 4)
    time_start = jax.random.randint(keys[0], (CLIPS,), 0, MELF - T_MASK + 1)
    time_width = jax.random.randint(keys[1], (CLIPS,), 1, T_MASK + 1)
    freq_start = jax.random.randint(keys[2], (CLIPS,), 0, NMEL - F_MASK + 1)
    freq_width = jax.random.randint(keys[3], (CLIPS,), 1, F_MASK + 1)
    return jnp.stack([time_start, time_width, freq_start, freq_width], axis=1).astype(jnp.int32)


def draw_live_slots(key, part):
    key = jax.random.fold_in(key, 2)
    keys = jax.random.split(key, 2)
    counts = jax.random.randint(keys[0], (N_DP,), 1, CLIP_DEV + 1)
    order = jax.random.permutation(keys[1], N_DP)
    counts = counts.at[order[0]].set(CLIP_DEV).at[order[1]].set(1)
    return counts.astype(jnp.int32)


def block_levels(rng, extent, cuts, least, high):
    factor_of = 1.0
    for position, blocks in cuts:
        steps = jax.random.uniform(jax.random.fold_in(jax.random.fold_in(rng, 6), position), (blocks,), jnp.float32, least / len(cuts), high / len(cuts))
        factor_of = factor_of * jnp.repeat(jnp.exp(steps), extent[position] // blocks).reshape((-1,) + (1,) * (len(extent) - 1 - position))
    return factor_of


def normal_values(key, shape, scale, bound, pieces=(), kind=jnp.bfloat16):
    drawn = jax.random.normal(key, shape, jnp.float32) * scale
    if len(pieces) > 0:
        drawn = block_levels(key, shape, pieces, -0.22, 0.18) * drawn
    return jnp.clip(drawn, min=-bound, max=bound).astype(kind)


def setup_inputs(seed: int = 0) -> dict:
    key_list = jax.random.split(jax.random.key(seed), 14)
    return {
        "log_mels": normal_values(key_list[0], (CLIPS, MELF, NMEL), 1.0, 6.0, ((0, 32),)),
        "mask_spans": draw_mask_spans(jax.random.fold_in(key_list[13], 71), 0),
        "live_slots": draw_live_slots(jax.random.fold_in(key_list[13], 71), 0),
        "first_conv": normal_values(key_list[3], (3, NMEL, D), (3 * NMEL) ** -0.5, 0.375, ((2, 32),)),
        "second_conv": normal_values(key_list[4], (3, D, D), (3 * D) ** -0.5, 0.15625, ((1, 32),)),
        "biases": normal_values(key_list[5], (8, D), 0.3, 2.0, ((1, 32),)),
        "norm_gains": jnp.clip(1.0 + 0.18 * jax.random.normal(key_list[6], (2, D), jnp.float32), 0.099609375, 1.8984375).astype(jnp.bfloat16),
        "qkv_weight": normal_values(key_list[7], (D, 3, D), D ** -0.5, 0.25, ((0, 32),)),
        "out_weight": normal_values(key_list[8], (D, D), (max(D * 4 // FR, 1)) ** -0.5, 6.0, ((0, 32),)),
        "up_weight": normal_values(key_list[9], (D, FF), D ** -0.5, 0.25, ((0, 32),)),
        "up_bias": normal_values(key_list[10], (FF,), 0.3, 2.0, ((0, 32),)),
        "down_weight": normal_values(key_list[11], (FF, D), FF ** -0.5, 0.125, ((0, 32),)),
        "cotangent": normal_values(key_list[12], (CLIPS, FR, D), 1.0, 6.0, ((0, 32),)),
    }


@jax.custom_vjp
def low(v):
    return lax.optimization_barrier(v.astype(jnp.bfloat16)).astype(jnp.float32)

@jax.custom_vjp
def low_back(v):
    return v

def low_keep(v):
    return (low(v), None)

def low_pass(kept, grad):
    return (grad,)

def back_keep(v):
    return (v, None)

def back_low(kept, grad):
    return (low(grad),)
low.defvjp(low_keep, low_pass)
low_back.defvjp(back_keep, back_low)
ln_eps = 1e-05

def product(left, right):
    return jnp.dot(left, right, precision=lax.Precision.HIGHEST, preferred_element_type=jnp.float32)

def round_both(inputs):
    return low(low_back(inputs))

def gelu_exact(inputs):
    return jax.nn.gelu(inputs, approximate=False)

def positions(frames, features):
    half_width = features // 2
    inverse_rate = jnp.exp(-(math.log(10000.0) / (half_width - 1)) * jnp.arange(half_width, dtype=jnp.float32))
    angles = jnp.arange(frames, dtype=jnp.float32)[:, None] * inverse_rate[None, :]
    return jnp.concatenate([jnp.sin(angles), jnp.cos(angles)], axis=1)

def normalize(inputs, gain_row, shift_row):
    row_mean = lax.optimization_barrier(jnp.mean(inputs, axis=-1, keepdims=True))
    centred = inputs - row_mean
    row_var = lax.optimization_barrier(jnp.mean(centred * centred, axis=-1, keepdims=True))
    return centred * lax.rsqrt(row_var + ln_eps) * gain_row + shift_row

def mel_mask(span_row, frames, bins_count):
    time_pos = jnp.arange(frames, dtype=jnp.int32)
    freq_pos = jnp.arange(bins_count, dtype=jnp.int32)
    time_keep = (time_pos < span_row[0]) | (time_pos >= span_row[0] + span_row[1])
    freq_keep = (freq_pos < span_row[2]) | (freq_pos >= span_row[2] + span_row[3])
    return (time_keep[:, None] & freq_keep[None, :]).astype(jnp.float32)

def head_attend(triple):
    queries, key_rows, value_rows = triple
    scores = low_back(product(queries, key_rows.T))
    weights = jax.nn.softmax(scores * HEAD_DIM ** (-0.5), axis=-1)
    return product(low(weights), value_rows)

def clip_forward(params, mel_clip, span_row, alive):
    first_conv, second_conv, biases, norm_gains, qkv_weight, out_weight, up_weight, up_bias, down_weight = params
    frames = mel_clip.shape[0]
    steps_out = frames // 2
    masked = mel_clip * mel_mask(span_row, frames, mel_clip.shape[1])
    padded = jnp.pad(masked, ((1, 1), (0, 0)))
    columns = jnp.concatenate([padded[:-2], padded[1:-1], padded[2:]], axis=1)
    first = low_back(product(columns, first_conv.reshape(-1, D)) + biases[0])
    active = low(gelu_exact(first))
    padded_act = jnp.pad(active, ((1, 1), (0, 0)))
    columns_two = jnp.concatenate([padded_act[0:frames:2], padded_act[1:frames + 1:2], padded_act[2:frames + 2:2]], axis=1)
    second = low_back(product(columns_two, second_conv.reshape(-1, D)) + biases[1])
    stream = gelu_exact(second) + positions(steps_out, D)
    normed = low(normalize(stream, norm_gains[0], biases[2]))
    bias_qkv = jnp.concatenate([biases[3], jnp.zeros((D,), jnp.float32), biases[4]])
    projected = round_both(product(normed, qkv_weight.reshape(D, 3 * D)) + bias_qkv)
    heads = projected.reshape(steps_out, 3, HEADS, HEAD_DIM).transpose(1, 2, 0, 3)
    attended = lax.map(jax.checkpoint(head_attend), (heads[0], heads[1], heads[2]))
    attended = round_both(attended.transpose(1, 0, 2).reshape(steps_out, D))
    after_attn = stream + low_back(product(attended, out_weight) + biases[5])
    normed_two = low(normalize(after_attn, norm_gains[1], biases[6]))
    hidden = low_back(product(normed_two, up_weight) + up_bias)
    result = after_attn + low_back(product(low(gelu_exact(hidden)), down_weight) + biases[7])
    return result * alive

def reference(log_mels, mask_spans, live_slots, first_conv, second_conv, biases, norm_gains, qkv_weight, out_weight, up_weight, up_bias, down_weight, cotangent):
    alive = (jnp.arange(CLIP_DEV, dtype=jnp.int32)[None, :] < live_slots[:, None]).astype(jnp.float32).reshape(-1)
    params = tuple((element.astype(jnp.float32) for element in (first_conv, second_conv, biases, norm_gains, qkv_weight, out_weight, up_weight, up_bias, down_weight)))
    mel_float = log_mels.astype(jnp.float32)
    clip_fn = jax.checkpoint(clip_forward)

    def forward(weights_in, mels_in):
        return lax.map(lambda element: clip_fn(weights_in, element[0], element[1], element[2]), (mels_in, mask_spans, alive))
    encoded, pull_back = jax.vjp(forward, params, mel_float)
    weight_grads, mel_grad = pull_back(cotangent.astype(jnp.float32))
    return (encoded.astype(jnp.bfloat16), mel_grad, weight_grads[0], weight_grads[1], weight_grads[2], weight_grads[3], weight_grads[4], weight_grads[5], weight_grads[6], weight_grads[7], weight_grads[8], weight_grads[2][6])
```

```python
import functools
import math

import jax
import jax.numpy as jnp
import numpy as np
from jax import lax
from jax.experimental import pallas as pl
from jax.experimental.pallas import tpu as pltpu
from jax.sharding import PartitionSpec as P

D = 512
FF = 2048
HEADS = 8
HEAD_DIM = 64
PAIRS = HEADS // 2
ROWS = 512
UNIT = 16
GROUPS = D // UNIT
LN_EPS = 1e-05
SCORE_SCALE = HEAD_DIM ** (-0.5)
LOG2E = math.log2(math.e)
VMEM = 60 * 1024 * 1024
BF = jnp.bfloat16
F32 = jnp.float32


def nn(left, right):
    return lax.dot_general(left, right, (((1,), (0,)), ((), ())), preferred_element_type=F32)


def tn(left, right):
    return lax.dot_general(left, right, (((0,), (0,)), ((), ())), preferred_element_type=F32)


def gelu_both(v):
    phi = 0.5 * lax.erf(v * math.sqrt(0.5)) + 0.5
    bell = jnp.exp2(v * v * (-0.5 * LOG2E))
    return v * phi, phi + v * bell * (1.0 / math.sqrt(2.0 * math.pi))


def row_stats(x):
    mean = jnp.mean(x, axis=-1, keepdims=True)
    centred = x - mean
    var = jnp.mean(centred * centred, axis=-1, keepdims=True)
    rate = lax.rsqrt(var + LN_EPS)
    return centred * rate, rate


def norm_back(hat, rate, gain, upstream):
    scaled = upstream * gain
    first = jnp.mean(scaled, axis=-1, keepdims=True)
    second = jnp.mean(scaled * hat, axis=-1, keepdims=True)
    return rate * (scaled - first - hat * second)


def col_sum(x):
    return jnp.sum(x, axis=0, keepdims=True)


def unit_rows(ref, start, count=UNIT):
    block = ref[:, start : start + count, :]
    return block.reshape(GROUPS * count, block.shape[2])


def prepare_kernel(frames, bins, spans, mels, ce, co, flat, tall):
    clip = pl.program_id(0)
    padded = ce.shape[1]
    place = lax.broadcasted_iota(jnp.int32, (bins, frames), 1)
    bin_at = lax.broadcasted_iota(jnp.int32, (bins, frames), 0)
    time_keep = (place < spans[clip, 0]) | (place >= spans[clip, 0] + spans[clip, 1])
    freq_keep = (bin_at < spans[clip, 2]) | (bin_at >= spans[clip, 2] + spans[clip, 3])

    @pl.when(clip == 0)
    def _():
        flat[...] = jnp.zeros_like(flat)
        tall[0:8, :] = jnp.zeros((8, 128), F32)
        tall[8 + 2 * padded :, :] = jnp.zeros((8, 128), F32)

    flat[0:bins, 0:frames] = jnp.where(time_keep & freq_keep, mels[0].astype(F32), 0.0)
    tall[8 : 8 + 2 * padded, :] = flat[...].T
    before, even, odd, after = (tall[pl.ds(7 + k, padded, stride=2), :] for k in range(4))
    lane = lax.broadcasted_iota(jnp.int32, (padded, 128), 1)
    wrap = 2 * bins - 128
    one = jnp.where(lane == wrap + bins, 1.0, 0.0)
    for out, taps in ((ce, (before, even, odd)), (co, (even, odd, after))):
        middle = pltpu.roll(taps[1], bins, 1)
        out[0, :, 0:128] = (taps[0] + jnp.where(lane >= bins, middle, 0.0)).astype(BF)
        last = pltpu.roll(taps[2], wrap, 1)
        out[0, :, 128:256] = (jnp.where(lane < wrap, middle, 0.0) + last + one).astype(BF)


def stem_kernel(
    order, ce, co, pos, mine, other, a_even, a_odd, d_even, d_odd, d_two, stream, w, vec, buf, first_t
):
    step = pl.program_id(1)
    rows = ce.shape[1]
    half = GROUPS // 2

    @pl.when((pl.program_id(0) == 0) & (step == 0))
    def _():
        for group in range(GROUPS):
            source = order[group]

            @pl.when(source < half)
            def _():
                w[group] = mine[source]

            @pl.when(source >= half)
            def _():
                w[group] = other[source - half]

        turned = unit_rows(w, 0)[:, 0:256].astype(F32).T
        vec[...] = turned[240:256, :]
        first_t[...] = turned.astype(BF)

    even, even_slope = gelu_both(nn(ce[0], first_t[...]))
    odd, odd_slope = gelu_both(nn(co[0], first_t[...]))
    even = even.astype(BF)
    a_even[0] = even
    d_even[0] = even_slope.astype(BF)
    d_odd[0] = odd_slope.astype(BF)
    odd_low = odd.astype(BF)
    a_odd[0] = odd_low

    @pl.when(step == 0)
    def _():
        buf[0:8, :] = jnp.zeros((8, D), F32)

    @pl.when(step > 0)
    def _():
        buf[0:8, :] = buf[rows : rows + 8, :]

    buf[8 : 8 + rows, :] = odd
    before = buf[7 : 7 + rows, :].astype(BF)
    second = nn(before, unit_rows(w, UNIT))
    second = second + nn(even, unit_rows(w, 2 * UNIT))
    second = second + nn(odd_low, unit_rows(w, 3 * UNIT)) + vec[1:2, :]
    wave, slope = gelu_both(second)
    d_two[0] = slope.astype(BF)
    stream[0] = wave + pos[...]


def project_kernel(stream, w, vec, qkv):
    hat, _ = row_stats(stream[0])
    normed = (hat * vec[8:9, :] + vec[2:3, :]).astype(BF)
    queries = nn(normed, unit_rows(w, 0)) + vec[3:4, :]
    qkv[0, :, 0:D] = queries.astype(BF)
    qkv[0, :, D : 2 * D] = nn(normed, unit_rows(w, UNIT)).astype(BF)
    qkv[0, :, 2 * D :] = (nn(normed, unit_rows(w, 2 * UNIT)) + vec[4:5, :]).astype(BF)


def head_mask(shape, head):
    lane = lax.broadcasted_iota(jnp.int32, shape, 1)
    return (lane >= head * HEAD_DIM) & (lane < (head + 1) * HEAD_DIM)


def row_mask(shape, head):
    row = lax.broadcasted_iota(jnp.int32, shape, 0)
    return (row >= head * HEAD_DIM) & (row < (head + 1) * HEAD_DIM)


def attend_kernel(
    length, q_ref, k_ref, v_ref, weights, attended, low_part, inverse, keys_t, wide, reach
):
    step = pl.program_id(2)
    rows = attended.shape[1]
    padded = k_ref.shape[1]
    edge = length // 128 * 128

    def longest(x):
        return jnp.max(jnp.sum(jnp.square(x.astype(F32)), axis=1))

    @pl.when(step == 0)
    def _():
        turned = k_ref[0].T
        for head in range(2):
            own = turned[head * HEAD_DIM : (head + 1) * HEAD_DIM, :]
            keys_t[head, 0:HEAD_DIM, :] = own
            keys_t[head, HEAD_DIM : 2 * HEAD_DIM, :] = own
        wide[:, 0 : 2 * HEAD_DIM] = v_ref[0]
        wide[:, 2 * HEAD_DIM :] = jnp.ones((padded, 2 * HEAD_DIM), BF)
        reach[0] = longest(q_ref[0]) * longest(k_ref[0])

    factor = SCORE_SCALE * LOG2E
    calm = reach[0] < (60.0 / factor) ** 2
    scaled = q_ref[0, pl.ds(pl.multiple_of(step * rows, rows), rows), :].astype(F32) * factor
    large = scaled.astype(BF)
    small = pltpu.roll(scaled - large.astype(F32), HEAD_DIM, 1).astype(BF)
    first = head_mask(large.shape, 0)
    queries = (jnp.where(first, large, small), jnp.where(first, small, large))

    def attend(shift):
        outs = []
        rates = []
        for head in range(2):
            scores = nn(queries[head], keys_t[head])
            body, rest = scores[:, :edge], scores[:, edge:]
            place = lax.broadcasted_iota(jnp.int32, rest.shape, 1) + edge
            rest = jnp.where(place < length, rest, -1e30)
            if shift:
                top = jnp.maximum(
                    jnp.max(body, axis=1, keepdims=True), jnp.max(rest, axis=1, keepdims=True)
                )
                body, rest = body - top, rest - top
            soft = jnp.concatenate([jnp.exp2(body).astype(BF), jnp.exp2(rest).astype(BF)], axis=1)
            weights[0, head] = soft
            mixed = nn(soft, wide[...])
            rate = 1.0 / mixed[:, 2 * HEAD_DIM :]
            outs.append(mixed[:, : 2 * HEAD_DIM] * rate)
            rates.append(rate)
        pick = head_mask(outs[0].shape, 0)
        both = jnp.where(pick, outs[0], outs[1])
        high = both.astype(BF)
        attended[0] = high
        low_part[0] = (both - high.astype(F32)).astype(BF)
        inverse[0] = jnp.where(pick, rates[0], rates[1])

    @pl.when(calm)
    def _():
        attend(False)

    @pl.when(jnp.logical_not(calm))
    def _():
        attend(True)


def attend_back_kernel(
    aliased, weights, grad_ref, att_ref, low_ref, inv_ref, q_ref, k_ref, v_ref, *rest
):
    rest = rest[3 * aliased :]
    dq, dk, dv, dk_sum, dv_sum, right = rest
    step = pl.program_id(1)
    scaled_low = (grad_ref[0].astype(F32) * inv_ref[0]).astype(BF)
    prod = scaled_low.astype(F32) * (att_ref[0].astype(F32) + low_ref[0].astype(F32))
    lane = lax.broadcasted_iota(jnp.int32, prod.shape, 1)
    dots = jnp.zeros(prod.shape, F32)
    for head in range(2):
        dot = -jnp.sum(jnp.where(head_mask(prod.shape, head), prod, 0.0), axis=1, keepdims=True)
        high = dot.astype(BF).astype(F32)
        dots = jnp.where(lane == 2 * head, high, dots)
        dots = jnp.where(lane == 2 * head + 1, dot - high, dots)
    left = jnp.concatenate([scaled_low, dots.astype(BF)], axis=1)
    q_turn = q_ref[0].T
    g_turn = scaled_low.T

    @pl.when(step == 0)
    def _():
        dk_sum[...] = jnp.zeros_like(dk_sum)
        dv_sum[...] = jnp.zeros_like(dv_sum)
        turned = v_ref[0].T
        zero = jnp.zeros_like(turned)
        row = lax.broadcasted_iota(jnp.int32, turned.shape, 0)
        for head in range(2):
            right[head, 0:128, :] = jnp.where(row_mask(turned.shape, head), turned, zero)
            right[head, 128:256, :] = jnp.where(
                (row == 2 * head) | (row == 2 * head + 1), zero + 1, zero
            )

    outs = []
    for head in range(2):
        soft = weights[0, head]
        score_grad = (soft.astype(F32) * nn(left, right[head])).astype(BF)
        outs.append(nn(score_grad, k_ref[0]))
        span = slice(head * HEAD_DIM, (head + 1) * HEAD_DIM)
        dk_sum[span, :] += nn(q_turn[span, :], score_grad)
        dv_sum[span, :] += nn(g_turn[span, :], soft)
    pick = head_mask(outs[0].shape, 0)
    dq[0] = (jnp.where(pick, outs[0], outs[1]) * SCORE_SCALE).astype(BF)

    @pl.when(step == pl.num_programs(1) - 1)
    def _():
        dk[0] = (dk_sum[...].T * SCORE_SCALE).astype(BF)
        dv[0] = dv_sum[...].T.astype(BF)


def mlp_kernel(
    length, live, att, stream, cot, w, vec, up_bias,
    encoded, att_grad, state_grad, packed, sums, up_sums,
    out_acc, up_acc, down_acc, out_t, up_t, down_t, mixed,
):
    step = pl.program_id(0)
    clip = pl.program_id(1)
    clips = pl.num_programs(1)
    rows = cot.shape[1]
    alive = clip < live[0]

    @pl.when((clip == 0) & (step == 0))
    def _():
        out_acc[...] = jnp.zeros_like(out_acc)
        up_acc[...] = jnp.zeros_like(up_acc)
        down_acc[...] = jnp.zeros_like(down_acc)
        sums[...] = jnp.zeros_like(sums)
        up_sums[...] = jnp.zeros_like(up_sums)
        out_t[...] = unit_rows(w, 0).T
        for part in range(FF // D):
            up_t[part] = unit_rows(w, (1 + part) * UNIT).T
            down_t[part] = unit_rows(w, 5 * UNIT, 4 * UNIT)[part * D : (part + 1) * D, :].T

    place = lax.broadcasted_iota(jnp.int32, (rows, D), 0) + step * rows
    reach = jnp.where(alive, length, 0)
    cot_float = jnp.where(place < reach, cot[0].astype(F32), 0.0)
    cot_low = cot_float.astype(BF)
    attended = att[0]
    out_w = unit_rows(w, 0)
    after = stream[0] + nn(attended, out_w) + vec[5:6, :]
    hat, rate = row_stats(after)
    normed = (hat * vec[9:10, :] + vec[6:7, :]).astype(BF)
    normed_turn = normed.T
    cot_turn = cot_low.T
    result = after + vec[7:8, :]
    normed_grad = jnp.zeros((rows, D), F32)
    down_all = unit_rows(w, 5 * UNIT, 4 * UNIT)
    for part in range(FF // D):
        span = slice(part * D, (part + 1) * D)
        up_w = unit_rows(w, (1 + part) * UNIT)
        down_w = down_all[span, :]
        hidden = nn(normed, up_w) + up_bias[0:1, span]
        gated, slope = gelu_both(hidden)
        gated = gated.astype(BF)
        result = result + nn(gated, down_w)
        hidden_grad = nn(cot_low, down_t[part]) * slope
        up_sums[0:1, span] += col_sum(hidden_grad)
        hidden_grad = hidden_grad.astype(BF)
        normed_grad = normed_grad + nn(hidden_grad, up_t[part])
        up_acc[part] += nn(normed_turn, hidden_grad)
        down_acc[part] += nn(cot_turn, gated)
    result = jnp.where(alive, result, 0.0)
    slots = mixed.shape[1] // rows
    for slot in range(slots):

        @pl.when(clip == slot)
        def _():
            for part in range(D // 128):
                lanes = slice(part * 128, (part + 1) * 128)
                mixed[part, pl.ds(slot, rows, stride=slots), :] = result[:, lanes]

    @pl.when(clip == clips - 1)
    def _():
        for part in range(D // 128):
            encoded[:, part * 128 : (part + 1) * 128] = mixed[part].astype(BF)

    total = cot_float + norm_back(hat, rate, vec[9:10, :], normed_grad)
    state_grad[0] = total
    sums[0:1, :] += col_sum(total)
    sums[1:2, :] += col_sum(normed_grad)
    sums[2:3, :] += col_sum(cot_float)
    sums[3:4, :] += col_sum(normed_grad * hat)
    low = total.astype(BF)
    att_grad[0] = nn(low, out_t[...]).astype(BF)
    out_acc[...] += tn(attended, low)

    @pl.when((clip == clips - 1) & (step == pl.num_programs(0) - 1))
    def _():
        packed[:, 0:UNIT, :] = out_acc[...].astype(BF).reshape(GROUPS, UNIT, D)
        for part in range(FF // D):
            at = (1 + part) * UNIT
            packed[:, at : at + UNIT, :] = up_acc[part].astype(BF).reshape(GROUPS, UNIT, D)
            owners = GROUPS // (FF // D)
            packed[part * owners : (part + 1) * owners, 5 * UNIT : 9 * UNIT, :] = (
                down_acc[part].T.astype(BF).reshape(owners, 4 * UNIT, D)
            )


def qkv_back_kernel(
    dq, dk, dv, stream, state_grad, d_two, w, vec, second_grad, packed, sums, acc, turned
):
    clip = pl.program_id(0)
    step = pl.program_id(1)

    @pl.when((clip == 0) & (step == 0))
    def _():
        acc[...] = jnp.zeros_like(acc)
        sums[...] = jnp.zeros_like(sums)
        for part in range(3):
            turned[part] = unit_rows(w, part * UNIT).T

    parts = (dq[0], dk[0], dv[0])
    hat, rate = row_stats(stream[0])
    normed_turn = (hat * vec[8:9, :] + vec[2:3, :]).astype(BF).T
    normed_grad = nn(parts[0], turned[0])
    normed_grad = normed_grad + nn(parts[1], turned[1])
    normed_grad = normed_grad + nn(parts[2], turned[2])
    for part in range(3):
        acc[part] += nn(normed_turn, parts[part])
    total = state_grad[0] + norm_back(hat, rate, vec[8:9, :], normed_grad)
    grad = total * d_two[0].astype(F32)
    second_grad[0] = grad.astype(BF)
    sums[0:1, :] += col_sum(grad)
    sums[1:2, :] += col_sum(normed_grad)
    sums[2:3, :] += col_sum(parts[0].astype(F32))
    sums[3:4, :] += col_sum(parts[2].astype(F32))
    sums[4:5, :] += col_sum(normed_grad * hat)

    @pl.when((clip == pl.num_programs(0) - 1) & (step == pl.num_programs(1) - 1))
    def _():
        for part in range(3):
            packed[:, part * UNIT : (part + 1) * UNIT, :] = (
                acc[part].astype(BF).reshape(GROUPS, UNIT, D)
            )


def stem_back_kernel(
    grad_ref, a_even, a_odd, d_even, d_odd, ce, co, w, qkv_sums, mlp_sums, up_cols,
    f_even, f_odd, packed, acc, w_acc, buf, extra, turned,
):
    clip = pl.program_id(0)
    step = pl.program_id(1)
    rows = grad_ref.shape[1]

    @pl.when((clip == 0) & (step == 0))
    def _():
        acc[...] = jnp.zeros_like(acc)
        w_acc[...] = jnp.zeros_like(w_acc)
        for part in range(3):
            turned[part] = unit_rows(w, (1 + part) * UNIT).T

    @pl.when(step == 0)
    def _():
        buf[rows : rows + 8, :] = jnp.zeros((8, D), F32)

    @pl.when(step > 0)
    def _():
        buf[rows : rows + 8, :] = buf[0:8, :]

    grad = grad_ref[0]
    buf[0:rows, :] = grad.astype(F32)
    after = buf[1 : rows + 1, :].astype(BF)
    even_grad = nn(grad, turned[1])
    odd_grad = nn(grad, turned[2]) + nn(after, turned[0])
    even_grad = (even_grad * d_even[0].astype(F32)).astype(BF)
    odd_grad = (odd_grad * d_odd[0].astype(F32)).astype(BF)
    f_even[0] = even_grad
    f_odd[0] = odd_grad
    odd_turn = a_odd[0].T
    acc[0] += nn(odd_turn, after)
    acc[1] += nn(a_even[0].T, grad)
    acc[2] += nn(odd_turn, grad)
    w_acc[...] += tn(even_grad, ce[0]) + tn(odd_grad, co[0])

    @pl.when((clip == pl.num_programs(0) - 1) & (step == pl.num_programs(1) - 1))
    def _():
        for part in range(3):
            at = (1 + part) * UNIT
            packed[:, at : at + UNIT, :] = acc[part].astype(BF).reshape(GROUPS, UNIT, D)
        extra[...] = jnp.zeros_like(extra)
        extra[113:117, :] = qkv_sums[0:4, :]
        extra[117:120, :] = mlp_sums[0:3, :]
        extra[120:121, :] = qkv_sums[4:5, :]
        extra[121:122, :] = mlp_sums[3:4, :]
        extra[122:126, :] = up_cols[0:4, :]
        small = jnp.concatenate(
            [w_acc[:, 0:128], w_acc[:, 128:256] + extra[...].T, jnp.zeros((D, D - 256), F32)],
            axis=1,
        )
        packed[:, 0:UNIT, :] = small.astype(BF).reshape(GROUPS, UNIT, D)


def mel_kernel(
    frames, bins, spans, f_even, f_odd, w, held, out, passed, mel_w, down_buf, up_buf, tall
):
    del held, passed
    clip = pl.program_id(0)
    rows = f_even.shape[1]

    @pl.when(clip == 0)
    def _():
        first_w = unit_rows(w, 0)[:, 0:256].astype(F32)
        lane = lax.broadcasted_iota(jnp.int32, (D, 128), 1)
        low, high = first_w[:, 0:128], first_w[:, 128:256]
        wrap = 2 * bins - 128
        keep = lane < bins
        zero = jnp.zeros((D, 128), BF)
        taps = (
            jnp.where(keep, low, 0.0).astype(BF),
            jnp.where(
                keep,
                jnp.where(lane < 128 - bins, pltpu.roll(low, 128 - bins, 1), pltpu.roll(high, 128 - bins, 1)),
                0.0,
            ).astype(BF),
            jnp.where(keep, pltpu.roll(high, 128 - wrap, 1), 0.0).astype(BF),
        )
        for at, tap in enumerate((taps[1], taps[2], zero, taps[0])):
            mel_w[0:D, at * 128 : (at + 1) * 128] = tap
        for at, tap in enumerate((taps[0], taps[1], taps[2], zero)):
            mel_w[D : 2 * D, at * 128 : (at + 1) * 128] = tap

    full = nn(f_even[0], mel_w[0:D, :]) + nn(f_odd[0], mel_w[D : 2 * D, :])
    down_buf[0:8, :] = jnp.zeros((8, 128), F32)
    down_buf[8 : 8 + rows, :] = full[:, 256:384]
    up_buf[0:rows, :] = full[:, 384:512]
    up_buf[rows : rows + 8, :] = jnp.zeros((8, 128), F32)
    tall[pl.ds(0, rows, stride=2), :] = full[:, 0:128] + down_buf[7 : 7 + rows, :]
    tall[pl.ds(1, rows, stride=2), :] = full[:, 128:256] + up_buf[1 : rows + 1, :]
    turned = tall[...].T[0:bins, 0:frames]
    place = lax.broadcasted_iota(jnp.int32, (bins, frames), 1)
    bin_at = lax.broadcasted_iota(jnp.int32, (bins, frames), 0)
    time_keep = (place < spans[clip, 0]) | (place >= spans[clip, 0] + spans[clip, 1])
    freq_keep = (bin_at < spans[clip, 2]) | (bin_at >= spans[clip, 2] + spans[clip, 3])
    out[0] = jnp.where(time_keep & freq_keep, turned, 0.0)


def whole(shape):
    return pl.BlockSpec(shape, lambda *_: (0,) * len(shape))


def params(semantics):
    return pltpu.CompilerParams(
        vmem_limit_bytes=VMEM, dimension_semantics=("arbitrary",) * semantics
    )


def cost(flops, moved):
    return pl.CostEstimate(flops=int(flops), bytes_accessed=int(moved), transcendentals=0)


SMEM = pl.BlockSpec(memory_space=pltpu.SMEM)


def ordered(kernel, operands, specs, token):
    if token is None:
        return kernel, operands, specs
    place = len(specs)

    def inner(*refs):
        kernel(*refs[:place], *refs[place + 1 :])

    return inner, list(operands) + [token], list(specs) + [whole(token.shape)]


def call_prepare(spans, mels, padded):
    clips, bins, frames = mels.shape
    row = pl.BlockSpec((1, padded, 256), lambda c: (c, 0, 0))
    return pl.pallas_call(
        functools.partial(prepare_kernel, frames, bins),
        grid=(clips,),
        in_specs=[SMEM, pl.BlockSpec((1, bins, frames), lambda c: (c, 0, 0))],
        out_specs=[row, row],
        out_shape=[jax.ShapeDtypeStruct((clips, padded, 256), BF)] * 2,
        scratch_shapes=[
            pltpu.VMEM((128, 2 * padded), F32),
            pltpu.VMEM((2 * padded + 16, 128), F32),
        ],
        compiler_params=params(1),
        cost_estimate=cost(8e9, clips * padded * 2048),
        name="mel_prepare",
    )(spans, mels)


def call_stem(order, ce, co, pos, mine, other):
    clips, padded, _ = ce.shape
    row = lambda width: pl.BlockSpec((1, ROWS, width), lambda c, i: (c, i, 0))
    out = lambda width, kind: jax.ShapeDtypeStruct((clips, padded, width), kind)
    return pl.pallas_call(
        stem_kernel,
        grid=(clips, padded // ROWS),
        in_specs=[
            SMEM, row(256), row(256), pl.BlockSpec((ROWS, D), lambda c, i: (i, 0)),
            whole(mine.shape), whole(other.shape),
        ],
        out_specs=[row(D)] * 6 + [whole((GROUPS, 4 * UNIT, D)), whole((UNIT, D))],
        out_shape=[out(D, BF)] * 5 + [
            out(D, F32),
            jax.ShapeDtypeStruct((GROUPS, 4 * UNIT, D), BF),
            jax.ShapeDtypeStruct((UNIT, D), F32),
        ],
        scratch_shapes=[pltpu.VMEM((ROWS + 8, D), F32), pltpu.VMEM((256, D), BF)],
        compiler_params=params(2),
        cost_estimate=cost(24e9, clips * padded * 9000),
        name="stem_forward",
    )(order, ce, co, pos, mine, other)


def call_project(stream, w, vec):
    clips, padded, _ = stream.shape
    row = lambda width: pl.BlockSpec((1, ROWS, width), lambda c, i: (c, i, 0))
    return pl.pallas_call(
        project_kernel,
        grid=(clips, padded // ROWS),
        in_specs=[row(D), whole(w.shape), whole(vec.shape)],
        out_specs=row(3 * D),
        out_shape=jax.ShapeDtypeStruct((clips, padded, 3 * D), BF),
        compiler_params=params(2),
        cost_estimate=cost(10e9, clips * padded * 5000),
        name="projection_forward",
    )(stream, w, vec)


def call_attend(qkv, length):
    clips, padded, _ = qkv.shape
    query = pl.BlockSpec((1, ROWS, 128), lambda c, h, i: (c, i, h))
    whole_rows = lambda at: pl.BlockSpec((1, padded, 128), lambda c, h, i: (c, 0, at + h))
    return pl.pallas_call(
        functools.partial(attend_kernel, length),
        grid=(clips, PAIRS, padded // ROWS),
        in_specs=[whole_rows(0), whole_rows(PAIRS), whole_rows(2 * PAIRS)],
        out_specs=[
            pl.BlockSpec((1, 2, ROWS, padded), lambda c, h, i: (c, h, i, 0)),
            query,
            query,
            query,
        ],
        out_shape=[
            jax.ShapeDtypeStruct((clips, HEADS, padded, padded), BF),
            jax.ShapeDtypeStruct((clips, padded, D), BF),
            jax.ShapeDtypeStruct((clips, padded, D), BF),
            jax.ShapeDtypeStruct((clips, padded, D), F32),
        ],
        scratch_shapes=[
            pltpu.VMEM((2, 128, padded), BF),
            pltpu.VMEM((padded, 256), BF),
            pltpu.SMEM((1,), F32),
        ],
        compiler_params=params(3),
        cost_estimate=cost(50e9, clips * padded * padded * 16),
        name="attention_forward",
    )(qkv, qkv, qkv)


def call_attend_back(clip, weights, grad, attended, low_part, inverse, qkv, earlier, token):
    clips, padded, _ = qkv.shape
    query = pl.BlockSpec((1, ROWS, 128), lambda h, i: (clip, i, h))
    keys = lambda at: pl.BlockSpec((1, padded, 128), lambda h, i: (clip, 0, at + h))
    shape = jax.ShapeDtypeStruct((clips, padded, D), BF)
    aliases = {}
    extra = []
    extra_specs = []
    if earlier is not None:
        extra = list(earlier)
        extra_specs = [pl.BlockSpec(memory_space=pl.ANY)] * 3
        aliases = {8: 0, 9: 1, 10: 2}
    kernel, operands, specs = ordered(
        functools.partial(attend_back_kernel, 0 if earlier is None else 1),
        [weights, grad, attended, low_part, inverse, qkv, qkv, qkv] + extra,
        [
            pl.BlockSpec((1, 2, ROWS, padded), lambda h, i: (clip, h, i, 0)),
            query, query, query, query, query, keys(PAIRS), keys(2 * PAIRS),
        ] + extra_specs,
        token,
    )
    return pl.pallas_call(
        kernel,
        grid=(PAIRS, padded // ROWS),
        in_specs=specs,
        out_specs=[query, keys(0), keys(0)],
        out_shape=[shape] * 3,
        scratch_shapes=[pltpu.VMEM((128, padded), F32)] * 2
        + [pltpu.VMEM((2, 256, padded), BF)],
        input_output_aliases=aliases,
        compiler_params=params(2),
        cost_estimate=cost(40e9, padded * padded * 16),
        name="attention_backward",
    )(*operands)


def call_mlp(live, attended, stream, cot, w, vec, up_bias):
    clips, padded, _ = attended.shape
    row = pl.BlockSpec((1, ROWS, D), lambda i, c: (c, i, 0))
    return pl.pallas_call(
        functools.partial(mlp_kernel, cot.shape[1]),
        grid=(padded // ROWS, clips),
        in_specs=[SMEM, row, row, row, whole(w.shape), whole(vec.shape), whole(up_bias.shape)],
        out_specs=[
            pl.BlockSpec((ROWS * clips, D), lambda i, c: (i, 0)), row, row,
            whole((GROUPS, 9 * UNIT, D)), whole((8, D)), whole((8, FF)),
        ],
        out_shape=[
            jax.ShapeDtypeStruct((cot.shape[1] * clips, D), BF),
            jax.ShapeDtypeStruct(attended.shape, BF),
            jax.ShapeDtypeStruct(attended.shape, F32),
            jax.ShapeDtypeStruct((GROUPS, 9 * UNIT, D), BF),
            jax.ShapeDtypeStruct((8, D), F32),
            jax.ShapeDtypeStruct((8, FF), F32),
        ],
        scratch_shapes=[
            pltpu.VMEM((D, D), F32),
            pltpu.VMEM((FF // D, D, D), F32),
            pltpu.VMEM((FF // D, D, D), F32),
            pltpu.VMEM((D, D), BF),
            pltpu.VMEM((FF // D, D, D), BF),
            pltpu.VMEM((FF // D, D, D), BF),
            pltpu.VMEM((D // 128, ROWS * clips, 128), F32),
        ],
        compiler_params=params(2),
        cost_estimate=cost(60e9, clips * padded * 8000),
        name="mlp_both_ways",
    )(live, attended, stream, cot, w, vec, up_bias)


def call_qkv_back(grads, stream, state_grad, d_two, w, vec, token):
    clips, padded, _ = stream.shape
    row = pl.BlockSpec((1, ROWS, D), lambda c, i: (c, i, 0))
    kernel, operands, specs = ordered(
        qkv_back_kernel,
        [*grads, stream, state_grad, d_two, w, vec],
        [row] * 6 + [whole(w.shape), whole(vec.shape)],
        token,
    )
    return pl.pallas_call(
        kernel,
        grid=(clips, padded // ROWS),
        in_specs=specs,
        out_specs=[row, whole((GROUPS, 3 * UNIT, D)), whole((8, D))],
        out_shape=[
            jax.ShapeDtypeStruct(stream.shape, BF),
            jax.ShapeDtypeStruct((GROUPS, 3 * UNIT, D), BF),
            jax.ShapeDtypeStruct((8, D), F32),
        ],
        scratch_shapes=[pltpu.VMEM((3, D, D), F32), pltpu.VMEM((3, D, D), BF)],
        compiler_params=params(2),
        cost_estimate=cost(18e9, clips * padded * 9000),
        name="projection_backward",
    )(*operands)


def call_stem_back(second_grad, a_even, a_odd, d_even, d_odd, ce, co, w, sums, token):
    clips, padded, _ = second_grad.shape
    last = padded // ROWS - 1
    row = lambda width: pl.BlockSpec((1, ROWS, width), lambda c, i: (c, last - i, 0))
    kernel, operands, specs = ordered(
        stem_back_kernel,
        [second_grad, a_even, a_odd, d_even, d_odd, ce, co, w, *sums],
        [row(D)] * 5 + [row(256)] * 2 + [whole(w.shape)] + [whole((8, D))] * 3,
        token,
    )
    return pl.pallas_call(
        kernel,
        grid=(clips, padded // ROWS),
        in_specs=specs,
        out_specs=[row(D), row(D), whole((GROUPS, 4 * UNIT, D))],
        out_shape=[
            jax.ShapeDtypeStruct(second_grad.shape, BF),
            jax.ShapeDtypeStruct(second_grad.shape, BF),
            jax.ShapeDtypeStruct((GROUPS, 4 * UNIT, D), BF),
        ],
        scratch_shapes=[
            pltpu.VMEM((3, D, D), F32),
            pltpu.VMEM((D, 256), F32),
            pltpu.VMEM((ROWS + 8, D), F32),
            pltpu.VMEM((128, D), F32),
            pltpu.VMEM((3, D, D), BF),
        ],
        compiler_params=params(2),
        cost_estimate=cost(18e9, clips * padded * 9000),
        name="stem_backward",
    )(*operands)


def call_mel(spans, f_even, f_odd, w, encoded, frames, bins, token):
    clips, padded, _ = f_even.shape
    row = pl.BlockSpec((1, padded, D), lambda c: (c, 0, 0))
    kernel, operands, specs = ordered(
        functools.partial(mel_kernel, frames, bins),
        [spans, f_even, f_odd, w, encoded],
        [SMEM, row, row, whole(w.shape), pl.BlockSpec(memory_space=pl.ANY)],
        token,
    )
    return pl.pallas_call(
        kernel,
        grid=(clips,),
        in_specs=specs,
        out_specs=[
            pl.BlockSpec((1, bins, frames), lambda c: (c, 0, 0)),
            pl.BlockSpec(memory_space=pl.ANY),
        ],
        out_shape=[
            jax.ShapeDtypeStruct((clips, bins, frames), F32),
            jax.ShapeDtypeStruct(encoded.shape, encoded.dtype),
        ],
        input_output_aliases={4: 1},
        scratch_shapes=[
            pltpu.VMEM((2 * D, D), BF),
            pltpu.VMEM((padded + 8, 128), F32),
            pltpu.VMEM((padded + 8, 128), F32),
            pltpu.VMEM((2 * padded, 128), F32),
        ],
        compiler_params=params(1),
        cost_estimate=cost(8e9, clips * padded * 4000),
        name="mel_backward",
    )(*operands)


def swap(x, mask, count):
    return lax.ppermute(x, "dp", [(i, i ^ mask) for i in range(count)])


def stages(count):
    bits = count.bit_length() - 1
    return [(0, 1)] + [(at, min(2, bits - at)) for at in range(1, bits, 2)]


def gather_xor(x, count, index):
    held = x[None]
    where = jnp.zeros((count,), jnp.int32)
    apart = jnp.arange(count, dtype=jnp.int32) ^ index
    token = None
    parts = None
    for first, many in reversed(stages(count)):
        if parts is not None:
            held = jnp.concatenate(parts)
        where = where + ((apart >> first) & ((1 << many) - 1)) * held.shape[0]
        parts = [held] + [swap(held, rel << first, count) for rel in range(1, 1 << many)]
        if first > 0:
            token = parts[-1]
    return parts, where, token


class Scatter:
    def __init__(self, x, count, index, pairs):
        self.held, self.count, self.index = x, count, index
        self.plan = stages(count) if pairs else [(b, 1) for b in range(count.bit_length() - 1)]

    def step(self):
        if not self.plan:
            return None
        first, many = self.plan.pop(0)
        radix = 1 << many
        held = self.held
        split = held.reshape((held.shape[0] // radix, radix) + held.shape[1:])
        mine = (self.index >> first) & (radix - 1)
        take = lambda at: lax.dynamic_index_in_dim(split, at, 1, keepdims=False)
        got = [
            swap(take(mine ^ rel).astype(BF), rel << first, self.count)
            for rel in range(1, radix)
        ]
        total = take(mine).astype(F32)
        for piece in got:
            total = total + piece.astype(F32)
        self.held = total
        return total[0, :1, :128]

    def owned(self):
        while self.plan:
            self.step()
        return self.held[0]


def rows_of(gathered, first, parts, unit):
    taken = gathered[:, first * unit : (first + parts) * unit]
    return taken.reshape(GROUPS, parts * UNIT, gathered.shape[2])


def to_groups(gathered, pieces, unit):
    if unit == UNIT:
        return gathered
    out = []
    at = 0
    for parts in pieces:
        out.append(rows_of(gathered, at, parts, unit))
        at += parts
    return jnp.concatenate(out, axis=1)


def from_groups(packed, pieces, count):
    unit = D // count
    if unit == UNIT:
        return packed
    out = []
    at = 0
    for parts in pieces:
        piece = packed[:, at * UNIT : (at + parts) * UNIT]
        out.append(piece.reshape(count, parts * unit, D))
        at += parts
    return jnp.concatenate(out, axis=1)


def position_table(frames):
    half = D // 2
    rate = np.exp(-(math.log(10000.0) / (half - 1)) * np.arange(half, dtype=np.float64))
    angle = np.arange(frames, dtype=np.float64)[:, None] * rate[None, :]
    return np.concatenate([np.sin(angle), np.cos(angle)], axis=1).astype(np.float32)


def per_device(
    count, log_mels, mask_spans, live_slots, first_conv, second_conv, biases, norm_gains,
    qkv_weight, out_weight, up_weight, up_bias, down_weight, cotangent,
):
    clips, frames, bins = log_mels.shape
    length = frames // 2
    padded = -(-length // ROWS) * ROWS
    index = lax.axis_index("dp")
    unit = D // count
    tap_lanes = 3 * bins
    ups = FF // D

    small = jnp.concatenate(
        [
            first_conv.reshape(tap_lanes, unit).T,
            biases.T,
            norm_gains.T,
            up_bias.reshape(unit, ups),
            jnp.zeros((unit, D - tap_lanes - 10 - ups), BF),
        ],
        axis=1,
    )
    near = jnp.concatenate([small, second_conv.reshape(3 * unit, D)])
    parts, order, token = gather_xor(near, count, index)
    if unit != UNIT:
        near = jnp.take(jnp.concatenate(parts), order, axis=0)
        near = to_groups(near, (1,) * 4, unit)
        parts = (near[: GROUPS // 2], near[GROUPS // 2 :])
        order = jnp.arange(GROUPS, dtype=jnp.int32)
    qkv_w = qkv_weight.transpose(1, 0, 2).reshape(3 * unit, D)
    qkv_w = to_groups(lax.all_gather(qkv_w, "dp", axis=0, tiled=False), (1,) * 3, unit)
    far = jnp.concatenate(
        [
            out_weight,
            up_weight.reshape(unit, ups, D).transpose(1, 0, 2).reshape(ups * unit, D),
            down_weight,
        ]
    )
    far = far + token[0, 0, D - 1]
    far = lax.all_gather(far, "dp", axis=0, tiled=False)
    far = to_groups(far, (1,) * (1 + ups) + (ups,), unit)

    col_even, col_odd = call_prepare(mask_spans, log_mels.transpose(0, 2, 1), padded)
    table = jnp.asarray(position_table(padded))
    a_even, a_odd, d_even, d_odd, d_two, stream, near, vec = call_stem(
        order, col_even, col_odd, table, *parts
    )
    qkv = call_project(stream, qkv_w, vec)
    up_row = jnp.pad(vec[10 : 10 + ups].T.reshape(1, FF), ((0, 7), (0, 0)))
    weights, attended, low_part, inverse = call_attend(qkv, length)
    encoded, att_grad, state_grad, mlp_packed, mlp_sums, up_sums = call_mlp(
        live_slots, attended, stream, cotangent, far, vec, up_row
    )
    mlp_packed = from_groups(mlp_packed, (1,) * (1 + ups) + (ups,), count)
    mlp_sum = Scatter(mlp_packed, count, index, False)
    up_cols = jnp.pad(up_sums[0].reshape(D, ups).T, ((0, 8 - ups), (0, 0)))
    grads = None
    for clip in range(clips):
        token = mlp_sum.step() if clip else None
        grads = call_attend_back(
            clip, weights, att_grad, attended, low_part, inverse, qkv, grads, token
        )
    second_grad, qkv_packed, qkv_sums = call_qkv_back(
        grads, stream, state_grad, d_two, qkv_w, vec, mlp_sum.step()
    )
    qkv_sum = Scatter(from_groups(qkv_packed, (1,) * 3, count), count, index, True)
    f_even, f_odd, stem_packed = call_stem_back(
        second_grad, a_even, a_odd, d_even, d_odd, col_even, col_odd, near,
        (qkv_sums, mlp_sums, up_cols), mlp_sum.step(),
    )
    stem_sum = Scatter(from_groups(stem_packed, (1,) * 4, count), count, index, True)
    token = mlp_sum.step() + qkv_sum.step()
    mel_turned, encoded = call_mel(
        mask_spans, f_even, f_odd, near, encoded, frames, bins, token
    )
    mel_grad = mel_turned.transpose(0, 2, 1)
    encoded = encoded.reshape(length, clips, D).transpose(1, 0, 2)
    mlp_owned, qkv_owned, stem_owned = mlp_sum.owned(), qkv_sum.owned(), stem_sum.owned()

    mixed = stem_owned[:unit]
    bias_grad = mixed[:, tap_lanes : tap_lanes + 8].T
    return (
        encoded,
        mel_grad,
        mixed[:, :tap_lanes].T.reshape(3, bins, unit),
        stem_owned[unit : 4 * unit].reshape(3, unit, D),
        bias_grad,
        mixed[:, tap_lanes + 8 : tap_lanes + 10].T,
        qkv_owned.reshape(3, unit, D).transpose(1, 0, 2),
        mlp_owned[:unit],
        mlp_owned[unit : (1 + ups) * unit]
        .reshape(ups, unit, D)
        .transpose(1, 0, 2)
        .reshape(unit, FF),
        mixed[:, tap_lanes + 10 : tap_lanes + 10 + ups].reshape(ups * unit),
        mlp_owned[(1 + ups) * unit :],
        bias_grad[6],
    )


def solution(mesh):
    return jax.shard_map(
        functools.partial(per_device, mesh.shape["dp"]),
        mesh=mesh,
        in_specs=(
            P("dp", None, None),
            P("dp", None),
            P("dp"),
            P(None, None, "dp"),
            P(None, "dp", None),
            P(None, "dp"),
            P(None, "dp"),
            P("dp", None, None),
            P("dp", None),
            P("dp", None),
            P("dp"),
            P("dp", None),
            P("dp", None, None),
        ),
        out_specs=(
            P("dp", None, None),
            P("dp", None, None),
            P(None, None, "dp"),
            P(None, "dp", None),
            P(None, "dp"),
            P(None, "dp"),
            P("dp", None, None),
            P("dp", None),
            P("dp", None),
            P("dp"),
            P("dp", None),
            P("dp"),
        ),
        check_vma=False,
    )
```

```python
import functools
import math

import jax
import jax.numpy as jnp
import numpy as np
from jax import lax
from jax.experimental import pallas as pl
from jax.experimental.pallas import tpu as pltpu
from jax.sharding import PartitionSpec as P

D = 512
FF = 2048
HEADS = 8
HEAD_DIM = 64
PAIRS = HEADS // 2
ROWS = 768
UNIT = 16
GROUPS = D // UNIT
LN_EPS = 1e-05
SCORE_SCALE = HEAD_DIM ** (-0.5)
LOG2E = math.log2(math.e)
VMEM = 60 * 1024 * 1024
BF = jnp.bfloat16
F32 = jnp.float32


def nn(left, right):
    return lax.dot_general(left, right, (((1,), (0,)), ((), ())), preferred_element_type=F32)


def tn(left, right):
    return lax.dot_general(left, right, (((0,), (0,)), ((), ())), preferred_element_type=F32)


def gelu_both(v):
    phi = 0.5 * lax.erf(v * math.sqrt(0.5)) + 0.5
    bell = jnp.exp2(v * v * (-0.5 * LOG2E))
    return v * phi, phi + v * bell * (1.0 / math.sqrt(2.0 * math.pi))


def row_stats(x):
    mean = jnp.mean(x, axis=-1, keepdims=True)
    centred = x - mean
    var = jnp.mean(centred * centred, axis=-1, keepdims=True)
    rate = lax.rsqrt(var + LN_EPS)
    return centred * rate, rate


def norm_back(hat, rate, gain, upstream):
    scaled = upstream * gain
    first = jnp.mean(scaled, axis=-1, keepdims=True)
    second = jnp.mean(scaled * hat, axis=-1, keepdims=True)
    return rate * (scaled - first - hat * second)


def col_sum(x):
    return jnp.sum(x, axis=0, keepdims=True)


def unit_rows(ref, start, count=UNIT):
    block = ref[:, start : start + count, :]
    return block.reshape(GROUPS * count, block.shape[2])


def prepare_kernel(frames, bins, spans, mels, ce, co, flat, tall):
    clip = pl.program_id(0)
    padded = ce.shape[1]
    place = lax.broadcasted_iota(jnp.int32, (bins, frames), 1)
    bin_at = lax.broadcasted_iota(jnp.int32, (bins, frames), 0)
    time_keep = (place < spans[clip, 0]) | (place >= spans[clip, 0] + spans[clip, 1])
    freq_keep = (bin_at < spans[clip, 2]) | (bin_at >= spans[clip, 2] + spans[clip, 3])

    @pl.when(clip == 0)
    def _():
        flat[...] = jnp.zeros_like(flat)
        tall[0:8, :] = jnp.zeros((8, 128), F32)
        tall[8 + 2 * padded :, :] = jnp.zeros((8, 128), F32)

    flat[0:bins, 0:frames] = jnp.where(time_keep & freq_keep, mels[0].astype(F32), 0.0)
    tall[8 : 8 + 2 * padded, :] = flat[...].T
    before, even, odd, after = (tall[pl.ds(7 + k, padded, stride=2), :] for k in range(4))
    lane = lax.broadcasted_iota(jnp.int32, (padded, 128), 1)
    wrap = 2 * bins - 128
    one = jnp.where(lane == wrap + bins, 1.0, 0.0)
    for out, taps in ((ce, (before, even, odd)), (co, (even, odd, after))):
        middle = pltpu.roll(taps[1], bins, 1)
        out[0, :, 0:128] = (taps[0] + jnp.where(lane >= bins, middle, 0.0)).astype(BF)
        last = pltpu.roll(taps[2], wrap, 1)
        out[0, :, 128:256] = (jnp.where(lane < wrap, middle, 0.0) + last + one).astype(BF)


def stem_kernel(
    order, ce, co, pos, mine, other, a_even, a_odd, d_even, d_odd, d_two, stream, w, vec, buf, first_t
):
    step = pl.program_id(1)
    rows = ce.shape[1]
    half = GROUPS // 2

    @pl.when((pl.program_id(0) == 0) & (step == 0))
    def _():
        for group in range(GROUPS):
            source = order[group]

            @pl.when(source < half)
            def _():
                w[group] = mine[source]

            @pl.when(source >= half)
            def _():
                w[group] = other[source - half]

        turned = unit_rows(w, 0)[:, 0:256].astype(F32).T
        vec[...] = turned[240:256, :]
        first_t[...] = turned.astype(BF)

    even, even_slope = gelu_both(nn(ce[0], first_t[...]))
    odd, odd_slope = gelu_both(nn(co[0], first_t[...]))
    even = even.astype(BF)
    a_even[0] = even
    d_even[0] = even_slope.astype(BF)
    d_odd[0] = odd_slope.astype(BF)
    odd_low = odd.astype(BF)
    a_odd[0] = odd_low

    @pl.when(step == 0)
    def _():
        buf[0:8, :] = jnp.zeros((8, D), F32)

    @pl.when(step > 0)
    def _():
        buf[0:8, :] = buf[rows : rows + 8, :]

    buf[8 : 8 + rows, :] = odd
    before = buf[7 : 7 + rows, :].astype(BF)
    second = nn(before, unit_rows(w, UNIT))
    second = second + nn(even, unit_rows(w, 2 * UNIT))
    second = second + nn(odd_low, unit_rows(w, 3 * UNIT)) + vec[1:2, :]
    wave, slope = gelu_both(second)
    d_two[0] = slope.astype(BF)
    stream[0] = wave + pos[...]


def project_kernel(stream, w, vec, qkv):
    hat, _ = row_stats(stream[0])
    normed = (hat * vec[8:9, :] + vec[2:3, :]).astype(BF)
    queries = nn(normed, unit_rows(w, 0)) + vec[3:4, :]
    qkv[0, :, 0:D] = queries.astype(BF)
    qkv[0, :, D : 2 * D] = nn(normed, unit_rows(w, UNIT)).astype(BF)
    qkv[0, :, 2 * D :] = (nn(normed, unit_rows(w, 2 * UNIT)) + vec[4:5, :]).astype(BF)


def head_mask(shape, head):
    lane = lax.broadcasted_iota(jnp.int32, shape, 1)
    return (lane >= head * HEAD_DIM) & (lane < (head + 1) * HEAD_DIM)


def row_mask(shape, head):
    row = lax.broadcasted_iota(jnp.int32, shape, 0)
    return (row >= head * HEAD_DIM) & (row < (head + 1) * HEAD_DIM)


def attend_kernel(
    length, q_ref, k_ref, v_ref, weights, attended, low_part, inverse, keys_t, wide, reach
):
    step = pl.program_id(2)
    rows = attended.shape[1]
    padded = k_ref.shape[1]
    edge = length // 128 * 128

    def longest(x):
        return jnp.max(jnp.sum(jnp.square(x.astype(F32)), axis=1))

    @pl.when(step == 0)
    def _():
        turned = k_ref[0].T
        for head in range(2):
            own = turned[head * HEAD_DIM : (head + 1) * HEAD_DIM, :]
            keys_t[head, 0:HEAD_DIM, :] = own
            keys_t[head, HEAD_DIM : 2 * HEAD_DIM, :] = own
        wide[:, 0 : 2 * HEAD_DIM] = v_ref[0]
        wide[:, 2 * HEAD_DIM :] = jnp.ones((padded, 2 * HEAD_DIM), BF)
        reach[0] = longest(q_ref[0]) * longest(k_ref[0])

    factor = SCORE_SCALE * LOG2E
    calm = reach[0] < (60.0 / factor) ** 2
    scaled = q_ref[0, pl.ds(pl.multiple_of(step * rows, rows), rows), :].astype(F32) * factor
    large = scaled.astype(BF)
    small = pltpu.roll(scaled - large.astype(F32), HEAD_DIM, 1).astype(BF)
    first = head_mask(large.shape, 0)
    queries = (jnp.where(first, large, small), jnp.where(first, small, large))

    def attend(shift):
        outs = []
        rates = []
        for head in range(2):
            scores = nn(queries[head], keys_t[head])
            body, rest = scores[:, :edge], scores[:, edge:]
            place = lax.broadcasted_iota(jnp.int32, rest.shape, 1) + edge
            rest = jnp.where(place < length, rest, -1e30)
            if shift:
                top = jnp.maximum(
                    jnp.max(body, axis=1, keepdims=True), jnp.max(rest, axis=1, keepdims=True)
                )
                body, rest = body - top, rest - top
            soft = jnp.concatenate([jnp.exp2(body).astype(BF), jnp.exp2(rest).astype(BF)], axis=1)
            weights[0, head] = soft
            mixed = nn(soft, wide[...])
            rate = 1.0 / mixed[:, 2 * HEAD_DIM :]
            outs.append(mixed[:, : 2 * HEAD_DIM] * rate)
            rates.append(rate)
        pick = head_mask(outs[0].shape, 0)
        both = jnp.where(pick, outs[0], outs[1])
        high = both.astype(BF)
        attended[0] = high
        low_part[0] = (both - high.astype(F32)).astype(BF)
        inverse[0] = jnp.where(pick, rates[0], rates[1])

    @pl.when(calm)
    def _():
        attend(False)

    @pl.when(jnp.logical_not(calm))
    def _():
        attend(True)


def attend_back_kernel(
    aliased, weights, grad_ref, att_ref, low_ref, inv_ref, q_ref, k_ref, v_ref, *rest
):
    rest = rest[3 * aliased :]
    dq, dk, dv, dk_sum, dv_sum, right = rest
    step = pl.program_id(1)
    scaled_low = (grad_ref[0].astype(F32) * inv_ref[0]).astype(BF)
    prod = scaled_low.astype(F32) * (att_ref[0].astype(F32) + low_ref[0].astype(F32))
    lane = lax.broadcasted_iota(jnp.int32, prod.shape, 1)
    dots = jnp.zeros(prod.shape, F32)
    for head in range(2):
        dot = -jnp.sum(jnp.where(head_mask(prod.shape, head), prod, 0.0), axis=1, keepdims=True)
        high = dot.astype(BF).astype(F32)
        dots = jnp.where(lane == 2 * head, high, dots)
        dots = jnp.where(lane == 2 * head + 1, dot - high, dots)
    left = jnp.concatenate([scaled_low, dots.astype(BF)], axis=1)
    q_turn = q_ref[0].T
    g_turn = scaled_low.T

    @pl.when(step == 0)
    def _():
        dk_sum[...] = jnp.zeros_like(dk_sum)
        dv_sum[...] = jnp.zeros_like(dv_sum)
        turned = v_ref[0].T
        zero = jnp.zeros_like(turned)
        row = lax.broadcasted_iota(jnp.int32, turned.shape, 0)
        for head in range(2):
            right[head, 0:128, :] = jnp.where(row_mask(turned.shape, head), turned, zero)
            right[head, 128:256, :] = jnp.where(
                (row == 2 * head) | (row == 2 * head + 1), zero + 1, zero
            )

    outs = []
    for head in range(2):
        soft = weights[0, head]
        score_grad = (soft.astype(F32) * nn(left, right[head])).astype(BF)
        outs.append(nn(score_grad, k_ref[0]))
        span = slice(head * HEAD_DIM, (head + 1) * HEAD_DIM)
        dk_sum[span, :] += nn(q_turn[span, :], score_grad)
        dv_sum[span, :] += nn(g_turn[span, :], soft)
    pick = head_mask(outs[0].shape, 0)
    dq[0] = (jnp.where(pick, outs[0], outs[1]) * SCORE_SCALE).astype(BF)

    @pl.when(step == pl.num_programs(1) - 1)
    def _():
        dk[0] = (dk_sum[...].T * SCORE_SCALE).astype(BF)
        dv[0] = dv_sum[...].T.astype(BF)


def mlp_kernel(
    length, live, att, stream, cot, w, vec, up_bias,
    encoded, att_grad, state_grad, packed, sums, up_sums,
    out_acc, up_acc, down_acc, out_t, up_t, down_t, mixed,
):
    step = pl.program_id(0)
    clip = pl.program_id(1)
    clips = pl.num_programs(1)
    rows = cot.shape[1]
    alive = clip < live[0]

    @pl.when((clip == 0) & (step == 0))
    def _():
        out_acc[...] = jnp.zeros_like(out_acc)
        up_acc[...] = jnp.zeros_like(up_acc)
        down_acc[...] = jnp.zeros_like(down_acc)
        sums[...] = jnp.zeros_like(sums)
        up_sums[...] = jnp.zeros_like(up_sums)
        out_t[...] = unit_rows(w, 0).T
        for part in range(FF // D):
            up_t[part] = unit_rows(w, (1 + part) * UNIT).T
            down_t[part] = unit_rows(w, 5 * UNIT, 4 * UNIT)[part * D : (part + 1) * D, :].T

    place = lax.broadcasted_iota(jnp.int32, (rows, D), 0) + step * rows
    reach = jnp.where(alive, length, 0)
    cot_float = jnp.where(place < reach, cot[0].astype(F32), 0.0)
    cot_low = cot_float.astype(BF)
    attended = att[0]
    out_w = unit_rows(w, 0)
    after = stream[0] + nn(attended, out_w) + vec[5:6, :]
    hat, rate = row_stats(after)
    normed = (hat * vec[9:10, :] + vec[6:7, :]).astype(BF)
    normed_turn = normed.T
    cot_turn = cot_low.T
    result = after + vec[7:8, :]
    normed_grad = jnp.zeros((rows, D), F32)
    down_all = unit_rows(w, 5 * UNIT, 4 * UNIT)
    for part in range(FF // D):
        span = slice(part * D, (part + 1) * D)
        up_w = unit_rows(w, (1 + part) * UNIT)
        down_w = down_all[span, :]
        hidden = nn(normed, up_w) + up_bias[0:1, span]
        gated, slope = gelu_both(hidden)
        gated = gated.astype(BF)
        result = result + nn(gated, down_w)
        hidden_grad = nn(cot_low, down_t[part]) * slope
        up_sums[0:1, span] += col_sum(hidden_grad)
        hidden_grad = hidden_grad.astype(BF)
        normed_grad = normed_grad + nn(hidden_grad, up_t[part])
        up_acc[part] += nn(normed_turn, hidden_grad)
        down_acc[part] += nn(cot_turn, gated)
    result = jnp.where(alive, result, 0.0)
    slots = mixed.shape[1] // rows
    for slot in range(slots):

        @pl.when(clip == slot)
        def _():
            for part in range(D // 128):
                lanes = slice(part * 128, (part + 1) * 128)
                mixed[part, pl.ds(slot, rows, stride=slots), :] = result[:, lanes]

    @pl.when(clip == clips - 1)
    def _():
        for part in range(D // 128):
            encoded[:, part * 128 : (part + 1) * 128] = mixed[part].astype(BF)

    total = cot_float + norm_back(hat, rate, vec[9:10, :], normed_grad)
    state_grad[0] = total
    sums[0:1, :] += col_sum(total)
    sums[1:2, :] += col_sum(normed_grad)
    sums[2:3, :] += col_sum(cot_float)
    sums[3:4, :] += col_sum(normed_grad * hat)
    low = total.astype(BF)
    att_grad[0] = nn(low, out_t[...]).astype(BF)
    out_acc[...] += tn(attended, low)

    @pl.when((clip == clips - 1) & (step == pl.num_programs(0) - 1))
    def _():
        packed[:, 0:UNIT, :] = out_acc[...].astype(BF).reshape(GROUPS, UNIT, D)
        for part in range(FF // D):
            at = (1 + part) * UNIT
            packed[:, at : at + UNIT, :] = up_acc[part].astype(BF).reshape(GROUPS, UNIT, D)
            owners = GROUPS // (FF // D)
            packed[part * owners : (part + 1) * owners, 5 * UNIT : 9 * UNIT, :] = (
                down_acc[part].T.astype(BF).reshape(owners, 4 * UNIT, D)
            )


def qkv_back_kernel(
    dq, dk, dv, stream, state_grad, d_two, w, vec, second_grad, packed, sums, acc, turned
):
    clip = pl.program_id(0)
    step = pl.program_id(1)

    @pl.when((clip == 0) & (step == 0))
    def _():
        acc[...] = jnp.zeros_like(acc)
        sums[...] = jnp.zeros_like(sums)
        for part in range(3):
            turned[part] = unit_rows(w, part * UNIT).T

    parts = (dq[0], dk[0], dv[0])
    hat, rate = row_stats(stream[0])
    normed_turn = (hat * vec[8:9, :] + vec[2:3, :]).astype(BF).T
    normed_grad = nn(parts[0], turned[0])
    normed_grad = normed_grad + nn(parts[1], turned[1])
    normed_grad = normed_grad + nn(parts[2], turned[2])
    for part in range(3):
        acc[part] += nn(normed_turn, parts[part])
    total = state_grad[0] + norm_back(hat, rate, vec[8:9, :], normed_grad)
    grad = total * d_two[0].astype(F32)
    second_grad[0] = grad.astype(BF)
    sums[0:1, :] += col_sum(grad)
    sums[1:2, :] += col_sum(normed_grad)
    sums[2:3, :] += col_sum(parts[0].astype(F32))
    sums[3:4, :] += col_sum(parts[2].astype(F32))
    sums[4:5, :] += col_sum(normed_grad * hat)

    @pl.when((clip == pl.num_programs(0) - 1) & (step == pl.num_programs(1) - 1))
    def _():
        for part in range(3):
            packed[:, part * UNIT : (part + 1) * UNIT, :] = (
                acc[part].astype(BF).reshape(GROUPS, UNIT, D)
            )


def stem_back_kernel(
    grad_ref, a_even, a_odd, d_even, d_odd, ce, co, w, qkv_sums, mlp_sums, up_cols,
    f_even, f_odd, packed, acc, w_acc, buf, extra, turned,
):
    clip = pl.program_id(0)
    step = pl.program_id(1)
    rows = grad_ref.shape[1]

    @pl.when((clip == 0) & (step == 0))
    def _():
        acc[...] = jnp.zeros_like(acc)
        w_acc[...] = jnp.zeros_like(w_acc)
        for part in range(3):
            turned[part] = unit_rows(w, (1 + part) * UNIT).T

    @pl.when(step == 0)
    def _():
        buf[rows : rows + 8, :] = jnp.zeros((8, D), F32)

    @pl.when(step > 0)
    def _():
        buf[rows : rows + 8, :] = buf[0:8, :]

    grad = grad_ref[0]
    buf[0:rows, :] = grad.astype(F32)
    after = buf[1 : rows + 1, :].astype(BF)
    even_grad = nn(grad, turned[1])
    odd_grad = nn(grad, turned[2]) + nn(after, turned[0])
    even_grad = (even_grad * d_even[0].astype(F32)).astype(BF)
    odd_grad = (odd_grad * d_odd[0].astype(F32)).astype(BF)
    f_even[0] = even_grad
    f_odd[0] = odd_grad
    odd_turn = a_odd[0].T
    acc[0] += nn(odd_turn, after)
    acc[1] += nn(a_even[0].T, grad)
    acc[2] += nn(odd_turn, grad)
    w_acc[...] += tn(even_grad, ce[0]) + tn(odd_grad, co[0])

    @pl.when((clip == pl.num_programs(0) - 1) & (step == pl.num_programs(1) - 1))
    def _():
        for part in range(3):
            at = (1 + part) * UNIT
            packed[:, at : at + UNIT, :] = acc[part].astype(BF).reshape(GROUPS, UNIT, D)
        extra[...] = jnp.zeros_like(extra)
        extra[113:117, :] = qkv_sums[0:4, :]
        extra[117:120, :] = mlp_sums[0:3, :]
        extra[120:121, :] = qkv_sums[4:5, :]
        extra[121:122, :] = mlp_sums[3:4, :]
        extra[122:126, :] = up_cols[0:4, :]
        small = jnp.concatenate(
            [w_acc[:, 0:128], w_acc[:, 128:256] + extra[...].T, jnp.zeros((D, D - 256), F32)],
            axis=1,
        )
        packed[:, 0:UNIT, :] = small.astype(BF).reshape(GROUPS, UNIT, D)


def mel_kernel(frames, bins, spans, f_even, f_odd, w, out, mel_w, down_buf, up_buf, tall):
    clip = pl.program_id(0)
    rows = f_even.shape[1]

    @pl.when(clip == 0)
    def _():
        first_w = unit_rows(w, 0)[:, 0:256].astype(F32)
        lane = lax.broadcasted_iota(jnp.int32, (D, 128), 1)
        low, high = first_w[:, 0:128], first_w[:, 128:256]
        wrap = 2 * bins - 128
        keep = lane < bins
        zero = jnp.zeros((D, 128), BF)
        taps = (
            jnp.where(keep, low, 0.0).astype(BF),
            jnp.where(
                keep,
                jnp.where(lane < 128 - bins, pltpu.roll(low, 128 - bins, 1), pltpu.roll(high, 128 - bins, 1)),
                0.0,
            ).astype(BF),
            jnp.where(keep, pltpu.roll(high, 128 - wrap, 1), 0.0).astype(BF),
        )
        for at, tap in enumerate((taps[1], taps[2], zero, taps[0])):
            mel_w[0:D, at * 128 : (at + 1) * 128] = tap
        for at, tap in enumerate((taps[0], taps[1], taps[2], zero)):
            mel_w[D : 2 * D, at * 128 : (at + 1) * 128] = tap

    full = nn(f_even[0], mel_w[0:D, :]) + nn(f_odd[0], mel_w[D : 2 * D, :])
    down_buf[0:8, :] = jnp.zeros((8, 128), F32)
    down_buf[8 : 8 + rows, :] = full[:, 256:384]
    up_buf[0:rows, :] = full[:, 384:512]
    up_buf[rows : rows + 8, :] = jnp.zeros((8, 128), F32)
    tall[pl.ds(0, rows, stride=2), :] = full[:, 0:128] + down_buf[7 : 7 + rows, :]
    tall[pl.ds(1, rows, stride=2), :] = full[:, 128:256] + up_buf[1 : rows + 1, :]
    turned = tall[...].T[0:bins, 0:frames]
    place = lax.broadcasted_iota(jnp.int32, (bins, frames), 1)
    bin_at = lax.broadcasted_iota(jnp.int32, (bins, frames), 0)
    time_keep = (place < spans[clip, 0]) | (place >= spans[clip, 0] + spans[clip, 1])
    freq_keep = (bin_at < spans[clip, 2]) | (bin_at >= spans[clip, 2] + spans[clip, 3])
    out[0] = jnp.where(time_keep & freq_keep, turned, 0.0)


def whole(shape):
    return pl.BlockSpec(shape, lambda *_: (0,) * len(shape), pipeline_mode=pl.Buffered(1))


def params(semantics):
    return pltpu.CompilerParams(
        vmem_limit_bytes=VMEM, dimension_semantics=("arbitrary",) * semantics
    )


def cost(flops, moved):
    return pl.CostEstimate(flops=int(flops), bytes_accessed=int(moved), transcendentals=0)


SMEM = pl.BlockSpec(memory_space=pltpu.SMEM)


def ordered(kernel, operands, specs, token):
    if token is None:
        return kernel, operands, specs
    place = len(specs)

    def inner(*refs):
        kernel(*refs[:place], *refs[place + 1 :])

    return inner, list(operands) + [token], list(specs) + [whole(token.shape)]


def call_prepare(spans, mels, padded):
    clips, bins, frames = mels.shape
    row = pl.BlockSpec((1, padded, 256), lambda c: (c, 0, 0))
    return pl.pallas_call(
        functools.partial(prepare_kernel, frames, bins),
        grid=(clips,),
        in_specs=[SMEM, pl.BlockSpec((1, bins, frames), lambda c: (c, 0, 0))],
        out_specs=[row, row],
        out_shape=[jax.ShapeDtypeStruct((clips, padded, 256), BF)] * 2,
        scratch_shapes=[
            pltpu.VMEM((128, 2 * padded), F32),
            pltpu.VMEM((2 * padded + 16, 128), F32),
        ],
        compiler_params=params(1),
        cost_estimate=cost(8e9, clips * padded * 2048),
        name="mel_prepare",
    )(spans, mels)


def call_stem(order, ce, co, pos, mine, other):
    clips, padded, _ = ce.shape
    row = lambda width: pl.BlockSpec((1, ROWS, width), lambda c, i: (c, i, 0))
    out = lambda width, kind: jax.ShapeDtypeStruct((clips, padded, width), kind)
    return pl.pallas_call(
        stem_kernel,
        grid=(clips, padded // ROWS),
        in_specs=[
            SMEM, row(256), row(256), pl.BlockSpec((ROWS, D), lambda c, i: (i, 0)),
            whole(mine.shape), whole(other.shape),
        ],
        out_specs=[row(D)] * 6 + [whole((GROUPS, 4 * UNIT, D)), whole((UNIT, D))],
        out_shape=[out(D, BF)] * 5 + [
            out(D, F32),
            jax.ShapeDtypeStruct((GROUPS, 4 * UNIT, D), BF),
            jax.ShapeDtypeStruct((UNIT, D), F32),
        ],
        scratch_shapes=[pltpu.VMEM((ROWS + 8, D), F32), pltpu.VMEM((256, D), BF)],
        compiler_params=params(2),
        cost_estimate=cost(24e9, clips * padded * 9000),
        name="stem_forward",
    )(order, ce, co, pos, mine, other)


def call_project(stream, w, vec):
    clips, padded, _ = stream.shape
    row = lambda width: pl.BlockSpec((1, ROWS, width), lambda c, i: (c, i, 0))
    return pl.pallas_call(
        project_kernel,
        grid=(clips, padded // ROWS),
        in_specs=[row(D), whole(w.shape), whole(vec.shape)],
        out_specs=row(3 * D),
        out_shape=jax.ShapeDtypeStruct((clips, padded, 3 * D), BF),
        compiler_params=params(2),
        cost_estimate=cost(10e9, clips * padded * 5000),
        name="projection_forward",
    )(stream, w, vec)


def call_attend(qkv, length):
    clips, padded, _ = qkv.shape
    query = pl.BlockSpec((1, ROWS, 128), lambda c, h, i: (c, i, h))
    whole_rows = lambda at: pl.BlockSpec((1, padded, 128), lambda c, h, i: (c, 0, at + h))
    return pl.pallas_call(
        functools.partial(attend_kernel, length),
        grid=(clips, PAIRS, padded // ROWS),
        in_specs=[whole_rows(0), whole_rows(PAIRS), whole_rows(2 * PAIRS)],
        out_specs=[
            pl.BlockSpec((1, 2, ROWS, padded), lambda c, h, i: (c, h, i, 0)),
            query,
            query,
            query,
        ],
        out_shape=[
            jax.ShapeDtypeStruct((clips, HEADS, padded, padded), BF),
            jax.ShapeDtypeStruct((clips, padded, D), BF),
            jax.ShapeDtypeStruct((clips, padded, D), BF),
            jax.ShapeDtypeStruct((clips, padded, D), F32),
        ],
        scratch_shapes=[
            pltpu.VMEM((2, 128, padded), BF),
            pltpu.VMEM((padded, 256), BF),
            pltpu.SMEM((1,), F32),
        ],
        compiler_params=params(3),
        cost_estimate=cost(50e9, clips * padded * padded * 16),
        name="attention_forward",
    )(qkv, qkv, qkv)


def call_attend_back(clip, weights, grad, attended, low_part, inverse, qkv, earlier, token):
    clips, padded, _ = qkv.shape
    query = pl.BlockSpec((1, ROWS, 128), lambda h, i: (clip, i, h))
    keys = lambda at: pl.BlockSpec((1, padded, 128), lambda h, i: (clip, 0, at + h))
    shape = jax.ShapeDtypeStruct((clips, padded, D), BF)
    aliases = {}
    extra = []
    extra_specs = []
    if earlier is not None:
        extra = list(earlier)
        extra_specs = [pl.BlockSpec(memory_space=pl.ANY)] * 3
        aliases = {8: 0, 9: 1, 10: 2}
    kernel, operands, specs = ordered(
        functools.partial(attend_back_kernel, 0 if earlier is None else 1),
        [weights, grad, attended, low_part, inverse, qkv, qkv, qkv] + extra,
        [
            pl.BlockSpec((1, 2, ROWS, padded), lambda h, i: (clip, h, i, 0)),
            query, query, query, query, query, keys(PAIRS), keys(2 * PAIRS),
        ] + extra_specs,
        token,
    )
    return pl.pallas_call(
        kernel,
        grid=(PAIRS, padded // ROWS),
        in_specs=specs,
        out_specs=[query, keys(0), keys(0)],
        out_shape=[shape] * 3,
        scratch_shapes=[pltpu.VMEM((128, padded), F32)] * 2
        + [pltpu.VMEM((2, 256, padded), BF)],
        input_output_aliases=aliases,
        compiler_params=params(2),
        cost_estimate=cost(40e9, padded * padded * 16),
        name="attention_backward",
    )(*operands)


def call_mlp(live, attended, stream, cot, w, vec, up_bias):
    clips, padded, _ = attended.shape
    row = pl.BlockSpec((1, ROWS, D), lambda i, c: (c, i, 0))
    return pl.pallas_call(
        functools.partial(mlp_kernel, cot.shape[1]),
        grid=(padded // ROWS, clips),
        in_specs=[SMEM, row, row, row, whole(w.shape), whole(vec.shape), whole(up_bias.shape)],
        out_specs=[
            pl.BlockSpec((ROWS * clips, D), lambda i, c: (i, 0)), row, row,
            whole((GROUPS, 9 * UNIT, D)), whole((8, D)), whole((8, FF)),
        ],
        out_shape=[
            jax.ShapeDtypeStruct((cot.shape[1] * clips, D), BF),
            jax.ShapeDtypeStruct(attended.shape, BF),
            jax.ShapeDtypeStruct(attended.shape, F32),
            jax.ShapeDtypeStruct((GROUPS, 9 * UNIT, D), BF),
            jax.ShapeDtypeStruct((8, D), F32),
            jax.ShapeDtypeStruct((8, FF), F32),
        ],
        scratch_shapes=[
            pltpu.VMEM((D, D), F32),
            pltpu.VMEM((FF // D, D, D), F32),
            pltpu.VMEM((FF // D, D, D), F32),
            pltpu.VMEM((D, D), BF),
            pltpu.VMEM((FF // D, D, D), BF),
            pltpu.VMEM((FF // D, D, D), BF),
            pltpu.VMEM((D // 128, ROWS * clips, 128), F32),
        ],
        compiler_params=params(2),
        cost_estimate=cost(60e9, clips * padded * 8000),
        name="mlp_both_ways",
    )(live, attended, stream, cot, w, vec, up_bias)


def call_qkv_back(grads, stream, state_grad, d_two, w, vec, token):
    clips, padded, _ = stream.shape
    row = pl.BlockSpec((1, ROWS, D), lambda c, i: (c, i, 0))
    kernel, operands, specs = ordered(
        qkv_back_kernel,
        [*grads, stream, state_grad, d_two, w, vec],
        [row] * 6 + [whole(w.shape), whole(vec.shape)],
        token,
    )
    return pl.pallas_call(
        kernel,
        grid=(clips, padded // ROWS),
        in_specs=specs,
        out_specs=[row, whole((GROUPS, 3 * UNIT, D)), whole((8, D))],
        out_shape=[
            jax.ShapeDtypeStruct(stream.shape, BF),
            jax.ShapeDtypeStruct((GROUPS, 3 * UNIT, D), BF),
            jax.ShapeDtypeStruct((8, D), F32),
        ],
        scratch_shapes=[pltpu.VMEM((3, D, D), F32), pltpu.VMEM((3, D, D), BF)],
        compiler_params=params(2),
        cost_estimate=cost(18e9, clips * padded * 9000),
        name="projection_backward",
    )(*operands)


def call_stem_back(second_grad, a_even, a_odd, d_even, d_odd, ce, co, w, sums, token):
    clips, padded, _ = second_grad.shape
    last = padded // ROWS - 1
    row = lambda width: pl.BlockSpec((1, ROWS, width), lambda c, i: (c, last - i, 0))
    kernel, operands, specs = ordered(
        stem_back_kernel,
        [second_grad, a_even, a_odd, d_even, d_odd, ce, co, w, *sums],
        [row(D)] * 5 + [row(256)] * 2 + [whole(w.shape)] + [whole((8, D))] * 3,
        token,
    )
    return pl.pallas_call(
        kernel,
        grid=(clips, padded // ROWS),
        in_specs=specs,
        out_specs=[row(D), row(D), whole((GROUPS, 4 * UNIT, D))],
        out_shape=[
            jax.ShapeDtypeStruct(second_grad.shape, BF),
            jax.ShapeDtypeStruct(second_grad.shape, BF),
            jax.ShapeDtypeStruct((GROUPS, 4 * UNIT, D), BF),
        ],
        scratch_shapes=[
            pltpu.VMEM((3, D, D), F32),
            pltpu.VMEM((D, 256), F32),
            pltpu.VMEM((ROWS + 8, D), F32),
            pltpu.VMEM((128, D), F32),
            pltpu.VMEM((3, D, D), BF),
        ],
        compiler_params=params(2),
        cost_estimate=cost(18e9, clips * padded * 9000),
        name="stem_backward",
    )(*operands)


def call_mel(spans, f_even, f_odd, w, frames, bins, token):
    clips, padded, _ = f_even.shape
    row = pl.BlockSpec((1, padded, D), lambda c: (c, 0, 0))
    kernel, operands, specs = ordered(
        functools.partial(mel_kernel, frames, bins),
        [spans, f_even, f_odd, w],
        [SMEM, row, row, whole(w.shape)],
        token,
    )
    return pl.pallas_call(
        kernel,
        grid=(clips,),
        in_specs=specs,
        out_specs=pl.BlockSpec((1, bins, frames), lambda c: (c, 0, 0)),
        out_shape=jax.ShapeDtypeStruct((clips, bins, frames), F32),
        scratch_shapes=[
            pltpu.VMEM((2 * D, D), BF),
            pltpu.VMEM((padded + 8, 128), F32),
            pltpu.VMEM((padded + 8, 128), F32),
            pltpu.VMEM((2 * padded, 128), F32),
        ],
        compiler_params=params(1),
        cost_estimate=cost(8e9, clips * padded * 4000),
        name="mel_backward",
    )(*operands)


def call_after(x, token):
    hold = pl.BlockSpec(memory_space=pl.ANY)

    def kernel(held, ready, passed):
        del held, ready, passed

    return pl.pallas_call(
        kernel,
        in_specs=[hold, pl.BlockSpec(token.shape, lambda: (0, 0))],
        out_specs=hold,
        out_shape=jax.ShapeDtypeStruct(x.shape, x.dtype),
        input_output_aliases={0: 0},
        name="after_stage",
    )(x, token)


def swap(x, mask, count):
    return lax.ppermute(x, "dp", [(i, i ^ mask) for i in range(count)])


def stages(count):
    bits = count.bit_length() - 1
    return [(0, 1)] + [(at, min(2, bits - at)) for at in range(1, bits, 2)]


def gather_xor(x, count, index):
    held = x[None]
    where = jnp.zeros((count,), jnp.int32)
    apart = jnp.arange(count, dtype=jnp.int32) ^ index
    token = None
    parts = None
    for first, many in reversed(stages(count)):
        if parts is not None:
            held = jnp.concatenate(parts)
        where = where + ((apart >> first) & ((1 << many) - 1)) * held.shape[0]
        parts = [held] + [swap(held, rel << first, count) for rel in range(1, 1 << many)]
        if first > 0:
            token = parts[-1]
    return parts, where, token


class Scatter:
    def __init__(self, x, count, index):
        self.held, self.count, self.index = x, count, index
        self.plan = stages(count)

    def step(self):
        if not self.plan:
            return None
        first, many = self.plan.pop(0)
        radix = 1 << many
        held = self.held
        split = held.reshape((held.shape[0] // radix, radix) + held.shape[1:])
        mine = (self.index >> first) & (radix - 1)
        take = lambda at: lax.dynamic_index_in_dim(split, at, 1, keepdims=False)
        got = [swap(take(mine ^ rel), rel << first, self.count) for rel in range(1, radix)]
        total = take(mine).astype(F32)
        for piece in got:
            total = total + piece.astype(F32)
        self.held = total.astype(BF) if self.plan else total
        return total[0, :1, :128]

    def join(self, other):
        self.held = jnp.concatenate([self.held, other.held], axis=1)

    def owned(self):
        while self.plan:
            self.step()
        return self.held[0]


def rows_of(gathered, first, parts, unit):
    taken = gathered[:, first * unit : (first + parts) * unit]
    return taken.reshape(GROUPS, parts * UNIT, gathered.shape[2])


def to_groups(gathered, pieces, unit):
    if unit == UNIT:
        return gathered
    out = []
    at = 0
    for parts in pieces:
        out.append(rows_of(gathered, at, parts, unit))
        at += parts
    return jnp.concatenate(out, axis=1)


def from_groups(packed, pieces, count):
    unit = D // count
    if unit == UNIT:
        return packed
    out = []
    at = 0
    for parts in pieces:
        piece = packed[:, at * UNIT : (at + parts) * UNIT]
        out.append(piece.reshape(count, parts * unit, D))
        at += parts
    return jnp.concatenate(out, axis=1)


def position_table(frames):
    half = D // 2
    rate = np.exp(-(math.log(10000.0) / (half - 1)) * np.arange(half, dtype=np.float64))
    angle = np.arange(frames, dtype=np.float64)[:, None] * rate[None, :]
    return np.concatenate([np.sin(angle), np.cos(angle)], axis=1).astype(np.float32)


def per_device(
    count, log_mels, mask_spans, live_slots, first_conv, second_conv, biases, norm_gains,
    qkv_weight, out_weight, up_weight, up_bias, down_weight, cotangent,
):
    clips, frames, bins = log_mels.shape
    length = frames // 2
    padded = -(-length // ROWS) * ROWS
    index = lax.axis_index("dp")
    unit = D // count
    tap_lanes = 3 * bins
    ups = FF // D

    small = jnp.concatenate(
        [
            first_conv.reshape(tap_lanes, unit).T,
            biases.T,
            norm_gains.T,
            up_bias.reshape(unit, ups),
            jnp.zeros((unit, D - tap_lanes - 10 - ups), BF),
        ],
        axis=1,
    )
    near = jnp.concatenate([small, second_conv.reshape(3 * unit, D)])
    parts, order, token = gather_xor(near, count, index)
    if unit != UNIT:
        near = jnp.take(jnp.concatenate(parts), order, axis=0)
        near = to_groups(near, (1,) * 4, unit)
        parts = (near[: GROUPS // 2], near[GROUPS // 2 :])
        order = jnp.arange(GROUPS, dtype=jnp.int32)
    qkv_w = qkv_weight.transpose(1, 0, 2).reshape(3 * unit, D)
    qkv_w = to_groups(lax.all_gather(qkv_w, "dp", axis=0, tiled=False), (1,) * 3, unit)
    far = jnp.concatenate(
        [
            out_weight,
            up_weight.reshape(unit, ups, D).transpose(1, 0, 2).reshape(ups * unit, D),
            down_weight,
        ]
    )
    far = far + token[0, 0, D - 1]
    far = lax.all_gather(far, "dp", axis=0, tiled=False)
    far = to_groups(far, (1,) * (1 + ups) + (ups,), unit)

    col_even, col_odd = call_prepare(mask_spans, log_mels.transpose(0, 2, 1), padded)
    table = jnp.asarray(position_table(padded))
    a_even, a_odd, d_even, d_odd, d_two, stream, near, vec = call_stem(
        order, col_even, col_odd, table, *parts
    )
    qkv = call_project(stream, qkv_w, vec)
    up_row = jnp.pad(vec[10 : 10 + ups].T.reshape(1, FF), ((0, 7), (0, 0)))
    weights, attended, low_part, inverse = call_attend(qkv, length)
    encoded, att_grad, state_grad, mlp_packed, mlp_sums, up_sums = call_mlp(
        live_slots, attended, stream, cotangent, far, vec, up_row
    )
    mlp_packed = from_groups(mlp_packed, (1,) * (1 + ups) + (ups,), count)
    mlp_sum = Scatter(mlp_packed, count, index)
    up_cols = jnp.pad(up_sums[0].reshape(D, ups).T, ((0, 8 - ups), (0, 0)))
    grads = None
    for clip in range(clips):
        token = mlp_sum.step() if clip else None
        grads = call_attend_back(
            clip, weights, att_grad, attended, low_part, inverse, qkv, grads, token
        )
    second_grad, qkv_packed, qkv_sums = call_qkv_back(
        grads, stream, state_grad, d_two, qkv_w, vec, mlp_sum.step()
    )
    qkv_sum = Scatter(from_groups(qkv_packed, (1,) * 3, count), count, index)
    f_even, f_odd, stem_packed = call_stem_back(
        second_grad, a_even, a_odd, d_even, d_odd, col_even, col_odd, near,
        (qkv_sums, mlp_sums, up_cols), mlp_sum.step(),
    )
    stem_sum = Scatter(from_groups(stem_packed, (1,) * 4, count), count, index)
    mel_turned = call_mel(mask_spans, f_even, f_odd, near, frames, bins, qkv_sum.step())
    mel_grad = mel_turned.transpose(0, 2, 1)
    encoded = call_after(encoded, stem_sum.step())
    encoded = encoded.reshape(length, clips, D).transpose(1, 0, 2)
    qkv_sum.step()
    stem_sum.step()
    if stem_sum.plan:
        stem_sum.join(qkv_sum)
        owned = stem_sum.owned()
    else:
        owned = jnp.concatenate([stem_sum.owned(), qkv_sum.owned()])
    mlp_owned, stem_owned, qkv_owned = mlp_sum.owned(), owned[: 4 * unit], owned[4 * unit :]

    mixed = stem_owned[:unit]
    bias_grad = mixed[:, tap_lanes : tap_lanes + 8].T
    return (
        encoded,
        mel_grad,
        mixed[:, :tap_lanes].T.reshape(3, bins, unit),
        stem_owned[unit : 4 * unit].reshape(3, unit, D),
        bias_grad,
        mixed[:, tap_lanes + 8 : tap_lanes + 10].T,
        qkv_owned.reshape(3, unit, D).transpose(1, 0, 2),
        mlp_owned[:unit],
        mlp_owned[unit : (1 + ups) * unit]
        .reshape(ups, unit, D)
        .transpose(1, 0, 2)
        .reshape(unit, FF),
        mixed[:, tap_lanes + 10 : tap_lanes + 10 + ups].reshape(ups * unit),
        mlp_owned[(1 + ups) * unit :],
        bias_grad[6],
    )


def solution(mesh):
    return jax.shard_map(
        functools.partial(per_device, mesh.shape["dp"]),
        mesh=mesh,
        in_specs=(
            P("dp", None, None),
            P("dp", None),
            P("dp"),
            P(None, None, "dp"),
            P(None, "dp", None),
            P(None, "dp"),
            P(None, "dp"),
            P("dp", None, None),
            P("dp", None),
            P("dp", None),
            P("dp"),
            P("dp", None),
            P("dp", None, None),
        ),
        out_specs=(
            P("dp", None, None),
            P("dp", None, None),
            P(None, None, "dp"),
            P(None, "dp", None),
            P(None, "dp"),
            P(None, "dp"),
            P("dp", None, None),
            P("dp", None),
            P("dp", None),
            P("dp"),
            P("dp", None),
            P("dp"),
        ),
        check_vma=False,
    )
```

```python
import functools
import math

import jax
import jax.numpy as jnp
import numpy as np
from jax import lax
from jax.experimental import pallas as pl
from jax.experimental.pallas import tpu as pltpu
from jax.sharding import PartitionSpec as P

D = 512
FF = 2048
HEADS = 8
HEAD_DIM = 64
PAIRS = HEADS // 2
ROWS = 768
CHUNK = 256
UNIT = 16
GROUPS = D // UNIT
LN_EPS = 1e-05
SCORE_SCALE = HEAD_DIM ** (-0.5)
LOG2E = math.log2(math.e)
VMEM = 60 * 1024 * 1024
BF = jnp.bfloat16
F32 = jnp.float32


def nn(left, right):
    return lax.dot_general(left, right, (((1,), (0,)), ((), ())), preferred_element_type=F32)


def tn(left, right):
    return lax.dot_general(left, right, (((0,), (0,)), ((), ())), preferred_element_type=F32)


def gelu_both(v):
    phi = 0.5 * lax.erf(v * math.sqrt(0.5)) + 0.5
    bell = jnp.exp2(v * v * (-0.5 * LOG2E))
    return v * phi, phi + v * bell * (1.0 / math.sqrt(2.0 * math.pi))


def staggered(count, *works):
    depth = len(works)
    for at in range(count + depth - 1):
        for lag, work in enumerate(works):
            if 0 <= at - lag < count:
                work(at - lag)


def row_stats(x):
    mean = jnp.mean(x, axis=-1, keepdims=True)
    centred = x - mean
    var = jnp.mean(centred * centred, axis=-1, keepdims=True)
    rate = lax.rsqrt(var + LN_EPS)
    return centred * rate, rate


def norm_back(hat, rate, gain, upstream):
    scaled = upstream * gain
    first = jnp.mean(scaled, axis=-1, keepdims=True)
    second = jnp.mean(scaled * hat, axis=-1, keepdims=True)
    return rate * (scaled - first - hat * second)


def col_sum(x):
    return jnp.sum(x, axis=0, keepdims=True)


def unit_rows(ref, start, count=UNIT):
    block = ref[:, start : start + count, :]
    return block.reshape(GROUPS * count, block.shape[2])


def prepare_kernel(frames, bins, spans, mels, ce, co, flat, tall):
    clip = pl.program_id(0)
    padded = ce.shape[1]
    place = lax.broadcasted_iota(jnp.int32, (bins, frames), 1)
    bin_at = lax.broadcasted_iota(jnp.int32, (bins, frames), 0)
    time_keep = (place < spans[clip, 0]) | (place >= spans[clip, 0] + spans[clip, 1])
    freq_keep = (bin_at < spans[clip, 2]) | (bin_at >= spans[clip, 2] + spans[clip, 3])

    @pl.when(clip == 0)
    def _():
        flat[...] = jnp.zeros_like(flat)
        tall[0:8, :] = jnp.zeros((8, 128), F32)
        tall[8 + 2 * padded :, :] = jnp.zeros((8, 128), F32)

    flat[0:bins, 0:frames] = jnp.where(time_keep & freq_keep, mels[0].astype(F32), 0.0)
    tall[8 : 8 + 2 * padded, :] = flat[...].T
    before, even, odd, after = (tall[pl.ds(7 + k, padded, stride=2), :] for k in range(4))
    lane = lax.broadcasted_iota(jnp.int32, (padded, 128), 1)
    wrap = 2 * bins - 128
    one = jnp.where(lane == wrap + bins, 1.0, 0.0)
    for out, taps in ((ce, (before, even, odd)), (co, (even, odd, after))):
        middle = pltpu.roll(taps[1], bins, 1)
        out[0, :, 0:128] = (taps[0] + jnp.where(lane >= bins, middle, 0.0)).astype(BF)
        last = pltpu.roll(taps[2], wrap, 1)
        out[0, :, 128:256] = (jnp.where(lane < wrap, middle, 0.0) + last + one).astype(BF)


def stem_kernel(
    order, ce, co, pos, mine, other, a_even, a_odd, d_even, d_odd, d_two, stream, w, vec, buf, first_t
):
    step = pl.program_id(0)
    clip = pl.program_id(1)
    rows = ce.shape[1]
    half = GROUPS // 2

    @pl.when((clip == 0) & (step == 0))
    def _():
        for group in range(GROUPS):
            source = order[group]

            @pl.when(source < half)
            def _():
                w[group] = mine[source]

            @pl.when(source >= half)
            def _():
                w[group] = other[source - half]

        turned = unit_rows(w, 0)[:, 0:256].astype(F32).T
        vec[...] = turned[240:256, :]
        first_t[...] = turned.astype(BF)

    even, even_slope = gelu_both(nn(ce[0], first_t[...]))
    odd, odd_slope = gelu_both(nn(co[0], first_t[...]))
    even = even.astype(BF)
    a_even[0] = even
    d_even[0] = even_slope.astype(BF)
    d_odd[0] = odd_slope.astype(BF)
    odd_low = odd.astype(BF)
    a_odd[0] = odd_low

    @pl.when(step == 0)
    def _():
        buf[clip, 0:8, :] = jnp.zeros((8, D), F32)

    @pl.when(step > 0)
    def _():
        buf[clip, 0:8, :] = buf[clip, rows : rows + 8, :]

    buf[clip, 8 : 8 + rows, :] = odd
    before = buf[clip, 7 : 7 + rows, :].astype(BF)
    second = nn(before, unit_rows(w, UNIT))
    second = second + nn(even, unit_rows(w, 2 * UNIT))
    second = second + nn(odd_low, unit_rows(w, 3 * UNIT)) + vec[1:2, :]
    wave, slope = gelu_both(second)
    d_two[0] = slope.astype(BF)
    stream[0] = wave + pos[...]


def project_kernel(stream, w, vec, qkv):
    hat, _ = row_stats(stream[0])
    normed = (hat * vec[8:9, :] + vec[2:3, :]).astype(BF)
    queries = nn(normed, unit_rows(w, 0)) + vec[3:4, :]
    qkv[0, :, 0:D] = queries.astype(BF)
    qkv[0, :, D : 2 * D] = nn(normed, unit_rows(w, UNIT)).astype(BF)
    qkv[0, :, 2 * D :] = (nn(normed, unit_rows(w, 2 * UNIT)) + vec[4:5, :]).astype(BF)


def head_mask(shape, head):
    lane = lax.broadcasted_iota(jnp.int32, shape, 1)
    return (lane >= head * HEAD_DIM) & (lane < (head + 1) * HEAD_DIM)


def row_mask(shape, head):
    row = lax.broadcasted_iota(jnp.int32, shape, 0)
    return (row >= head * HEAD_DIM) & (row < (head + 1) * HEAD_DIM)


def attend_kernel(
    length, q_ref, k_ref, v_ref, weights, attended, low_part, inverse, keys_t, wide, reach
):
    step = pl.program_id(2)
    rows = attended.shape[1]
    padded = k_ref.shape[1]
    edge = length // 128 * 128

    def longest(x):
        return jnp.max(jnp.sum(jnp.square(x.astype(F32)), axis=1))

    @pl.when(step == 0)
    def _():
        turned = k_ref[0].T
        for head in range(2):
            own = turned[head * HEAD_DIM : (head + 1) * HEAD_DIM, :]
            keys_t[head, 0:HEAD_DIM, :] = own
            keys_t[head, HEAD_DIM : 2 * HEAD_DIM, :] = own
        wide[:, 0 : 2 * HEAD_DIM] = v_ref[0]
        wide[:, 2 * HEAD_DIM :] = jnp.ones((padded, 2 * HEAD_DIM), BF)
        reach[0] = longest(q_ref[0]) * longest(k_ref[0])

    factor = SCORE_SCALE * LOG2E
    calm = reach[0] < (60.0 / factor) ** 2
    scaled = q_ref[0, pl.ds(pl.multiple_of(step * rows, rows), rows), :].astype(F32) * factor
    large = scaled.astype(BF)
    small = pltpu.roll(scaled - large.astype(F32), HEAD_DIM, 1).astype(BF)
    first = head_mask(large.shape, 0)
    queries = (jnp.where(first, large, small), jnp.where(first, small, large))

    def attend(shift):
        parts = [(at, head) for at in range(0, rows, CHUNK) for head in range(2)]
        scores, soft, mixed = {}, {}, {}

        def score(i):
            at, head = parts[i]
            scores[i] = nn(queries[head][at : at + CHUNK], keys_t[head])

        def soften(i):
            at, head = parts[i]
            values = scores.pop(i)
            body, rest = values[:, :edge], values[:, edge:]
            place = lax.broadcasted_iota(jnp.int32, rest.shape, 1) + edge
            rest = jnp.where(place < length, rest, -1e30)
            if shift:
                top = jnp.maximum(
                    jnp.max(body, axis=1, keepdims=True), jnp.max(rest, axis=1, keepdims=True)
                )
                body, rest = body - top, rest - top
            body, rest = jnp.exp2(body).astype(BF), jnp.exp2(rest).astype(BF)
            soft[i] = jnp.concatenate([body, rest], axis=1)
            weights[0, head, at : at + CHUNK, :] = soft[i]

        def mix(i):
            at, head = parts[i]
            mixed[head] = nn(soft.pop(i), wide[...])
            if head == 0:
                return
            rates = [1.0 / mixed[k][:, 2 * HEAD_DIM :] for k in range(2)]
            outs = [mixed[k][:, : 2 * HEAD_DIM] * rates[k] for k in range(2)]
            pick = head_mask(outs[0].shape, 0)
            both = jnp.where(pick, outs[0], outs[1])
            high = both.astype(BF)
            attended[0, at : at + CHUNK, :] = high
            low_part[0, at : at + CHUNK, :] = (both - high.astype(F32)).astype(BF)
            inverse[0, at : at + CHUNK, :] = jnp.where(pick, rates[0], rates[1])

        staggered(len(parts), score, soften, mix)

    @pl.when(calm)
    def _():
        attend(False)

    @pl.when(jnp.logical_not(calm))
    def _():
        attend(True)


def attend_back_kernel(
    aliased, weights, grad_ref, att_ref, low_ref, inv_ref, q_ref, k_ref, v_ref, *rest
):
    rest = rest[3 * aliased :]
    dq, dk, dv, dk_sum, dv_sum, right, score_grad = rest
    step = pl.program_id(1)
    scaled_low = (grad_ref[0].astype(F32) * inv_ref[0]).astype(BF)
    prod = scaled_low.astype(F32) * (att_ref[0].astype(F32) + low_ref[0].astype(F32))
    lane = lax.broadcasted_iota(jnp.int32, prod.shape, 1)
    dots = jnp.zeros(prod.shape, F32)
    for head in range(2):
        dot = -jnp.sum(jnp.where(head_mask(prod.shape, head), prod, 0.0), axis=1, keepdims=True)
        high = dot.astype(BF).astype(F32)
        dots = jnp.where(lane == 2 * head, high, dots)
        dots = jnp.where(lane == 2 * head + 1, dot - high, dots)
    left = jnp.concatenate([scaled_low, dots.astype(BF)], axis=1)
    q_turn = q_ref[0].T
    g_turn = scaled_low.T

    @pl.when(step == 0)
    def _():
        dk_sum[...] = jnp.zeros_like(dk_sum)
        dv_sum[...] = jnp.zeros_like(dv_sum)
        turned = v_ref[0].T
        zero = jnp.zeros_like(turned)
        row = lax.broadcasted_iota(jnp.int32, turned.shape, 0)
        for head in range(2):
            right[head, 0:128, :] = jnp.where(row_mask(turned.shape, head), turned, zero)
            right[head, 128:256, :] = jnp.where(
                (row == 2 * head) | (row == 2 * head + 1), zero + 1, zero
            )

    rows = scaled_low.shape[0]
    parts = [(at, head) for at in range(0, rows, CHUNK) for head in range(2)]
    grads, outs = {}, {}

    def weight_grad(i):
        at, head = parts[i]
        grads[i] = nn(left[at : at + CHUNK], right[head])

    def multiply(i):
        at, head = parts[i]
        soft = weights[0, head, at : at + CHUNK, :].astype(F32)
        score_grad[head, at : at + CHUNK, :] = (soft * grads.pop(i)).astype(BF)

    def query_grad(i):
        at, head = parts[i]
        outs[head] = nn(score_grad[head, at : at + CHUNK, :], k_ref[0])
        if head == 1:
            pick = head_mask(outs[0].shape, 0)
            total = jnp.where(pick, outs[0], outs[1]) * SCORE_SCALE
            dq[0, at : at + CHUNK, :] = total.astype(BF)

    staggered(len(parts), weight_grad, multiply, query_grad)
    for head in range(2):
        span = slice(head * HEAD_DIM, (head + 1) * HEAD_DIM)
        dv_sum[span, :] += nn(g_turn[span, :], weights[0, head])
        dk_sum[span, :] += nn(q_turn[span, :], score_grad[head])

    @pl.when(step == pl.num_programs(1) - 1)
    def _():
        dk[0] = (dk_sum[...].T * SCORE_SCALE).astype(BF)
        dv[0] = dv_sum[...].T.astype(BF)


def mlp_kernel(
    length, live, att, stream, cot, w, vec, up_bias,
    encoded, att_grad, state_grad, packed, sums, up_sums,
    out_acc, up_acc, down_acc, out_t, up_t, down_t, mixed, gated, hidden_grad,
):
    step = pl.program_id(0)
    clip = pl.program_id(1)
    clips = pl.num_programs(1)
    rows = cot.shape[1]
    alive = clip < live[0]

    @pl.when((clip == 0) & (step == 0))
    def _():
        out_acc[...] = jnp.zeros_like(out_acc)
        up_acc[...] = jnp.zeros_like(up_acc)
        down_acc[...] = jnp.zeros_like(down_acc)
        sums[...] = jnp.zeros_like(sums)
        up_sums[...] = jnp.zeros_like(up_sums)
        out_t[...] = unit_rows(w, 0).T
        for part in range(FF // D):
            up_t[part * D : (part + 1) * D, :] = unit_rows(w, (1 + part) * UNIT).T
            down_t[part] = unit_rows(w, 5 * UNIT, 4 * UNIT)[part * D : (part + 1) * D, :].T

    place = lax.broadcasted_iota(jnp.int32, (rows, D), 0) + step * rows
    reach = jnp.where(alive, length, 0)
    cot_float = jnp.where(place < reach, cot[0].astype(F32), 0.0)
    cot_low = cot_float.astype(BF)
    attended = att[0]
    out_w = unit_rows(w, 0)
    after = stream[0] + nn(attended, out_w) + vec[5:6, :]
    hat, rate = row_stats(after)
    normed = (hat * vec[9:10, :] + vec[6:7, :]).astype(BF)
    normed_turn = normed.T
    cot_turn = cot_low.T
    spans = [slice(part * D, (part + 1) * D) for part in range(FF // D)]
    ahead = {}
    sides = [after + vec[7:8, :], None]

    def enter(part):
        ahead[part] = (
            nn(normed, unit_rows(w, (1 + part) * UNIT)) + up_bias[0:1, spans[part]],
            nn(cot_low, down_t[part]),
        )

    def activate(part):
        hidden, grad = ahead.pop(part)
        wave, slope = gelu_both(hidden)
        gated[:, spans[part]] = wave.astype(BF)
        grad = grad * slope
        up_sums[0:1, spans[part]] += col_sum(grad)
        hidden_grad[:, spans[part]] = grad.astype(BF)

    def leave(part):
        wave, grad = gated[:, spans[part]], hidden_grad[:, spans[part]]
        down_w = unit_rows(w, 5 * UNIT, 4 * UNIT)[spans[part], :]
        back = nn(grad, up_t[spans[part], :])
        sides[0] = sides[0] + nn(wave, down_w)
        sides[1] = back if sides[1] is None else sides[1] + back
        up_acc[part] += nn(normed_turn, grad)
        down_acc[part] += nn(cot_turn, wave)

    staggered(FF // D, enter, activate, leave)
    result, normed_grad = sides
    result = jnp.where(alive, result, 0.0)
    slots = mixed.shape[1] // rows
    for slot in range(slots):

        @pl.when(clip == slot)
        def _():
            for part in range(D // 128):
                lanes = slice(part * 128, (part + 1) * 128)
                mixed[part, pl.ds(slot, rows, stride=slots), :] = result[:, lanes]

    @pl.when(clip == clips - 1)
    def _():
        for part in range(D // 128):
            encoded[:, part * 128 : (part + 1) * 128] = mixed[part].astype(BF)

    total = cot_float + norm_back(hat, rate, vec[9:10, :], normed_grad)
    low = total.astype(BF)
    state_grad[0] = low
    sums[0:1, :] += col_sum(total)
    sums[1:2, :] += col_sum(normed_grad)
    sums[2:3, :] += col_sum(cot_float)
    sums[3:4, :] += col_sum(normed_grad * hat)
    att_grad[0] = nn(low, out_t[...]).astype(BF)
    out_acc[...] += tn(attended, low)

    @pl.when((clip == clips - 1) & (step == pl.num_programs(0) - 1))
    def _():
        packed[:, 0:UNIT, :] = out_acc[...].astype(BF).reshape(GROUPS, UNIT, D)
        for part in range(FF // D):
            at = (1 + part) * UNIT
            packed[:, at : at + UNIT, :] = up_acc[part].astype(BF).reshape(GROUPS, UNIT, D)
            owners = GROUPS // (FF // D)
            packed[part * owners : (part + 1) * owners, 5 * UNIT : 9 * UNIT, :] = (
                down_acc[part].T.astype(BF).reshape(owners, 4 * UNIT, D)
            )


def qkv_back_kernel(
    dq, dk, dv, stream, state_grad, d_two, w, vec, second_grad, packed, sums, acc, turned
):
    clip = pl.program_id(0)
    step = pl.program_id(1)

    @pl.when((clip == 0) & (step == 0))
    def _():
        acc[...] = jnp.zeros_like(acc)
        sums[...] = jnp.zeros_like(sums)
        for part in range(3):
            turned[part] = unit_rows(w, part * UNIT).T

    parts = (dq, dk, dv)
    rows = stream.shape[1]
    hat, rate = row_stats(stream[0])
    normed_turn = (hat * vec[8:9, :] + vec[2:3, :]).astype(BF).T
    ahead = {}

    def enter(i):
        at = slice(i * CHUNK, (i + 1) * CHUNK)
        total = nn(parts[0][0, at, :], turned[0])
        for part in range(1, 3):
            total = total + nn(parts[part][0, at, :], turned[part])
        ahead[i] = total

    def leave(i):
        at = slice(i * CHUNK, (i + 1) * CHUNK)
        normed_grad = ahead.pop(i)
        total = norm_back(hat[at], rate[at], vec[8:9, :], normed_grad)
        total = total + state_grad[0, at, :].astype(F32)
        grad = total * d_two[0, at, :].astype(F32)
        second_grad[0, at, :] = grad.astype(BF)
        sums[0:1, :] += col_sum(grad)
        sums[1:2, :] += col_sum(normed_grad)
        sums[2:3, :] += col_sum(dq[0, at, :].astype(F32))
        sums[3:4, :] += col_sum(dv[0, at, :].astype(F32))
        sums[4:5, :] += col_sum(normed_grad * hat[at])

    def gather(i):
        for part in range(i, 3, rows // CHUNK):
            acc[part] += nn(normed_turn, parts[part][0])

    staggered(rows // CHUNK, enter, gather, leave)

    @pl.when((clip == pl.num_programs(0) - 1) & (step == pl.num_programs(1) - 1))
    def _():
        for part in range(3):
            packed[:, part * UNIT : (part + 1) * UNIT, :] = (
                acc[part].astype(BF).reshape(GROUPS, UNIT, D)
            )


def stem_back_kernel(
    grad_ref, a_even, a_odd, d_even, d_odd, ce, co, w, qkv_sums, mlp_sums, up_cols,
    f_even, f_odd, packed, acc, w_acc, buf, extra, turned,
):
    clip = pl.program_id(0)
    step = pl.program_id(1)
    rows = grad_ref.shape[1]

    @pl.when((clip == 0) & (step == 0))
    def _():
        acc[...] = jnp.zeros_like(acc)
        w_acc[...] = jnp.zeros_like(w_acc)
        for part in range(3):
            turned[part] = unit_rows(w, (1 + part) * UNIT).T

    @pl.when(step == 0)
    def _():
        buf[rows : rows + 8, :] = jnp.zeros((8, D), F32)

    @pl.when(step > 0)
    def _():
        buf[rows : rows + 8, :] = buf[0:8, :]

    grad = grad_ref[0]
    buf[0:rows, :] = grad.astype(F32)
    after = buf[1 : rows + 1, :].astype(BF)
    even_grad = nn(grad, turned[1])
    odd_grad = nn(grad, turned[2]) + nn(after, turned[0])
    even_grad = (even_grad * d_even[0].astype(F32)).astype(BF)
    odd_grad = (odd_grad * d_odd[0].astype(F32)).astype(BF)
    f_even[0] = even_grad
    f_odd[0] = odd_grad
    odd_turn = a_odd[0].T
    acc[0] += nn(odd_turn, after)
    acc[1] += nn(a_even[0].T, grad)
    acc[2] += nn(odd_turn, grad)
    w_acc[...] += tn(ce[0], even_grad) + tn(co[0], odd_grad)

    @pl.when((clip == pl.num_programs(0) - 1) & (step == pl.num_programs(1) - 1))
    def _():
        for part in range(3):
            at = (1 + part) * UNIT
            packed[:, at : at + UNIT, :] = acc[part].astype(BF).reshape(GROUPS, UNIT, D)
        extra[...] = jnp.zeros_like(extra)
        extra[113:117, :] = qkv_sums[0:4, :]
        extra[117:120, :] = mlp_sums[0:3, :]
        extra[120:121, :] = qkv_sums[4:5, :]
        extra[121:122, :] = mlp_sums[3:4, :]
        extra[122:126, :] = up_cols[0:4, :]
        w_acc[128:256, :] += extra[...]
        small = jnp.concatenate([w_acc[...].T, jnp.zeros((D, D - 256), F32)], axis=1)
        packed[:, 0:UNIT, :] = small.astype(BF).reshape(GROUPS, UNIT, D)


def mel_kernel(frames, bins, spans, f_even, f_odd, w, out, mel_w, down_buf, up_buf, tall):
    clip = pl.program_id(0)
    rows = f_even.shape[1]

    @pl.when(clip == 0)
    def _():
        first_w = unit_rows(w, 0)[:, 0:256].astype(F32)
        lane = lax.broadcasted_iota(jnp.int32, (D, 128), 1)
        low, high = first_w[:, 0:128], first_w[:, 128:256]
        wrap = 2 * bins - 128
        keep = lane < bins
        zero = jnp.zeros((D, 128), BF)
        taps = (
            jnp.where(keep, low, 0.0).astype(BF),
            jnp.where(
                keep,
                jnp.where(lane < 128 - bins, pltpu.roll(low, 128 - bins, 1), pltpu.roll(high, 128 - bins, 1)),
                0.0,
            ).astype(BF),
            jnp.where(keep, pltpu.roll(high, 128 - wrap, 1), 0.0).astype(BF),
        )
        for at, tap in enumerate((taps[1], taps[2], zero, taps[0])):
            mel_w[0:D, at * 128 : (at + 1) * 128] = tap
        for at, tap in enumerate((taps[0], taps[1], taps[2], zero)):
            mel_w[D : 2 * D, at * 128 : (at + 1) * 128] = tap

    full = nn(f_even[0], mel_w[0:D, :]) + nn(f_odd[0], mel_w[D : 2 * D, :])
    down_buf[0:8, :] = jnp.zeros((8, 128), F32)
    down_buf[8 : 8 + rows, :] = full[:, 256:384]
    up_buf[0:rows, :] = full[:, 384:512]
    up_buf[rows : rows + 8, :] = jnp.zeros((8, 128), F32)
    tall[pl.ds(0, rows, stride=2), :] = full[:, 0:128] + down_buf[7 : 7 + rows, :]
    tall[pl.ds(1, rows, stride=2), :] = full[:, 128:256] + up_buf[1 : rows + 1, :]
    turned = tall[...].T[0:bins, 0:frames]
    place = lax.broadcasted_iota(jnp.int32, (bins, frames), 1)
    bin_at = lax.broadcasted_iota(jnp.int32, (bins, frames), 0)
    time_keep = (place < spans[clip, 0]) | (place >= spans[clip, 0] + spans[clip, 1])
    freq_keep = (bin_at < spans[clip, 2]) | (bin_at >= spans[clip, 2] + spans[clip, 3])
    out[0] = jnp.where(time_keep & freq_keep, turned, 0.0)


def whole(shape):
    return pl.BlockSpec(shape, lambda *_: (0,) * len(shape), pipeline_mode=pl.Buffered(1))


def params(semantics):
    return pltpu.CompilerParams(
        vmem_limit_bytes=VMEM, dimension_semantics=("arbitrary",) * semantics
    )


def cost(flops, moved):
    return pl.CostEstimate(flops=int(flops), bytes_accessed=int(moved), transcendentals=0)


SMEM = pl.BlockSpec(memory_space=pltpu.SMEM)


def ordered(kernel, operands, specs, token):
    if token is None:
        return kernel, operands, specs
    place = len(specs)

    def inner(*refs):
        kernel(*refs[:place], *refs[place + 1 :])

    return inner, list(operands) + [token], list(specs) + [whole(token.shape)]


def call_prepare(spans, mels, padded):
    clips, bins, frames = mels.shape
    row = pl.BlockSpec((1, padded, 256), lambda c: (c, 0, 0))
    return pl.pallas_call(
        functools.partial(prepare_kernel, frames, bins),
        grid=(clips,),
        in_specs=[SMEM, pl.BlockSpec((1, bins, frames), lambda c: (c, 0, 0))],
        out_specs=[row, row],
        out_shape=[jax.ShapeDtypeStruct((clips, padded, 256), BF)] * 2,
        scratch_shapes=[
            pltpu.VMEM((128, 2 * padded), F32),
            pltpu.VMEM((2 * padded + 16, 128), F32),
        ],
        compiler_params=params(1),
        cost_estimate=cost(8e9, clips * padded * 2048),
        name="mel_prepare",
    )(spans, mels)


def call_stem(order, ce, co, pos, mine, other):
    clips, padded, _ = ce.shape
    row = lambda width: pl.BlockSpec((1, ROWS, width), lambda i, c: (c, i, 0))
    out = lambda width, kind: jax.ShapeDtypeStruct((clips, padded, width), kind)
    return pl.pallas_call(
        stem_kernel,
        grid=(padded // ROWS, clips),
        in_specs=[
            SMEM, row(256), row(256), pl.BlockSpec((ROWS, D), lambda i, c: (i, 0)),
            whole(mine.shape), whole(other.shape),
        ],
        out_specs=[row(D)] * 6 + [whole((GROUPS, 4 * UNIT, D)), whole((UNIT, D))],
        out_shape=[out(D, BF)] * 5 + [
            out(D, F32),
            jax.ShapeDtypeStruct((GROUPS, 4 * UNIT, D), BF),
            jax.ShapeDtypeStruct((UNIT, D), F32),
        ],
        scratch_shapes=[pltpu.VMEM((clips, ROWS + 8, D), F32), pltpu.VMEM((256, D), BF)],
        compiler_params=params(2),
        cost_estimate=cost(24e9, clips * padded * 9000),
        name="stem_forward",
    )(order, ce, co, pos, mine, other)


def call_project(stream, w, vec):
    clips, padded, _ = stream.shape
    row = lambda width: pl.BlockSpec((1, ROWS, width), lambda c, i: (c, i, 0))
    return pl.pallas_call(
        project_kernel,
        grid=(clips, padded // ROWS),
        in_specs=[row(D), whole(w.shape), whole(vec.shape)],
        out_specs=row(3 * D),
        out_shape=jax.ShapeDtypeStruct((clips, padded, 3 * D), BF),
        compiler_params=params(2),
        cost_estimate=cost(10e9, clips * padded * 5000),
        name="projection_forward",
    )(stream, w, vec)


def call_attend(qkv, length):
    clips, padded, _ = qkv.shape
    query = pl.BlockSpec((1, ROWS, 128), lambda c, h, i: (c, i, h))
    whole_rows = lambda at: pl.BlockSpec((1, padded, 128), lambda c, h, i: (c, 0, at + h))
    return pl.pallas_call(
        functools.partial(attend_kernel, length),
        grid=(clips, PAIRS, padded // ROWS),
        in_specs=[whole_rows(0), whole_rows(PAIRS), whole_rows(2 * PAIRS)],
        out_specs=[
            pl.BlockSpec((1, 2, ROWS, padded), lambda c, h, i: (c, h, i, 0)),
            query,
            query,
            query,
        ],
        out_shape=[
            jax.ShapeDtypeStruct((clips, HEADS, padded, padded), BF),
            jax.ShapeDtypeStruct((clips, padded, D), BF),
            jax.ShapeDtypeStruct((clips, padded, D), BF),
            jax.ShapeDtypeStruct((clips, padded, D), F32),
        ],
        scratch_shapes=[
            pltpu.VMEM((2, 128, padded), BF),
            pltpu.VMEM((padded, 256), BF),
            pltpu.SMEM((1,), F32),
        ],
        compiler_params=params(3),
        cost_estimate=cost(50e9, clips * padded * padded * 16),
        name="attention_forward",
    )(qkv, qkv, qkv)


def call_attend_back(clip, weights, grad, attended, low_part, inverse, qkv, earlier, token):
    clips, padded, _ = qkv.shape
    query = pl.BlockSpec((1, ROWS, 128), lambda h, i: (clip, i, h))
    keys = lambda at: pl.BlockSpec((1, padded, 128), lambda h, i: (clip, 0, at + h))
    shape = jax.ShapeDtypeStruct((clips, padded, D), BF)
    aliases = {}
    extra = []
    extra_specs = []
    if earlier is not None:
        extra = list(earlier)
        extra_specs = [pl.BlockSpec(memory_space=pl.ANY)] * 3
        aliases = {8: 0, 9: 1, 10: 2}
    kernel, operands, specs = ordered(
        functools.partial(attend_back_kernel, 0 if earlier is None else 1),
        [weights, grad, attended, low_part, inverse, qkv, qkv, qkv] + extra,
        [
            pl.BlockSpec((1, 2, ROWS, padded), lambda h, i: (clip, h, i, 0)),
            query, query, query, query, query, keys(PAIRS), keys(2 * PAIRS),
        ] + extra_specs,
        token,
    )
    return pl.pallas_call(
        kernel,
        grid=(PAIRS, padded // ROWS),
        in_specs=specs,
        out_specs=[query, keys(0), keys(0)],
        out_shape=[shape] * 3,
        scratch_shapes=[pltpu.VMEM((128, padded), F32)] * 2
        + [pltpu.VMEM((2, 256, padded), BF), pltpu.VMEM((2, ROWS, padded), BF)],
        input_output_aliases=aliases,
        compiler_params=params(2),
        cost_estimate=cost(40e9, padded * padded * 16),
        name="attention_backward",
    )(*operands)


def call_mlp(live, attended, stream, cot, w, vec, up_bias):
    clips, padded, _ = attended.shape
    row = pl.BlockSpec((1, ROWS, D), lambda i, c: (c, i, 0))
    return pl.pallas_call(
        functools.partial(mlp_kernel, cot.shape[1]),
        grid=(padded // ROWS, clips),
        in_specs=[SMEM, row, row, row, whole(w.shape), whole(vec.shape), whole(up_bias.shape)],
        out_specs=[
            pl.BlockSpec((ROWS * clips, D), lambda i, c: (i, 0)), row, row,
            whole((GROUPS, 9 * UNIT, D)), whole((8, D)), whole((8, FF)),
        ],
        out_shape=[
            jax.ShapeDtypeStruct((cot.shape[1] * clips, D), BF),
            jax.ShapeDtypeStruct(attended.shape, BF),
            jax.ShapeDtypeStruct(attended.shape, BF),
            jax.ShapeDtypeStruct((GROUPS, 9 * UNIT, D), BF),
            jax.ShapeDtypeStruct((8, D), F32),
            jax.ShapeDtypeStruct((8, FF), F32),
        ],
        scratch_shapes=[
            pltpu.VMEM((D, D), F32),
            pltpu.VMEM((FF // D, D, D), F32),
            pltpu.VMEM((FF // D, D, D), F32),
            pltpu.VMEM((D, D), BF),
            pltpu.VMEM((FF, D), BF),
            pltpu.VMEM((FF // D, D, D), BF),
            pltpu.VMEM((D // 128, ROWS * clips, 128), F32),
            pltpu.VMEM((ROWS, FF), BF),
            pltpu.VMEM((ROWS, FF), BF),
        ],
        compiler_params=params(2),
        cost_estimate=cost(60e9, clips * padded * 8000),
        name="mlp_both_ways",
    )(live, attended, stream, cot, w, vec, up_bias)


def call_qkv_back(grads, stream, state_grad, d_two, w, vec, token):
    clips, padded, _ = stream.shape
    row = pl.BlockSpec((1, ROWS, D), lambda c, i: (c, i, 0))
    kernel, operands, specs = ordered(
        qkv_back_kernel,
        [*grads, stream, state_grad, d_two, w, vec],
        [row] * 6 + [whole(w.shape), whole(vec.shape)],
        token,
    )
    return pl.pallas_call(
        kernel,
        grid=(clips, padded // ROWS),
        in_specs=specs,
        out_specs=[row, whole((GROUPS, 3 * UNIT, D)), whole((8, D))],
        out_shape=[
            jax.ShapeDtypeStruct(stream.shape, BF),
            jax.ShapeDtypeStruct((GROUPS, 3 * UNIT, D), BF),
            jax.ShapeDtypeStruct((8, D), F32),
        ],
        scratch_shapes=[pltpu.VMEM((3, D, D), F32), pltpu.VMEM((3, D, D), BF)],
        compiler_params=params(2),
        cost_estimate=cost(18e9, clips * padded * 9000),
        name="projection_backward",
    )(*operands)


def call_stem_back(second_grad, a_even, a_odd, d_even, d_odd, ce, co, w, sums, token):
    clips, padded, _ = second_grad.shape
    last = padded // ROWS - 1
    row = lambda width: pl.BlockSpec((1, ROWS, width), lambda c, i: (c, last - i, 0))
    kernel, operands, specs = ordered(
        stem_back_kernel,
        [second_grad, a_even, a_odd, d_even, d_odd, ce, co, w, *sums],
        [row(D)] * 5 + [row(256)] * 2 + [whole(w.shape)] + [whole((8, D))] * 3,
        token,
    )
    return pl.pallas_call(
        kernel,
        grid=(clips, padded // ROWS),
        in_specs=specs,
        out_specs=[row(D), row(D), whole((GROUPS, 4 * UNIT, D))],
        out_shape=[
            jax.ShapeDtypeStruct(second_grad.shape, BF),
            jax.ShapeDtypeStruct(second_grad.shape, BF),
            jax.ShapeDtypeStruct((GROUPS, 4 * UNIT, D), BF),
        ],
        scratch_shapes=[
            pltpu.VMEM((3, D, D), F32),
            pltpu.VMEM((256, D), F32),
            pltpu.VMEM((ROWS + 8, D), F32),
            pltpu.VMEM((128, D), F32),
            pltpu.VMEM((3, D, D), BF),
        ],
        compiler_params=params(2),
        cost_estimate=cost(18e9, clips * padded * 9000),
        name="stem_backward",
    )(*operands)


def call_mel(spans, f_even, f_odd, w, frames, bins, token):
    clips, padded, _ = f_even.shape
    row = pl.BlockSpec((1, padded, D), lambda c: (c, 0, 0))
    kernel, operands, specs = ordered(
        functools.partial(mel_kernel, frames, bins),
        [spans, f_even, f_odd, w],
        [SMEM, row, row, whole(w.shape)],
        token,
    )
    return pl.pallas_call(
        kernel,
        grid=(clips,),
        in_specs=specs,
        out_specs=pl.BlockSpec((1, bins, frames), lambda c: (c, 0, 0)),
        out_shape=jax.ShapeDtypeStruct((clips, bins, frames), F32),
        scratch_shapes=[
            pltpu.VMEM((2 * D, D), BF),
            pltpu.VMEM((padded + 8, 128), F32),
            pltpu.VMEM((padded + 8, 128), F32),
            pltpu.VMEM((2 * padded, 128), F32),
        ],
        compiler_params=params(1),
        cost_estimate=cost(8e9, clips * padded * 4000),
        name="mel_backward",
    )(*operands)


def call_after(x, token):
    hold = pl.BlockSpec(memory_space=pl.ANY)

    def kernel(held, ready, passed):
        del held, ready, passed

    return pl.pallas_call(
        kernel,
        in_specs=[hold, pl.BlockSpec(token.shape, lambda: (0, 0))],
        out_specs=hold,
        out_shape=jax.ShapeDtypeStruct(x.shape, x.dtype),
        input_output_aliases={0: 0},
        name="after_stage",
    )(x, token)


def swap(x, mask, count):
    return lax.ppermute(x, "dp", [(i, i ^ mask) for i in range(count)])


def stages(count):
    bits = count.bit_length() - 1
    return [(0, 1)] + [(at, min(2, bits - at)) for at in range(1, bits, 2)]


def gather_xor(x, count, index, filler):
    held = x[None]
    where = jnp.zeros((count,), jnp.int32)
    apart = jnp.arange(count, dtype=jnp.int32) ^ index
    token = None
    parts = None
    for first, many in reversed(stages(count)):
        if parts is not None:
            if first == 0:
                parts[-1] = parts[-1] + filler
            held = jnp.concatenate(parts)
        where = where + ((apart >> first) & ((1 << many) - 1)) * held.shape[0]
        parts = [held] + [swap(held, rel << first, count) for rel in range(1, 1 << many)]
        if first > 0:
            token = parts[-1]
    return parts, where, token


class Scatter:
    def __init__(self, x, count, index):
        self.held, self.count, self.index = x, count, index
        self.plan = stages(count)

    def step(self):
        if not self.plan:
            return None
        first, many = self.plan.pop(0)
        radix = 1 << many
        held = self.held
        split = held.reshape((held.shape[0] // radix, radix) + held.shape[1:])
        mine = (self.index >> first) & (radix - 1)
        take = lambda at: lax.dynamic_index_in_dim(split, at, 1, keepdims=False)
        got = [swap(take(mine ^ rel), rel << first, self.count) for rel in range(1, radix)]
        total = take(mine).astype(F32)
        for piece in got:
            total = total + piece.astype(F32)
        self.held = total.astype(BF) if self.plan else total
        return total[0, :1, :128]

    def join(self, other):
        self.held = jnp.concatenate([self.held, other.held], axis=1)

    def owned(self):
        while self.plan:
            self.step()
        return self.held[0]


def rows_of(gathered, first, parts, unit):
    taken = gathered[:, first * unit : (first + parts) * unit]
    return taken.reshape(GROUPS, parts * UNIT, gathered.shape[2])


def to_groups(gathered, pieces, unit):
    if unit == UNIT:
        return gathered
    out = []
    at = 0
    for parts in pieces:
        out.append(rows_of(gathered, at, parts, unit))
        at += parts
    return jnp.concatenate(out, axis=1)


def from_groups(packed, pieces, count):
    unit = D // count
    if unit == UNIT:
        return packed
    out = []
    at = 0
    for parts in pieces:
        piece = packed[:, at * UNIT : (at + parts) * UNIT]
        out.append(piece.reshape(count, parts * unit, D))
        at += parts
    return jnp.concatenate(out, axis=1)


def position_table(frames):
    half = D // 2
    rate = np.exp(-(math.log(10000.0) / (half - 1)) * np.arange(half, dtype=np.float64))
    angle = np.arange(frames, dtype=np.float64)[:, None] * rate[None, :]
    return np.concatenate([np.sin(angle), np.cos(angle)], axis=1).astype(np.float32)


def per_device(
    count, log_mels, mask_spans, live_slots, first_conv, second_conv, biases, norm_gains,
    qkv_weight, out_weight, up_weight, up_bias, down_weight, cotangent,
):
    clips, frames, bins = log_mels.shape
    length = frames // 2
    padded = -(-length // ROWS) * ROWS
    index = lax.axis_index("dp")
    unit = D // count
    tap_lanes = 3 * bins
    ups = FF // D

    small = jnp.concatenate(
        [
            first_conv.reshape(tap_lanes, unit).T,
            biases.T,
            norm_gains.T,
            up_bias.reshape(unit, ups),
            jnp.zeros((unit, D - tap_lanes - 10 - ups), BF),
        ],
        axis=1,
    )
    near = jnp.concatenate([small, second_conv.reshape(3 * unit, D)])
    col_even, col_odd = call_prepare(mask_spans, log_mels.transpose(0, 2, 1), padded)
    parts, order, token = gather_xor(near, count, index, col_even[0, padded - 1, 255])
    if unit != UNIT:
        near = jnp.take(jnp.concatenate(parts), order, axis=0)
        near = to_groups(near, (1,) * 4, unit)
        parts = (near[: GROUPS // 2], near[GROUPS // 2 :])
        order = jnp.arange(GROUPS, dtype=jnp.int32)
    qkv_w = qkv_weight.transpose(1, 0, 2).reshape(3 * unit, D)
    qkv_w = to_groups(lax.all_gather(qkv_w, "dp", axis=0, tiled=False), (1,) * 3, unit)
    far = jnp.concatenate(
        [
            out_weight,
            up_weight.reshape(unit, ups, D).transpose(1, 0, 2).reshape(ups * unit, D),
            down_weight,
        ]
    )
    far = far + token[0, 0, D - 1]
    far = lax.all_gather(far, "dp", axis=0, tiled=False)
    far = to_groups(far, (1,) * (1 + ups) + (ups,), unit)

    table = jnp.asarray(position_table(padded))
    a_even, a_odd, d_even, d_odd, d_two, stream, near, vec = call_stem(
        order, col_even, col_odd, table, *parts
    )
    qkv = call_project(stream, qkv_w, vec)
    up_row = jnp.pad(vec[10 : 10 + ups].T.reshape(1, FF), ((0, 7), (0, 0)))
    weights, attended, low_part, inverse = call_attend(qkv, length)
    encoded, att_grad, state_grad, mlp_packed, mlp_sums, up_sums = call_mlp(
        live_slots, attended, stream, cotangent, far, vec, up_row
    )
    mlp_packed = from_groups(mlp_packed, (1,) * (1 + ups) + (ups,), count)
    mlp_sum = Scatter(mlp_packed, count, index)
    up_cols = jnp.pad(up_sums[0].reshape(D, ups).T, ((0, 8 - ups), (0, 0)))
    grads = None
    for clip in range(clips):
        token = mlp_sum.step() if clip else None
        grads = call_attend_back(
            clip, weights, att_grad, attended, low_part, inverse, qkv, grads, token
        )
    second_grad, qkv_packed, qkv_sums = call_qkv_back(
        grads, stream, state_grad, d_two, qkv_w, vec, mlp_sum.step()
    )
    qkv_sum = Scatter(from_groups(qkv_packed, (1,) * 3, count), count, index)
    f_even, f_odd, stem_packed = call_stem_back(
        second_grad, a_even, a_odd, d_even, d_odd, col_even, col_odd, near,
        (qkv_sums, mlp_sums, up_cols), mlp_sum.step(),
    )
    stem_sum = Scatter(from_groups(stem_packed, (1,) * 4, count), count, index)
    mel_turned = call_mel(mask_spans, f_even, f_odd, near, frames, bins, qkv_sum.step())
    mel_grad = mel_turned.transpose(0, 2, 1)
    encoded = call_after(encoded, stem_sum.step())
    encoded = encoded.reshape(length, clips, D).transpose(1, 0, 2)
    qkv_sum.step()
    stem_sum.step()
    if stem_sum.plan:
        stem_sum.join(qkv_sum)
        owned = stem_sum.owned()
    else:
        owned = jnp.concatenate([stem_sum.owned(), qkv_sum.owned()])
    mlp_owned, stem_owned, qkv_owned = mlp_sum.owned(), owned[: 4 * unit], owned[4 * unit :]

    mixed = stem_owned[:unit]
    bias_grad = mixed[:, tap_lanes : tap_lanes + 8].T
    return (
        encoded,
        mel_grad,
        mixed[:, :tap_lanes].T.reshape(3, bins, unit),
        stem_owned[unit : 4 * unit].reshape(3, unit, D),
        bias_grad,
        mixed[:, tap_lanes + 8 : tap_lanes + 10].T,
        qkv_owned.reshape(3, unit, D).transpose(1, 0, 2),
        mlp_owned[:unit],
        mlp_owned[unit : (1 + ups) * unit]
        .reshape(ups, unit, D)
        .transpose(1, 0, 2)
        .reshape(unit, FF),
        mixed[:, tap_lanes + 10 : tap_lanes + 10 + ups].reshape(ups * unit),
        mlp_owned[(1 + ups) * unit :],
        bias_grad[6],
    )


def solution(mesh):
    return jax.shard_map(
        functools.partial(per_device, mesh.shape["dp"]),
        mesh=mesh,
        in_specs=(
            P("dp", None, None),
            P("dp", None),
            P("dp"),
            P(None, None, "dp"),
            P(None, "dp", None),
            P(None, "dp"),
            P(None, "dp"),
            P("dp", None, None),
            P("dp", None),
            P("dp", None),
            P("dp"),
            P("dp", None),
            P("dp", None, None),
        ),
        out_specs=(
            P("dp", None, None),
            P("dp", None, None),
            P(None, None, "dp"),
            P(None, "dp", None),
            P(None, "dp"),
            P(None, "dp"),
            P("dp", None, None),
            P("dp", None),
            P("dp", None),
            P("dp"),
            P("dp", None),
            P("dp"),
        ),
        check_vma=False,
    )
```

```python
import functools
import math

import jax
import jax.numpy as jnp
import numpy as np
from jax import lax
from jax.experimental import pallas as pl
from jax.experimental.pallas import tpu as pltpu
from jax.sharding import PartitionSpec as P

D = 512
FF = 2048
HEADS = 8
HEAD_DIM = 64
PAIRS = HEADS // 2
ROWS = 768
CHUNK = 256
UNIT = 16
GROUPS = D // UNIT
LN_EPS = 1e-05
SCORE_SCALE = HEAD_DIM ** (-0.5)
LOG2E = math.log2(math.e)
VMEM = 60 * 1024 * 1024
BF = jnp.bfloat16
F32 = jnp.float32


def nn(left, right):
    return lax.dot_general(left, right, (((1,), (0,)), ((), ())), preferred_element_type=F32)


def tn(left, right):
    return lax.dot_general(left, right, (((0,), (0,)), ((), ())), preferred_element_type=F32)


def gelu_both(v):
    phi = 0.5 * lax.erf(v * math.sqrt(0.5)) + 0.5
    bell = jnp.exp2(v * v * (-0.5 * LOG2E))
    return v * phi, phi + v * bell * (1.0 / math.sqrt(2.0 * math.pi))


def staggered(count, *works):
    depth = len(works)
    for at in range(count + depth - 1):
        for lag, work in enumerate(works):
            if 0 <= at - lag < count:
                work(at - lag)


def row_stats(x):
    mean = jnp.mean(x, axis=-1, keepdims=True)
    centred = x - mean
    var = jnp.mean(centred * centred, axis=-1, keepdims=True)
    rate = lax.rsqrt(var + LN_EPS)
    return centred * rate, rate


def norm_back(hat, rate, gain, upstream):
    scaled = upstream * gain
    first = jnp.mean(scaled, axis=-1, keepdims=True)
    second = jnp.mean(scaled * hat, axis=-1, keepdims=True)
    return rate * (scaled - first - hat * second)


def col_sum(x):
    return jnp.sum(x, axis=0, keepdims=True)


def unit_rows(ref, start, count=UNIT):
    block = ref[:, start : start + count, :]
    return block.reshape(GROUPS * count, block.shape[2])


def prepare_kernel(frames, bins, spans, mels, ce, co, flat, tall):
    clip = pl.program_id(0)
    padded = ce.shape[1]
    place = lax.broadcasted_iota(jnp.int32, (bins, frames), 1)
    bin_at = lax.broadcasted_iota(jnp.int32, (bins, frames), 0)
    time_keep = (place < spans[clip, 0]) | (place >= spans[clip, 0] + spans[clip, 1])
    freq_keep = (bin_at < spans[clip, 2]) | (bin_at >= spans[clip, 2] + spans[clip, 3])

    @pl.when(clip == 0)
    def _():
        flat[...] = jnp.zeros_like(flat)
        tall[0:8, :] = jnp.zeros((8, 128), F32)
        tall[8 + 2 * padded :, :] = jnp.zeros((8, 128), F32)

    flat[0:bins, 0:frames] = jnp.where(time_keep & freq_keep, mels[0].astype(F32), 0.0)
    tall[8 : 8 + 2 * padded, :] = flat[...].T
    before, even, odd, after = (tall[pl.ds(7 + k, padded, stride=2), :] for k in range(4))
    lane = lax.broadcasted_iota(jnp.int32, (padded, 128), 1)
    wrap = 2 * bins - 128
    one = jnp.where(lane == wrap + bins, 1.0, 0.0)
    for out, taps in ((ce, (before, even, odd)), (co, (even, odd, after))):
        middle = pltpu.roll(taps[1], bins, 1)
        out[0, :, 0:128] = (taps[0] + jnp.where(lane >= bins, middle, 0.0)).astype(BF)
        last = pltpu.roll(taps[2], wrap, 1)
        out[0, :, 128:256] = (jnp.where(lane < wrap, middle, 0.0) + last + one).astype(BF)


def stem_kernel(
    order, ce, co, pos, mine, other, a_even, a_odd, d_even, d_odd, d_two, stream, w, vec, buf, first_t
):
    step = pl.program_id(0)
    clip = pl.program_id(1)
    rows = ce.shape[1]
    half = GROUPS // 2

    @pl.when((clip == 0) & (step == 0))
    def _():
        for group in range(GROUPS):
            source = order[group]

            @pl.when(source < half)
            def _():
                w[group] = mine[source]

            @pl.when(source >= half)
            def _():
                w[group] = other[source - half]

        turned = unit_rows(w, 0)[:, 0:256].astype(F32).T
        vec[...] = turned[240:256, :]
        first_t[...] = turned.astype(BF)

    @pl.when(step == 0)
    def _():
        buf[clip, 0:8, :] = jnp.zeros((8, D), F32)

    @pl.when(step > 0)
    def _():
        buf[clip, 0:8, :] = buf[clip, rows : rows + 8, :]

    firsts, seconds = {}, {}

    def first_conv(i):
        at = slice(i * CHUNK, (i + 1) * CHUNK)
        firsts[i] = nn(ce[0, at, :], first_t[...]), nn(co[0, at, :], first_t[...])

    def first_gelu(i):
        at = slice(i * CHUNK, (i + 1) * CHUNK)
        even, odd = firsts.pop(i)
        even, slope = gelu_both(even)
        a_even[0, at, :] = even.astype(BF)
        d_even[0, at, :] = slope.astype(BF)
        odd, slope = gelu_both(odd)
        a_odd[0, at, :] = odd.astype(BF)
        d_odd[0, at, :] = slope.astype(BF)
        buf[clip, 8 + i * CHUNK : 8 + (i + 1) * CHUNK, :] = odd

    def second_conv(i):
        at = slice(i * CHUNK, (i + 1) * CHUNK)
        before = buf[clip, 7 + i * CHUNK : 7 + (i + 1) * CHUNK, :].astype(BF)
        second = nn(before, unit_rows(w, UNIT))
        second = second + nn(a_even[0, at, :], unit_rows(w, 2 * UNIT))
        seconds[i] = second + nn(a_odd[0, at, :], unit_rows(w, 3 * UNIT)) + vec[1:2, :]

    def second_gelu(i):
        at = slice(i * CHUNK, (i + 1) * CHUNK)
        wave, slope = gelu_both(seconds.pop(i))
        d_two[0, at, :] = slope.astype(BF)
        stream[0, at, :] = wave + pos[at, :]

    staggered(rows // CHUNK, first_conv, first_gelu, second_conv, second_gelu)


def project_kernel(stream, w, vec, qkv):
    hat, _ = row_stats(stream[0])
    normed = (hat * vec[8:9, :] + vec[2:3, :]).astype(BF)
    queries = nn(normed, unit_rows(w, 0)) + vec[3:4, :]
    qkv[0, :, 0:D] = queries.astype(BF)
    qkv[0, :, D : 2 * D] = nn(normed, unit_rows(w, UNIT)).astype(BF)
    qkv[0, :, 2 * D :] = (nn(normed, unit_rows(w, 2 * UNIT)) + vec[4:5, :]).astype(BF)


def head_mask(shape, head):
    lane = lax.broadcasted_iota(jnp.int32, shape, 1)
    return (lane >= head * HEAD_DIM) & (lane < (head + 1) * HEAD_DIM)


def row_mask(shape, head):
    row = lax.broadcasted_iota(jnp.int32, shape, 0)
    return (row >= head * HEAD_DIM) & (row < (head + 1) * HEAD_DIM)


def attend_kernel(
    length, q_ref, k_ref, v_ref, weights, attended, low_part, inverse, keys_t, wide, reach
):
    step = pl.program_id(2)
    rows = attended.shape[1]
    padded = k_ref.shape[1]

    def longest(x):
        return jnp.max(jnp.sum(jnp.square(x.astype(F32)), axis=1))

    @pl.when(step == 0)
    def _():
        turned = k_ref[0].T
        for head in range(2):
            own = turned[head * HEAD_DIM : (head + 1) * HEAD_DIM, :]
            keys_t[head, 0:HEAD_DIM, :] = own
            keys_t[head, HEAD_DIM : 2 * HEAD_DIM, :] = own
        wide[:, 0 : 2 * HEAD_DIM] = v_ref[0]
        wide[:, 2 * HEAD_DIM :] = jnp.ones((padded, 2 * HEAD_DIM), BF)
        reach[0] = longest(q_ref[0]) * longest(k_ref[0])

    factor = SCORE_SCALE * LOG2E
    calm = reach[0] < (60.0 / factor) ** 2
    scaled = q_ref[0, pl.ds(pl.multiple_of(step * rows, rows), rows), :].astype(F32) * factor
    large = scaled.astype(BF)
    small = pltpu.roll(scaled - large.astype(F32), HEAD_DIM, 1).astype(BF)
    first = head_mask(large.shape, 0)
    queries = (jnp.where(first, large, small), jnp.where(first, small, large))

    def finish(at, mixed):
        rates = [1.0 / mixed[k][:, 2 * HEAD_DIM :] for k in range(2)]
        outs = [mixed[k][:, : 2 * HEAD_DIM] * rates[k] for k in range(2)]
        pick = head_mask(outs[0].shape, 0)
        both = jnp.where(pick, outs[0], outs[1])
        high = both.astype(BF)
        attended[0, at : at + CHUNK, :] = high
        low_part[0, at : at + CHUNK, :] = (both - high.astype(F32)).astype(BF)
        inverse[0, at : at + CHUNK, :] = jnp.where(pick, rates[0], rates[1])

    def bounded(scores, first):
        if first + scores.shape[1] <= length:
            return scores
        place = lax.broadcasted_iota(jnp.int32, scores.shape, 1) + first
        return jnp.where(place < length, scores, -1e30)

    def attend_calm():
        tiles = [
            (at, head, key)
            for at in range(0, rows, CHUNK)
            for head in range(2)
            for key in range(0, padded, CHUNK)
        ]
        scores, soft, mixed = {}, {}, {}

        def score(i):
            at, head, key = tiles[i]
            scores[i] = nn(queries[head][at : at + CHUNK], keys_t[head, :, key : key + CHUNK])

        def soften(i):
            at, head, key = tiles[i]
            soft[i] = jnp.exp2(bounded(scores.pop(i), key)).astype(BF)
            weights[0, head, at : at + CHUNK, key : key + CHUNK] = soft[i]

        def mix(i):
            at, head, key = tiles[i]
            part = nn(soft.pop(i), wide[key : key + CHUNK, :])
            mixed[head] = part if key == 0 else mixed[head] + part
            if head == 1 and key + CHUNK == padded:
                finish(at, mixed)

        staggered(len(tiles), score, soften, mix)

    def attend_shifted():
        for at in range(0, rows, CHUNK):
            mixed = {}
            for head in range(2):
                scores = bounded(nn(queries[head][at : at + CHUNK], keys_t[head]), 0)
                top = jnp.max(scores, axis=1, keepdims=True)
                soft = jnp.exp2(scores - top).astype(BF)
                weights[0, head, at : at + CHUNK, :] = soft
                mixed[head] = nn(soft, wide[...])
            finish(at, mixed)

    @pl.when(calm)
    def _():
        attend_calm()

    @pl.when(jnp.logical_not(calm))
    def _():
        attend_shifted()


def attend_back_kernel(
    aliased, weights, grad_ref, att_ref, low_ref, inv_ref, q_ref, k_ref, v_ref, *rest
):
    rest = rest[3 * aliased :]
    dq, dk, dv, dk_sum, dv_sum, right, score_grad = rest
    step = pl.program_id(1)
    scaled_low = (grad_ref[0].astype(F32) * inv_ref[0]).astype(BF)
    prod = scaled_low.astype(F32) * (att_ref[0].astype(F32) + low_ref[0].astype(F32))
    lane = lax.broadcasted_iota(jnp.int32, prod.shape, 1)
    dots = jnp.zeros(prod.shape, F32)
    for head in range(2):
        dot = -jnp.sum(jnp.where(head_mask(prod.shape, head), prod, 0.0), axis=1, keepdims=True)
        high = dot.astype(BF).astype(F32)
        dots = jnp.where(lane == 2 * head, high, dots)
        dots = jnp.where(lane == 2 * head + 1, dot - high, dots)
    left = jnp.concatenate([scaled_low, dots.astype(BF)], axis=1)
    q_turn = q_ref[0].T
    g_turn = scaled_low.T

    @pl.when(step == 0)
    def _():
        dk_sum[...] = jnp.zeros_like(dk_sum)
        dv_sum[...] = jnp.zeros_like(dv_sum)
        turned = v_ref[0].T
        zero = jnp.zeros_like(turned)
        row = lax.broadcasted_iota(jnp.int32, turned.shape, 0)
        for head in range(2):
            right[head, 0:128, :] = jnp.where(row_mask(turned.shape, head), turned, zero)
            right[head, 128:256, :] = jnp.where(
                (row == 2 * head) | (row == 2 * head + 1), zero + 1, zero
            )

    rows = scaled_low.shape[0]
    parts = [(at, head) for at in range(0, rows, CHUNK) for head in range(2)]
    grads, outs = {}, {}

    def weight_grad(i):
        at, head = parts[i]
        grads[i] = nn(left[at : at + CHUNK], right[head])

    def multiply(i):
        at, head = parts[i]
        soft = weights[0, head, at : at + CHUNK, :].astype(F32)
        score_grad[head, at : at + CHUNK, :] = (soft * grads.pop(i)).astype(BF)

    def query_grad(i):
        at, head = parts[i]
        outs[head] = nn(score_grad[head, at : at + CHUNK, :], k_ref[0])
        if head == 1:
            pick = head_mask(outs[0].shape, 0)
            total = jnp.where(pick, outs[0], outs[1]) * SCORE_SCALE
            dq[0, at : at + CHUNK, :] = total.astype(BF)

    staggered(len(parts), weight_grad, multiply, query_grad)
    for head in range(2):
        span = slice(head * HEAD_DIM, (head + 1) * HEAD_DIM)
        dv_sum[span, :] += nn(g_turn[span, :], weights[0, head])
        dk_sum[span, :] += nn(q_turn[span, :], score_grad[head])

    @pl.when(step == pl.num_programs(1) - 1)
    def _():
        dk[0] = (dk_sum[...].T * SCORE_SCALE).astype(BF)
        dv[0] = dv_sum[...].T.astype(BF)


def mlp_kernel(
    length, live, att, stream, cot, w, vec, up_bias,
    encoded, att_grad, state_grad, packed, sums, up_sums,
    out_acc, up_acc, down_acc, out_t, up_t, down_t, mixed, gated, hidden_grad,
):
    step = pl.program_id(0)
    clip = pl.program_id(1)
    clips = pl.num_programs(1)
    rows = cot.shape[1]
    alive = clip < live[0]

    @pl.when((clip == 0) & (step == 0))
    def _():
        out_acc[...] = jnp.zeros_like(out_acc)
        up_acc[...] = jnp.zeros_like(up_acc)
        down_acc[...] = jnp.zeros_like(down_acc)
        sums[...] = jnp.zeros_like(sums)
        up_sums[...] = jnp.zeros_like(up_sums)
        out_t[...] = unit_rows(w, 0).T
        for part in range(FF // D):
            up_t[part * D : (part + 1) * D, :] = unit_rows(w, (1 + part) * UNIT).T
            down_t[part] = unit_rows(w, 5 * UNIT, 4 * UNIT)[part * D : (part + 1) * D, :].T

    place = lax.broadcasted_iota(jnp.int32, (rows, D), 0) + step * rows
    reach = jnp.where(alive, length, 0)
    cot_float = jnp.where(place < reach, cot[0].astype(F32), 0.0)
    cot_low = cot_float.astype(BF)
    attended = att[0]
    out_w = unit_rows(w, 0)
    after = stream[0] + nn(attended, out_w) + vec[5:6, :]
    hat, rate = row_stats(after)
    normed = (hat * vec[9:10, :] + vec[6:7, :]).astype(BF)
    normed_turn = normed.T
    cot_turn = cot_low.T
    spans = [slice(part * D, (part + 1) * D) for part in range(FF // D)]
    ahead = {}
    sides = [after + vec[7:8, :], None]

    def enter(part):
        ahead[part] = (
            nn(normed, unit_rows(w, (1 + part) * UNIT)) + up_bias[0:1, spans[part]],
            nn(cot_low, down_t[part]),
        )

    def activate(part):
        hidden, grad = ahead.pop(part)
        wave, slope = gelu_both(hidden)
        gated[:, spans[part]] = wave.astype(BF)
        grad = grad * slope
        up_sums[0:1, spans[part]] += col_sum(grad)
        hidden_grad[:, spans[part]] = grad.astype(BF)

    def leave(part):
        wave, grad = gated[:, spans[part]], hidden_grad[:, spans[part]]
        down_w = unit_rows(w, 5 * UNIT, 4 * UNIT)[spans[part], :]
        back = nn(grad, up_t[spans[part], :])
        sides[0] = sides[0] + nn(wave, down_w)
        sides[1] = back if sides[1] is None else sides[1] + back
        up_acc[part] += nn(normed_turn, grad)
        down_acc[part] += nn(cot_turn, wave)

    staggered(FF // D, enter, activate, leave)
    result, normed_grad = sides
    result = jnp.where(alive, result, 0.0)
    slots = mixed.shape[1] // rows
    for slot in range(slots):

        @pl.when(clip == slot)
        def _():
            for part in range(D // 128):
                lanes = slice(part * 128, (part + 1) * 128)
                mixed[part, pl.ds(slot, rows, stride=slots), :] = result[:, lanes]

    @pl.when(clip == clips - 1)
    def _():
        for part in range(D // 128):
            encoded[:, part * 128 : (part + 1) * 128] = mixed[part].astype(BF)

    total = cot_float + norm_back(hat, rate, vec[9:10, :], normed_grad)
    low = total.astype(BF)
    state_grad[0] = low
    sums[0:1, :] += col_sum(total)
    sums[1:2, :] += col_sum(normed_grad)
    sums[2:3, :] += col_sum(cot_float)
    sums[3:4, :] += col_sum(normed_grad * hat)
    att_grad[0] = nn(low, out_t[...]).astype(BF)
    out_acc[...] += tn(attended, low)

    @pl.when((clip == clips - 1) & (step == pl.num_programs(0) - 1))
    def _():
        packed[:, 0:UNIT, :] = out_acc[...].astype(BF).reshape(GROUPS, UNIT, D)
        for part in range(FF // D):
            at = (1 + part) * UNIT
            packed[:, at : at + UNIT, :] = up_acc[part].astype(BF).reshape(GROUPS, UNIT, D)
            owners = GROUPS // (FF // D)
            packed[part * owners : (part + 1) * owners, 5 * UNIT : 9 * UNIT, :] = (
                down_acc[part].T.astype(BF).reshape(owners, 4 * UNIT, D)
            )


def qkv_back_kernel(
    dq, dk, dv, stream, state_grad, d_two, w, vec, second_grad, packed, sums, acc, turned
):
    clip = pl.program_id(0)
    step = pl.program_id(1)

    @pl.when((clip == 0) & (step == 0))
    def _():
        acc[...] = jnp.zeros_like(acc)
        sums[...] = jnp.zeros_like(sums)
        for part in range(3):
            turned[part] = unit_rows(w, part * UNIT).T

    parts = (dq, dk, dv)
    rows = stream.shape[1]
    hat, rate = row_stats(stream[0])
    normed_turn = (hat * vec[8:9, :] + vec[2:3, :]).astype(BF).T
    ahead = {}

    def enter(i):
        at = slice(i * CHUNK, (i + 1) * CHUNK)
        total = nn(parts[0][0, at, :], turned[0])
        for part in range(1, 3):
            total = total + nn(parts[part][0, at, :], turned[part])
        ahead[i] = total

    def leave(i):
        at = slice(i * CHUNK, (i + 1) * CHUNK)
        normed_grad = ahead.pop(i)
        total = norm_back(hat[at], rate[at], vec[8:9, :], normed_grad)
        total = total + state_grad[0, at, :].astype(F32)
        grad = total * d_two[0, at, :].astype(F32)
        second_grad[0, at, :] = grad.astype(BF)
        sums[0:1, :] += col_sum(grad)
        sums[1:2, :] += col_sum(normed_grad)
        sums[2:3, :] += col_sum(dq[0, at, :].astype(F32))
        sums[3:4, :] += col_sum(dv[0, at, :].astype(F32))
        sums[4:5, :] += col_sum(normed_grad * hat[at])

    def gather(i):
        for part in range(i, 3, rows // CHUNK):
            acc[part] += nn(normed_turn, parts[part][0])

    staggered(rows // CHUNK, enter, gather, leave)

    @pl.when((clip == pl.num_programs(0) - 1) & (step == pl.num_programs(1) - 1))
    def _():
        for part in range(3):
            packed[:, part * UNIT : (part + 1) * UNIT, :] = (
                acc[part].astype(BF).reshape(GROUPS, UNIT, D)
            )


def stem_back_kernel(
    grad_ref, a_even, a_odd, d_even, d_odd, ce, co, w, qkv_sums, mlp_sums, up_cols,
    f_even, f_odd, packed, acc, w_acc, buf, extra, turned,
):
    clip = pl.program_id(0)
    step = pl.program_id(1)
    rows = grad_ref.shape[1]

    @pl.when((clip == 0) & (step == 0))
    def _():
        acc[...] = jnp.zeros_like(acc)
        w_acc[...] = jnp.zeros_like(w_acc)
        for part in range(3):
            turned[part] = unit_rows(w, (1 + part) * UNIT).T

    @pl.when(step == 0)
    def _():
        buf[rows : rows + 8, :] = jnp.zeros((8, D), F32)

    @pl.when(step > 0)
    def _():
        buf[rows : rows + 8, :] = buf[0:8, :]

    grad = grad_ref[0]
    buf[0:rows, :] = grad.astype(F32)
    after = buf[1 : rows + 1, :].astype(BF)
    even_grad = nn(grad, turned[1])
    odd_grad = nn(grad, turned[2]) + nn(after, turned[0])
    even_grad = (even_grad * d_even[0].astype(F32)).astype(BF)
    odd_grad = (odd_grad * d_odd[0].astype(F32)).astype(BF)
    f_even[0] = even_grad
    f_odd[0] = odd_grad
    odd_turn = a_odd[0].T
    acc[0] += nn(odd_turn, after)
    acc[1] += nn(a_even[0].T, grad)
    acc[2] += nn(odd_turn, grad)
    w_acc[...] += tn(ce[0], even_grad) + tn(co[0], odd_grad)

    @pl.when((clip == pl.num_programs(0) - 1) & (step == pl.num_programs(1) - 1))
    def _():
        for part in range(3):
            at = (1 + part) * UNIT
            packed[:, at : at + UNIT, :] = acc[part].astype(BF).reshape(GROUPS, UNIT, D)
        extra[...] = jnp.zeros_like(extra)
        extra[113:117, :] = qkv_sums[0:4, :]
        extra[117:120, :] = mlp_sums[0:3, :]
        extra[120:121, :] = qkv_sums[4:5, :]
        extra[121:122, :] = mlp_sums[3:4, :]
        extra[122:126, :] = up_cols[0:4, :]
        w_acc[128:256, :] += extra[...]
        small = jnp.concatenate([w_acc[...].T, jnp.zeros((D, D - 256), F32)], axis=1)
        packed[:, 0:UNIT, :] = small.astype(BF).reshape(GROUPS, UNIT, D)


def mel_kernel(frames, bins, spans, f_even, f_odd, w, out, mel_w, down_buf, up_buf, tall):
    clip = pl.program_id(0)
    rows = f_even.shape[1]

    @pl.when(clip == 0)
    def _():
        first_w = unit_rows(w, 0)[:, 0:256].astype(F32)
        lane = lax.broadcasted_iota(jnp.int32, (D, 128), 1)
        low, high = first_w[:, 0:128], first_w[:, 128:256]
        wrap = 2 * bins - 128
        keep = lane < bins
        zero = jnp.zeros((D, 128), BF)
        taps = (
            jnp.where(keep, low, 0.0).astype(BF),
            jnp.where(
                keep,
                jnp.where(lane < 128 - bins, pltpu.roll(low, 128 - bins, 1), pltpu.roll(high, 128 - bins, 1)),
                0.0,
            ).astype(BF),
            jnp.where(keep, pltpu.roll(high, 128 - wrap, 1), 0.0).astype(BF),
        )
        for at, tap in enumerate((taps[1], taps[2], zero, taps[0])):
            mel_w[0:D, at * 128 : (at + 1) * 128] = tap
        for at, tap in enumerate((taps[0], taps[1], taps[2], zero)):
            mel_w[D : 2 * D, at * 128 : (at + 1) * 128] = tap

    full = nn(f_even[0], mel_w[0:D, :]) + nn(f_odd[0], mel_w[D : 2 * D, :])
    down_buf[0:8, :] = jnp.zeros((8, 128), F32)
    down_buf[8 : 8 + rows, :] = full[:, 256:384]
    up_buf[0:rows, :] = full[:, 384:512]
    up_buf[rows : rows + 8, :] = jnp.zeros((8, 128), F32)
    tall[pl.ds(0, rows, stride=2), :] = full[:, 0:128] + down_buf[7 : 7 + rows, :]
    tall[pl.ds(1, rows, stride=2), :] = full[:, 128:256] + up_buf[1 : rows + 1, :]
    turned = tall[...].T[0:bins, 0:frames]
    place = lax.broadcasted_iota(jnp.int32, (bins, frames), 1)
    bin_at = lax.broadcasted_iota(jnp.int32, (bins, frames), 0)
    time_keep = (place < spans[clip, 0]) | (place >= spans[clip, 0] + spans[clip, 1])
    freq_keep = (bin_at < spans[clip, 2]) | (bin_at >= spans[clip, 2] + spans[clip, 3])
    out[0] = jnp.where(time_keep & freq_keep, turned, 0.0)


def whole(shape):
    return pl.BlockSpec(shape, lambda *_: (0,) * len(shape), pipeline_mode=pl.Buffered(1))


def params(semantics):
    return pltpu.CompilerParams(
        vmem_limit_bytes=VMEM, dimension_semantics=("arbitrary",) * semantics
    )


def cost(flops, moved):
    return pl.CostEstimate(flops=int(flops), bytes_accessed=int(moved), transcendentals=0)


SMEM = pl.BlockSpec(memory_space=pltpu.SMEM)


def ordered(kernel, operands, specs, token):
    if token is None:
        return kernel, operands, specs
    place = len(specs)

    def inner(*refs):
        kernel(*refs[:place], *refs[place + 1 :])

    return inner, list(operands) + [token], list(specs) + [whole(token.shape)]


def call_prepare(spans, mels, padded):
    clips, bins, frames = mels.shape
    row = pl.BlockSpec((1, padded, 256), lambda c: (c, 0, 0))
    return pl.pallas_call(
        functools.partial(prepare_kernel, frames, bins),
        grid=(clips,),
        in_specs=[SMEM, pl.BlockSpec((1, bins, frames), lambda c: (c, 0, 0))],
        out_specs=[row, row],
        out_shape=[jax.ShapeDtypeStruct((clips, padded, 256), BF)] * 2,
        scratch_shapes=[
            pltpu.VMEM((128, 2 * padded), F32),
            pltpu.VMEM((2 * padded + 16, 128), F32),
        ],
        compiler_params=params(1),
        cost_estimate=cost(8e9, clips * padded * 2048),
        name="mel_prepare",
    )(spans, mels)


def call_stem(order, ce, co, pos, mine, other):
    clips, padded, _ = ce.shape
    row = lambda width: pl.BlockSpec((1, ROWS, width), lambda i, c: (c, i, 0))
    out = lambda width, kind: jax.ShapeDtypeStruct((clips, padded, width), kind)
    return pl.pallas_call(
        stem_kernel,
        grid=(padded // ROWS, clips),
        in_specs=[
            SMEM, row(256), row(256), pl.BlockSpec((ROWS, D), lambda i, c: (i, 0)),
            whole(mine.shape), whole(other.shape),
        ],
        out_specs=[row(D)] * 6 + [whole((GROUPS, 4 * UNIT, D)), whole((UNIT, D))],
        out_shape=[out(D, BF)] * 5 + [
            out(D, F32),
            jax.ShapeDtypeStruct((GROUPS, 4 * UNIT, D), BF),
            jax.ShapeDtypeStruct((UNIT, D), F32),
        ],
        scratch_shapes=[pltpu.VMEM((clips, ROWS + 8, D), F32), pltpu.VMEM((256, D), BF)],
        compiler_params=params(2),
        cost_estimate=cost(24e9, clips * padded * 9000),
        name="stem_forward",
    )(order, ce, co, pos, mine, other)


def call_project(stream, w, vec):
    clips, padded, _ = stream.shape
    row = lambda width: pl.BlockSpec((1, ROWS, width), lambda c, i: (c, i, 0))
    return pl.pallas_call(
        project_kernel,
        grid=(clips, padded // ROWS),
        in_specs=[row(D), whole(w.shape), whole(vec.shape)],
        out_specs=row(3 * D),
        out_shape=jax.ShapeDtypeStruct((clips, padded, 3 * D), BF),
        compiler_params=params(2),
        cost_estimate=cost(10e9, clips * padded * 5000),
        name="projection_forward",
    )(stream, w, vec)


def call_attend(qkv, length):
    clips, padded, _ = qkv.shape
    query = pl.BlockSpec((1, ROWS, 128), lambda c, h, i: (c, i, h))
    whole_rows = lambda at: pl.BlockSpec((1, padded, 128), lambda c, h, i: (c, 0, at + h))
    return pl.pallas_call(
        functools.partial(attend_kernel, length),
        grid=(clips, PAIRS, padded // ROWS),
        in_specs=[whole_rows(0), whole_rows(PAIRS), whole_rows(2 * PAIRS)],
        out_specs=[
            pl.BlockSpec((1, 2, ROWS, padded), lambda c, h, i: (c, h, i, 0)),
            query,
            query,
            query,
        ],
        out_shape=[
            jax.ShapeDtypeStruct((clips, HEADS, padded, padded), BF),
            jax.ShapeDtypeStruct((clips, padded, D), BF),
            jax.ShapeDtypeStruct((clips, padded, D), BF),
            jax.ShapeDtypeStruct((clips, padded, D), F32),
        ],
        scratch_shapes=[
            pltpu.VMEM((2, 128, padded), BF),
            pltpu.VMEM((padded, 256), BF),
            pltpu.SMEM((1,), F32),
        ],
        compiler_params=params(3),
        cost_estimate=cost(50e9, clips * padded * padded * 16),
        name="attention_forward",
    )(qkv, qkv, qkv)


def call_attend_back(clip, weights, grad, attended, low_part, inverse, qkv, earlier, token):
    clips, padded, _ = qkv.shape
    query = pl.BlockSpec((1, ROWS, 128), lambda h, i: (clip, i, h))
    keys = lambda at: pl.BlockSpec((1, padded, 128), lambda h, i: (clip, 0, at + h))
    shape = jax.ShapeDtypeStruct((clips, padded, D), BF)
    aliases = {}
    extra = []
    extra_specs = []
    if earlier is not None:
        extra = list(earlier)
        extra_specs = [pl.BlockSpec(memory_space=pl.ANY)] * 3
        aliases = {8: 0, 9: 1, 10: 2}
    kernel, operands, specs = ordered(
        functools.partial(attend_back_kernel, 0 if earlier is None else 1),
        [weights, grad, attended, low_part, inverse, qkv, qkv, qkv] + extra,
        [
            pl.BlockSpec((1, 2, ROWS, padded), lambda h, i: (clip, h, i, 0)),
            query, query, query, query, query, keys(PAIRS), keys(2 * PAIRS),
        ] + extra_specs,
        token,
    )
    return pl.pallas_call(
        kernel,
        grid=(PAIRS, padded // ROWS),
        in_specs=specs,
        out_specs=[query, keys(0), keys(0)],
        out_shape=[shape] * 3,
        scratch_shapes=[pltpu.VMEM((128, padded), F32)] * 2
        + [pltpu.VMEM((2, 256, padded), BF), pltpu.VMEM((2, ROWS, padded), BF)],
        input_output_aliases=aliases,
        compiler_params=params(2),
        cost_estimate=cost(40e9, padded * padded * 16),
        name="attention_backward",
    )(*operands)


def call_mlp(live, attended, stream, cot, w, vec, up_bias):
    clips, padded, _ = attended.shape
    row = pl.BlockSpec((1, ROWS, D), lambda i, c: (c, i, 0))
    return pl.pallas_call(
        functools.partial(mlp_kernel, cot.shape[1]),
        grid=(padded // ROWS, clips),
        in_specs=[SMEM, row, row, row, whole(w.shape), whole(vec.shape), whole(up_bias.shape)],
        out_specs=[
            pl.BlockSpec((ROWS * clips, D), lambda i, c: (i, 0)), row, row,
            whole((GROUPS, 9 * UNIT, D)), whole((8, D)), whole((8, FF)),
        ],
        out_shape=[
            jax.ShapeDtypeStruct((cot.shape[1] * clips, D), BF),
            jax.ShapeDtypeStruct(attended.shape, BF),
            jax.ShapeDtypeStruct(attended.shape, BF),
            jax.ShapeDtypeStruct((GROUPS, 9 * UNIT, D), BF),
            jax.ShapeDtypeStruct((8, D), F32),
            jax.ShapeDtypeStruct((8, FF), F32),
        ],
        scratch_shapes=[
            pltpu.VMEM((D, D), F32),
            pltpu.VMEM((FF // D, D, D), F32),
            pltpu.VMEM((FF // D, D, D), F32),
            pltpu.VMEM((D, D), BF),
            pltpu.VMEM((FF, D), BF),
            pltpu.VMEM((FF // D, D, D), BF),
            pltpu.VMEM((D // 128, ROWS * clips, 128), F32),
            pltpu.VMEM((ROWS, FF), BF),
            pltpu.VMEM((ROWS, FF), BF),
        ],
        compiler_params=params(2),
        cost_estimate=cost(60e9, clips * padded * 8000),
        name="mlp_both_ways",
    )(live, attended, stream, cot, w, vec, up_bias)


def call_qkv_back(grads, stream, state_grad, d_two, w, vec, token):
    clips, padded, _ = stream.shape
    row = pl.BlockSpec((1, ROWS, D), lambda c, i: (c, i, 0))
    kernel, operands, specs = ordered(
        qkv_back_kernel,
        [*grads, stream, state_grad, d_two, w, vec],
        [row] * 6 + [whole(w.shape), whole(vec.shape)],
        token,
    )
    return pl.pallas_call(
        kernel,
        grid=(clips, padded // ROWS),
        in_specs=specs,
        out_specs=[row, whole((GROUPS, 3 * UNIT, D)), whole((8, D))],
        out_shape=[
            jax.ShapeDtypeStruct(stream.shape, BF),
            jax.ShapeDtypeStruct((GROUPS, 3 * UNIT, D), BF),
            jax.ShapeDtypeStruct((8, D), F32),
        ],
        scratch_shapes=[pltpu.VMEM((3, D, D), F32), pltpu.VMEM((3, D, D), BF)],
        compiler_params=params(2),
        cost_estimate=cost(18e9, clips * padded * 9000),
        name="projection_backward",
    )(*operands)


def call_stem_back(second_grad, a_even, a_odd, d_even, d_odd, ce, co, w, sums, token):
    clips, padded, _ = second_grad.shape
    last = padded // ROWS - 1
    row = lambda width: pl.BlockSpec((1, ROWS, width), lambda c, i: (c, last - i, 0))
    kernel, operands, specs = ordered(
        stem_back_kernel,
        [second_grad, a_even, a_odd, d_even, d_odd, ce, co, w, *sums],
        [row(D)] * 5 + [row(256)] * 2 + [whole(w.shape)] + [whole((8, D))] * 3,
        token,
    )
    return pl.pallas_call(
        kernel,
        grid=(clips, padded // ROWS),
        in_specs=specs,
        out_specs=[row(D), row(D), whole((GROUPS, 4 * UNIT, D))],
        out_shape=[
            jax.ShapeDtypeStruct(second_grad.shape, BF),
            jax.ShapeDtypeStruct(second_grad.shape, BF),
            jax.ShapeDtypeStruct((GROUPS, 4 * UNIT, D), BF),
        ],
        scratch_shapes=[
            pltpu.VMEM((3, D, D), F32),
            pltpu.VMEM((256, D), F32),
            pltpu.VMEM((ROWS + 8, D), F32),
            pltpu.VMEM((128, D), F32),
            pltpu.VMEM((3, D, D), BF),
        ],
        compiler_params=params(2),
        cost_estimate=cost(18e9, clips * padded * 9000),
        name="stem_backward",
    )(*operands)


def call_mel(spans, f_even, f_odd, w, frames, bins, token):
    clips, padded, _ = f_even.shape
    row = pl.BlockSpec((1, padded, D), lambda c: (c, 0, 0))
    kernel, operands, specs = ordered(
        functools.partial(mel_kernel, frames, bins),
        [spans, f_even, f_odd, w],
        [SMEM, row, row, whole(w.shape)],
        token,
    )
    return pl.pallas_call(
        kernel,
        grid=(clips,),
        in_specs=specs,
        out_specs=pl.BlockSpec((1, bins, frames), lambda c: (c, 0, 0)),
        out_shape=jax.ShapeDtypeStruct((clips, bins, frames), F32),
        scratch_shapes=[
            pltpu.VMEM((2 * D, D), BF),
            pltpu.VMEM((padded + 8, 128), F32),
            pltpu.VMEM((padded + 8, 128), F32),
            pltpu.VMEM((2 * padded, 128), F32),
        ],
        compiler_params=params(1),
        cost_estimate=cost(8e9, clips * padded * 4000),
        name="mel_backward",
    )(*operands)


def call_after(x, token):
    hold = pl.BlockSpec(memory_space=pl.ANY)

    def kernel(held, ready, passed):
        del held, ready, passed

    return pl.pallas_call(
        kernel,
        in_specs=[hold, pl.BlockSpec(token.shape, lambda: (0, 0))],
        out_specs=hold,
        out_shape=jax.ShapeDtypeStruct(x.shape, x.dtype),
        input_output_aliases={0: 0},
        name="after_stage",
    )(x, token)


def swap(x, mask, count):
    return lax.ppermute(x, "dp", [(i, i ^ mask) for i in range(count)])


def stages(count):
    bits = count.bit_length() - 1
    return [(0, 1)] + [(at, min(2, bits - at)) for at in range(1, bits, 2)]


def gather_xor(x, count, index, filler):
    held = x[None]
    where = jnp.zeros((count,), jnp.int32)
    apart = jnp.arange(count, dtype=jnp.int32) ^ index
    token = None
    parts = None
    for first, many in reversed(stages(count)):
        if parts is not None:
            if first == 0:
                parts[-1] = parts[-1] + filler
            held = jnp.concatenate(parts)
        where = where + ((apart >> first) & ((1 << many) - 1)) * held.shape[0]
        parts = [held] + [swap(held, rel << first, count) for rel in range(1, 1 << many)]
        if first > 0:
            token = parts[-1]
    return parts, where, token


class Scatter:
    def __init__(self, x, count, index):
        self.held, self.count, self.index = x, count, index
        self.plan = stages(count)

    def step(self):
        if not self.plan:
            return None
        first, many = self.plan.pop(0)
        radix = 1 << many
        held = self.held
        split = held.reshape((held.shape[0] // radix, radix) + held.shape[1:])
        mine = (self.index >> first) & (radix - 1)
        take = lambda at: lax.dynamic_index_in_dim(split, at, 1, keepdims=False)
        got = [swap(take(mine ^ rel), rel << first, self.count) for rel in range(1, radix)]
        total = take(mine).astype(F32)
        for piece in got:
            total = total + piece.astype(F32)
        self.held = total.astype(BF) if self.plan else total
        return total[0, :1, :128]

    def join(self, other):
        self.held = jnp.concatenate([self.held, other.held], axis=1)

    def owned(self):
        while self.plan:
            self.step()
        return self.held[0]


def rows_of(gathered, first, parts, unit):
    taken = gathered[:, first * unit : (first + parts) * unit]
    return taken.reshape(GROUPS, parts * UNIT, gathered.shape[2])


def to_groups(gathered, pieces, unit):
    if unit == UNIT:
        return gathered
    out = []
    at = 0
    for parts in pieces:
        out.append(rows_of(gathered, at, parts, unit))
        at += parts
    return jnp.concatenate(out, axis=1)


def from_groups(packed, pieces, count):
    unit = D // count
    if unit == UNIT:
        return packed
    out = []
    at = 0
    for parts in pieces:
        piece = packed[:, at * UNIT : (at + parts) * UNIT]
        out.append(piece.reshape(count, parts * unit, D))
        at += parts
    return jnp.concatenate(out, axis=1)


def position_table(frames):
    half = D // 2
    rate = np.exp(-(math.log(10000.0) / (half - 1)) * np.arange(half, dtype=np.float64))
    angle = np.arange(frames, dtype=np.float64)[:, None] * rate[None, :]
    return np.concatenate([np.sin(angle), np.cos(angle)], axis=1).astype(np.float32)


def per_device(
    count, log_mels, mask_spans, live_slots, first_conv, second_conv, biases, norm_gains,
    qkv_weight, out_weight, up_weight, up_bias, down_weight, cotangent,
):
    clips, frames, bins = log_mels.shape
    length = frames // 2
    padded = -(-length // ROWS) * ROWS
    index = lax.axis_index("dp")
    unit = D // count
    tap_lanes = 3 * bins
    ups = FF // D

    small = jnp.concatenate(
        [
            first_conv.reshape(tap_lanes, unit).T,
            biases.T,
            norm_gains.T,
            up_bias.reshape(unit, ups),
            jnp.zeros((unit, D - tap_lanes - 10 - ups), BF),
        ],
        axis=1,
    )
    near = jnp.concatenate([small, second_conv.reshape(3 * unit, D)])
    col_even, col_odd = call_prepare(mask_spans, log_mels.transpose(0, 2, 1), padded)
    parts, order, token = gather_xor(near, count, index, col_even[0, padded - 1, 255])
    if unit != UNIT:
        near = jnp.take(jnp.concatenate(parts), order, axis=0)
        near = to_groups(near, (1,) * 4, unit)
        parts = (near[: GROUPS // 2], near[GROUPS // 2 :])
        order = jnp.arange(GROUPS, dtype=jnp.int32)
    qkv_w = qkv_weight.transpose(1, 0, 2).reshape(3 * unit, D)
    qkv_w = to_groups(lax.all_gather(qkv_w, "dp", axis=0, tiled=False), (1,) * 3, unit)
    far = jnp.concatenate(
        [
            out_weight,
            up_weight.reshape(unit, ups, D).transpose(1, 0, 2).reshape(ups * unit, D),
            down_weight,
        ]
    )
    far = far + token[0, 0, D - 1]
    far = lax.all_gather(far, "dp", axis=0, tiled=False)
    far = to_groups(far, (1,) * (1 + ups) + (ups,), unit)

    table = jnp.asarray(position_table(padded))
    a_even, a_odd, d_even, d_odd, d_two, stream, near, vec = call_stem(
        order, col_even, col_odd, table, *parts
    )
    qkv = call_project(stream, qkv_w, vec)
    up_row = jnp.pad(vec[10 : 10 + ups].T.reshape(1, FF), ((0, 7), (0, 0)))
    weights, attended, low_part, inverse = call_attend(qkv, length)
    encoded, att_grad, state_grad, mlp_packed, mlp_sums, up_sums = call_mlp(
        live_slots, attended, stream, cotangent, far, vec, up_row
    )
    mlp_packed = from_groups(mlp_packed, (1,) * (1 + ups) + (ups,), count)
    mlp_sum = Scatter(mlp_packed, count, index)
    up_cols = jnp.pad(up_sums[0].reshape(D, ups).T, ((0, 8 - ups), (0, 0)))
    grads = None
    for clip in range(clips):
        token = mlp_sum.step() if clip else None
        grads = call_attend_back(
            clip, weights, att_grad, attended, low_part, inverse, qkv, grads, token
        )
    second_grad, qkv_packed, qkv_sums = call_qkv_back(
        grads, stream, state_grad, d_two, qkv_w, vec, mlp_sum.step()
    )
    qkv_sum = Scatter(from_groups(qkv_packed, (1,) * 3, count), count, index)
    f_even, f_odd, stem_packed = call_stem_back(
        second_grad, a_even, a_odd, d_even, d_odd, col_even, col_odd, near,
        (qkv_sums, mlp_sums, up_cols), mlp_sum.step(),
    )
    stem_sum = Scatter(from_groups(stem_packed, (1,) * 4, count), count, index)
    mel_turned = call_mel(mask_spans, f_even, f_odd, near, frames, bins, qkv_sum.step())
    mel_grad = mel_turned.transpose(0, 2, 1)
    encoded = call_after(encoded, stem_sum.step())
    encoded = encoded.reshape(length, clips, D).transpose(1, 0, 2)
    qkv_sum.step()
    stem_sum.step()
    if stem_sum.plan:
        stem_sum.join(qkv_sum)
        owned = stem_sum.owned()
    else:
        owned = jnp.concatenate([stem_sum.owned(), qkv_sum.owned()])
    mlp_owned, stem_owned, qkv_owned = mlp_sum.owned(), owned[: 4 * unit], owned[4 * unit :]

    mixed = stem_owned[:unit]
    bias_grad = mixed[:, tap_lanes : tap_lanes + 8].T
    return (
        encoded,
        mel_grad,
        mixed[:, :tap_lanes].T.reshape(3, bins, unit),
        stem_owned[unit : 4 * unit].reshape(3, unit, D),
        bias_grad,
        mixed[:, tap_lanes + 8 : tap_lanes + 10].T,
        qkv_owned.reshape(3, unit, D).transpose(1, 0, 2),
        mlp_owned[:unit],
        mlp_owned[unit : (1 + ups) * unit]
        .reshape(ups, unit, D)
        .transpose(1, 0, 2)
        .reshape(unit, FF),
        mixed[:, tap_lanes + 10 : tap_lanes + 10 + ups].reshape(ups * unit),
        mlp_owned[(1 + ups) * unit :],
        bias_grad[6],
    )


def solution(mesh):
    return jax.shard_map(
        functools.partial(per_device, mesh.shape["dp"]),
        mesh=mesh,
        in_specs=(
            P("dp", None, None),
            P("dp", None),
            P("dp"),
            P(None, None, "dp"),
            P(None, "dp", None),
            P(None, "dp"),
            P(None, "dp"),
            P("dp", None, None),
            P("dp", None),
            P("dp", None),
            P("dp"),
            P("dp", None),
            P("dp", None, None),
        ),
        out_specs=(
            P("dp", None, None),
            P("dp", None, None),
            P(None, None, "dp"),
            P(None, "dp", None),
            P(None, "dp"),
            P(None, "dp"),
            P("dp", None, None),
            P("dp", None),
            P("dp", None),
            P("dp"),
            P("dp", None),
            P("dp"),
        ),
        check_vma=False,
    )
```

```python
import functools
import math

import jax
import jax.numpy as jnp
import numpy as np
from jax import lax
from jax.experimental import pallas as pl
from jax.experimental.pallas import tpu as pltpu
from jax.sharding import PartitionSpec as P

D = 512
FF = 2048
HEADS = 8
HEAD_DIM = 64
PAIRS = HEADS // 2
ROWS = 768
CHUNK = 256
UNIT = 16
GROUPS = D // UNIT
LN_EPS = 1e-05
SCORE_SCALE = HEAD_DIM ** (-0.5)
LOG2E = math.log2(math.e)
VMEM = 60 * 1024 * 1024
BF = jnp.bfloat16
F32 = jnp.float32


def nn(left, right):
    return lax.dot_general(left, right, (((1,), (0,)), ((), ())), preferred_element_type=F32)


def tn(left, right):
    return lax.dot_general(left, right, (((0,), (0,)), ((), ())), preferred_element_type=F32)


def gelu_both(v):
    phi = 0.5 * lax.erf(v * math.sqrt(0.5)) + 0.5
    bell = jnp.exp2(v * v * (-0.5 * LOG2E))
    return v * phi, phi + v * bell * (1.0 / math.sqrt(2.0 * math.pi))


def staggered(count, *works):
    depth = len(works)
    for at in range(count + depth - 1):
        for lag, work in enumerate(works):
            if 0 <= at - lag < count:
                work(at - lag)


def row_stats(x):
    mean = jnp.mean(x, axis=-1, keepdims=True)
    centred = x - mean
    var = jnp.mean(centred * centred, axis=-1, keepdims=True)
    rate = lax.rsqrt(var + LN_EPS)
    return centred * rate, rate


def norm_back(hat, rate, gain, upstream):
    scaled = upstream * gain
    first = jnp.mean(scaled, axis=-1, keepdims=True)
    second = jnp.mean(scaled * hat, axis=-1, keepdims=True)
    return rate * (scaled - first - hat * second)


def col_sum(x):
    return jnp.sum(x, axis=0, keepdims=True)


def unit_rows(ref, start, count=UNIT):
    block = ref[:, start : start + count, :]
    return block.reshape(GROUPS * count, block.shape[2])


def prepare_kernel(frames, bins, spans, mels, ce, co, flat, tall):
    clip = pl.program_id(0)
    padded = ce.shape[1]
    place = lax.broadcasted_iota(jnp.int32, (bins, frames), 1)
    bin_at = lax.broadcasted_iota(jnp.int32, (bins, frames), 0)
    time_keep = (place < spans[clip, 0]) | (place >= spans[clip, 0] + spans[clip, 1])
    freq_keep = (bin_at < spans[clip, 2]) | (bin_at >= spans[clip, 2] + spans[clip, 3])

    @pl.when(clip == 0)
    def _():
        flat[...] = jnp.zeros_like(flat)
        tall[0:8, :] = jnp.zeros((8, 128), F32)
        tall[8 + 2 * padded :, :] = jnp.zeros((8, 128), F32)

    flat[0:bins, 0:frames] = jnp.where(time_keep & freq_keep, mels[0].astype(F32), 0.0)
    tall[8 : 8 + 2 * padded, :] = flat[...].T
    before, even, odd, after = (tall[pl.ds(7 + k, padded, stride=2), :] for k in range(4))
    lane = lax.broadcasted_iota(jnp.int32, (padded, 128), 1)
    wrap = 2 * bins - 128
    one = jnp.where(lane == wrap + bins, 1.0, 0.0)
    for out, taps in ((ce, (before, even, odd)), (co, (even, odd, after))):
        middle = pltpu.roll(taps[1], bins, 1)
        out[0, :, 0:128] = (taps[0] + jnp.where(lane >= bins, middle, 0.0)).astype(BF)
        last = pltpu.roll(taps[2], wrap, 1)
        out[0, :, 128:256] = (jnp.where(lane < wrap, middle, 0.0) + last + one).astype(BF)


def stem_kernel(
    order, ce, co, pos, mine, other, a_even, a_odd, d_even, d_odd, d_two, stream, w, vec, buf, first_t
):
    step = pl.program_id(0)
    clip = pl.program_id(1)
    rows = ce.shape[1]
    half = GROUPS // 2

    @pl.when((clip == 0) & (step == 0))
    def _():
        for group in range(GROUPS):
            source = order[group]

            @pl.when(source < half)
            def _():
                w[group] = mine[source]

            @pl.when(source >= half)
            def _():
                w[group] = other[source - half]

        turned = unit_rows(w, 0)[:, 0:256].astype(F32).T
        vec[...] = turned[240:256, :]
        first_t[...] = turned.astype(BF)

    even, even_slope = gelu_both(nn(ce[0], first_t[...]))
    odd, odd_slope = gelu_both(nn(co[0], first_t[...]))
    even = even.astype(BF)
    a_even[0] = even
    d_even[0] = even_slope.astype(BF)
    d_odd[0] = odd_slope.astype(BF)
    odd_low = odd.astype(BF)
    a_odd[0] = odd_low

    @pl.when(step == 0)
    def _():
        buf[clip, 0:8, :] = jnp.zeros((8, D), F32)

    @pl.when(step > 0)
    def _():
        buf[clip, 0:8, :] = buf[clip, rows : rows + 8, :]

    buf[clip, 8 : 8 + rows, :] = odd
    before = buf[clip, 7 : 7 + rows, :].astype(BF)
    second = nn(before, unit_rows(w, UNIT))
    second = second + nn(even, unit_rows(w, 2 * UNIT))
    second = second + nn(odd_low, unit_rows(w, 3 * UNIT)) + vec[1:2, :]
    wave, slope = gelu_both(second)
    d_two[0] = slope.astype(BF)
    stream[0] = wave + pos[...]


def project_kernel(stream, w, vec, qkv):
    hat, _ = row_stats(stream[0])
    normed = (hat * vec[8:9, :] + vec[2:3, :]).astype(BF)
    queries = nn(normed, unit_rows(w, 0)) + vec[3:4, :]
    qkv[0, :, 0:D] = queries.astype(BF)
    qkv[0, :, D : 2 * D] = nn(normed, unit_rows(w, UNIT)).astype(BF)
    qkv[0, :, 2 * D :] = (nn(normed, unit_rows(w, 2 * UNIT)) + vec[4:5, :]).astype(BF)


def head_mask(shape, head):
    lane = lax.broadcasted_iota(jnp.int32, shape, 1)
    return (lane >= head * HEAD_DIM) & (lane < (head + 1) * HEAD_DIM)


def row_mask(shape, head):
    row = lax.broadcasted_iota(jnp.int32, shape, 0)
    return (row >= head * HEAD_DIM) & (row < (head + 1) * HEAD_DIM)


def attend_kernel(
    length, q_ref, k_ref, v_ref, weights, attended, low_part, inverse, keys_t, wide, reach
):
    step = pl.program_id(2)
    rows = attended.shape[1]
    padded = k_ref.shape[1]
    edge = length // 128 * 128

    def longest(x):
        return jnp.max(jnp.sum(jnp.square(x.astype(F32)), axis=1))

    @pl.when(step == 0)
    def _():
        turned = k_ref[0].T
        for head in range(2):
            own = turned[head * HEAD_DIM : (head + 1) * HEAD_DIM, :]
            keys_t[head, 0:HEAD_DIM, :] = own
            keys_t[head, HEAD_DIM : 2 * HEAD_DIM, :] = own
        wide[:, 0 : 2 * HEAD_DIM] = v_ref[0]
        wide[:, 2 * HEAD_DIM :] = jnp.ones((padded, 2 * HEAD_DIM), BF)
        reach[0] = longest(q_ref[0]) * longest(k_ref[0])

    factor = SCORE_SCALE * LOG2E
    calm = reach[0] < (60.0 / factor) ** 2
    scaled = q_ref[0, pl.ds(pl.multiple_of(step * rows, rows), rows), :].astype(F32) * factor
    large = scaled.astype(BF)
    small = pltpu.roll(scaled - large.astype(F32), HEAD_DIM, 1).astype(BF)
    first = head_mask(large.shape, 0)
    queries = (jnp.where(first, large, small), jnp.where(first, small, large))

    def attend(shift):
        parts = [(at, head) for at in range(0, rows, CHUNK) for head in range(2)]
        scores, soft, mixed = {}, {}, {}

        def score(i):
            at, head = parts[i]
            scores[i] = nn(queries[head][at : at + CHUNK], keys_t[head])

        def soften(i):
            at, head = parts[i]
            values = scores.pop(i)
            body, rest = values[:, :edge], values[:, edge:]
            place = lax.broadcasted_iota(jnp.int32, rest.shape, 1) + edge
            rest = jnp.where(place < length, rest, -1e30)
            if shift:
                top = jnp.maximum(
                    jnp.max(body, axis=1, keepdims=True), jnp.max(rest, axis=1, keepdims=True)
                )
                body, rest = body - top, rest - top
            body, rest = jnp.exp2(body).astype(BF), jnp.exp2(rest).astype(BF)
            soft[i] = jnp.concatenate([body, rest], axis=1)
            weights[0, head, at : at + CHUNK, :] = soft[i]

        def mix(i):
            at, head = parts[i]
            mixed[head] = nn(soft.pop(i), wide[...])
            if head == 0:
                return
            rates = [1.0 / mixed[k][:, 2 * HEAD_DIM :] for k in range(2)]
            outs = [mixed[k][:, : 2 * HEAD_DIM] * rates[k] for k in range(2)]
            pick = head_mask(outs[0].shape, 0)
            both = jnp.where(pick, outs[0], outs[1])
            high = both.astype(BF)
            attended[0, at : at + CHUNK, :] = high
            low_part[0, at : at + CHUNK, :] = (both - high.astype(F32)).astype(BF)
            inverse[0, at : at + CHUNK, :] = jnp.where(pick, rates[0], rates[1])

        staggered(len(parts), score, soften, mix)

    @pl.when(calm)
    def _():
        attend(False)

    @pl.when(jnp.logical_not(calm))
    def _():
        attend(True)


def attend_back_kernel(
    aliased, weights, grad_ref, att_ref, low_ref, inv_ref, q_ref, k_ref, v_ref, *rest
):
    rest = rest[3 * aliased :]
    dq, dk, dv, dk_sum, dv_sum, right, score_grad = rest
    step = pl.program_id(1)
    scaled_low = (grad_ref[0].astype(F32) * inv_ref[0]).astype(BF)
    prod = scaled_low.astype(F32) * (att_ref[0].astype(F32) + low_ref[0].astype(F32))
    lane = lax.broadcasted_iota(jnp.int32, prod.shape, 1)
    dots = jnp.zeros(prod.shape, F32)
    for head in range(2):
        dot = -jnp.sum(jnp.where(head_mask(prod.shape, head), prod, 0.0), axis=1, keepdims=True)
        high = dot.astype(BF).astype(F32)
        dots = jnp.where(lane == 2 * head, high, dots)
        dots = jnp.where(lane == 2 * head + 1, dot - high, dots)
    left = jnp.concatenate([scaled_low, dots.astype(BF)], axis=1)
    q_turn = q_ref[0].T
    g_turn = scaled_low.T

    @pl.when(step == 0)
    def _():
        dk_sum[...] = jnp.zeros_like(dk_sum)
        dv_sum[...] = jnp.zeros_like(dv_sum)
        turned = v_ref[0].T
        zero = jnp.zeros_like(turned)
        row = lax.broadcasted_iota(jnp.int32, turned.shape, 0)
        for head in range(2):
            right[head, 0:128, :] = jnp.where(row_mask(turned.shape, head), turned, zero)
            right[head, 128:256, :] = jnp.where(
                (row == 2 * head) | (row == 2 * head + 1), zero + 1, zero
            )

    rows = scaled_low.shape[0]
    parts = [(at, head) for at in range(0, rows, CHUNK) for head in range(2)]
    grads, outs = {}, {}

    def weight_grad(i):
        at, head = parts[i]
        grads[i] = nn(left[at : at + CHUNK], right[head])

    def multiply(i):
        at, head = parts[i]
        soft = weights[0, head, at : at + CHUNK, :].astype(F32)
        score_grad[head, at : at + CHUNK, :] = (soft * grads.pop(i)).astype(BF)

    def query_grad(i):
        at, head = parts[i]
        outs[head] = nn(score_grad[head, at : at + CHUNK, :], k_ref[0])
        if head == 1:
            pick = head_mask(outs[0].shape, 0)
            total = jnp.where(pick, outs[0], outs[1]) * SCORE_SCALE
            dq[0, at : at + CHUNK, :] = total.astype(BF)

    staggered(len(parts), weight_grad, multiply, query_grad)
    for head in range(2):
        span = slice(head * HEAD_DIM, (head + 1) * HEAD_DIM)
        dv_sum[span, :] += nn(g_turn[span, :], weights[0, head])
        dk_sum[span, :] += nn(q_turn[span, :], score_grad[head])

    @pl.when(step == pl.num_programs(1) - 1)
    def _():
        dk[0] = (dk_sum[...].T * SCORE_SCALE).astype(BF)
        dv[0] = dv_sum[...].T.astype(BF)


def mlp_kernel(
    length, live, att, stream, cot, w, vec, up_bias,
    encoded, att_grad, state_grad, packed, sums, up_sums,
    out_acc, up_acc, down_acc, out_t, up_t, down_t, mixed, gated, hidden_grad,
):
    step = pl.program_id(0)
    clip = pl.program_id(1)
    clips = pl.num_programs(1)
    rows = cot.shape[1]
    alive = clip < live[0]

    @pl.when((clip == 0) & (step == 0))
    def _():
        out_acc[...] = jnp.zeros_like(out_acc)
        up_acc[...] = jnp.zeros_like(up_acc)
        down_acc[...] = jnp.zeros_like(down_acc)
        sums[...] = jnp.zeros_like(sums)
        up_sums[...] = jnp.zeros_like(up_sums)
        out_t[...] = unit_rows(w, 0).T
        for part in range(FF // D):
            up_t[part * D : (part + 1) * D, :] = unit_rows(w, (1 + part) * UNIT).T
            down_t[part] = unit_rows(w, 5 * UNIT, 4 * UNIT)[part * D : (part + 1) * D, :].T

    place = lax.broadcasted_iota(jnp.int32, (rows, D), 0) + step * rows
    reach = jnp.where(alive, length, 0)
    cot_float = jnp.where(place < reach, cot[0].astype(F32), 0.0)
    cot_low = cot_float.astype(BF)
    attended = att[0]
    out_w = unit_rows(w, 0)
    after = stream[0] + nn(attended, out_w) + vec[5:6, :]
    hat, rate = row_stats(after)
    normed = (hat * vec[9:10, :] + vec[6:7, :]).astype(BF)
    normed_turn = normed.T
    cot_turn = cot_low.T
    spans = [slice(part * D, (part + 1) * D) for part in range(FF // D)]
    ahead = {}
    sides = [after + vec[7:8, :], None]

    def enter(part):
        ahead[part] = (
            nn(normed, unit_rows(w, (1 + part) * UNIT)) + up_bias[0:1, spans[part]],
            nn(cot_low, down_t[part]),
        )

    def activate(part):
        hidden, grad = ahead.pop(part)
        wave, slope = gelu_both(hidden)
        gated[:, spans[part]] = wave.astype(BF)
        grad = grad * slope
        up_sums[0:1, spans[part]] += col_sum(grad)
        hidden_grad[:, spans[part]] = grad.astype(BF)

    def leave(part):
        wave, grad = gated[:, spans[part]], hidden_grad[:, spans[part]]
        down_w = unit_rows(w, 5 * UNIT, 4 * UNIT)[spans[part], :]
        back = nn(grad, up_t[spans[part], :])
        sides[0] = sides[0] + nn(wave, down_w)
        sides[1] = back if sides[1] is None else sides[1] + back
        up_acc[part] += nn(normed_turn, grad)
        down_acc[part] += nn(cot_turn, wave)

    staggered(FF // D, enter, activate, leave)
    result, normed_grad = sides
    result = jnp.where(alive, result, 0.0)
    slots = mixed.shape[1] // rows
    for slot in range(slots):

        @pl.when(clip == slot)
        def _():
            for part in range(D // 128):
                lanes = slice(part * 128, (part + 1) * 128)
                mixed[part, pl.ds(slot, rows, stride=slots), :] = result[:, lanes]

    @pl.when(clip == clips - 1)
    def _():
        for part in range(D // 128):
            encoded[:, part * 128 : (part + 1) * 128] = mixed[part].astype(BF)

    total = cot_float + norm_back(hat, rate, vec[9:10, :], normed_grad)
    low = total.astype(BF)
    state_grad[0] = low
    sums[0:1, :] += col_sum(total)
    sums[1:2, :] += col_sum(normed_grad)
    sums[2:3, :] += col_sum(cot_float)
    sums[3:4, :] += col_sum(normed_grad * hat)
    att_grad[0] = nn(low, out_t[...]).astype(BF)
    out_acc[...] += tn(attended, low)

    @pl.when((clip == clips - 1) & (step == pl.num_programs(0) - 1))
    def _():
        packed[:, 0:UNIT, :] = out_acc[...].astype(BF).reshape(GROUPS, UNIT, D)
        for part in range(FF // D):
            at = (1 + part) * UNIT
            packed[:, at : at + UNIT, :] = up_acc[part].astype(BF).reshape(GROUPS, UNIT, D)
            owners = GROUPS // (FF // D)
            packed[part * owners : (part + 1) * owners, 5 * UNIT : 9 * UNIT, :] = (
                down_acc[part].T.astype(BF).reshape(owners, 4 * UNIT, D)
            )


def qkv_back_kernel(
    dq, dk, dv, stream, state_grad, d_two, w, vec, second_grad, packed, sums, acc, turned
):
    clip = pl.program_id(0)
    step = pl.program_id(1)

    @pl.when((clip == 0) & (step == 0))
    def _():
        acc[...] = jnp.zeros_like(acc)
        sums[...] = jnp.zeros_like(sums)
        for part in range(3):
            turned[part] = unit_rows(w, part * UNIT).T

    parts = (dq, dk, dv)
    rows = stream.shape[1]
    hat, rate = row_stats(stream[0])
    normed_turn = (hat * vec[8:9, :] + vec[2:3, :]).astype(BF).T
    ahead = {}

    def enter(i):
        at = slice(i * CHUNK, (i + 1) * CHUNK)
        total = nn(parts[0][0, at, :], turned[0])
        for part in range(1, 3):
            total = total + nn(parts[part][0, at, :], turned[part])
        ahead[i] = total

    def leave(i):
        at = slice(i * CHUNK, (i + 1) * CHUNK)
        normed_grad = ahead.pop(i)
        total = norm_back(hat[at], rate[at], vec[8:9, :], normed_grad)
        total = total + state_grad[0, at, :].astype(F32)
        grad = total * d_two[0, at, :].astype(F32)
        second_grad[0, at, :] = grad.astype(BF)
        sums[0:1, :] += col_sum(grad)
        sums[1:2, :] += col_sum(normed_grad)
        sums[2:3, :] += col_sum(dq[0, at, :].astype(F32))
        sums[3:4, :] += col_sum(dv[0, at, :].astype(F32))
        sums[4:5, :] += col_sum(normed_grad * hat[at])

    def gather(i):
        for part in range(i, 3, rows // CHUNK):
            acc[part] += nn(normed_turn, parts[part][0])

    staggered(rows // CHUNK, enter, gather, leave)

    @pl.when((clip == pl.num_programs(0) - 1) & (step == pl.num_programs(1) - 1))
    def _():
        for part in range(3):
            packed[:, part * UNIT : (part + 1) * UNIT, :] = (
                acc[part].astype(BF).reshape(GROUPS, UNIT, D)
            )


def stem_back_kernel(
    grad_ref, a_even, a_odd, d_even, d_odd, ce, co, w, qkv_sums, mlp_sums, up_cols, qkv_packed,
    f_even, f_odd, packed, acc, w_acc, buf, extra, turned,
):
    clip = pl.program_id(0)
    step = pl.program_id(1)
    rows = grad_ref.shape[1]

    @pl.when((clip == 0) & (step == 0))
    def _():
        acc[...] = jnp.zeros_like(acc)
        w_acc[...] = jnp.zeros_like(w_acc)
        for part in range(3):
            turned[part] = unit_rows(w, (1 + part) * UNIT).T

    @pl.when(step == 0)
    def _():
        buf[rows : rows + 8, :] = jnp.zeros((8, D), F32)

    @pl.when(step > 0)
    def _():
        buf[rows : rows + 8, :] = buf[0:8, :]

    grad = grad_ref[0]
    buf[0:rows, :] = grad.astype(F32)
    after = buf[1 : rows + 1, :].astype(BF)
    even_grad = nn(grad, turned[1])
    odd_grad = nn(grad, turned[2]) + nn(after, turned[0])
    even_grad = (even_grad * d_even[0].astype(F32)).astype(BF)
    odd_grad = (odd_grad * d_odd[0].astype(F32)).astype(BF)
    f_even[0] = even_grad
    f_odd[0] = odd_grad
    odd_turn = a_odd[0].T
    acc[0] += nn(odd_turn, after)
    acc[1] += nn(a_even[0].T, grad)
    acc[2] += nn(odd_turn, grad)
    w_acc[...] += tn(ce[0], even_grad) + tn(co[0], odd_grad)

    @pl.when((clip == pl.num_programs(0) - 1) & (step == pl.num_programs(1) - 1))
    def _():
        for part in range(3):
            at = (1 + part) * UNIT
            packed[:, at : at + UNIT, :] = acc[part].astype(BF).reshape(GROUPS, UNIT, D)
        packed[:, 4 * UNIT : 7 * UNIT, :] = qkv_packed[...]
        extra[...] = jnp.zeros_like(extra)
        extra[113:117, :] = qkv_sums[0:4, :]
        extra[117:120, :] = mlp_sums[0:3, :]
        extra[120:121, :] = qkv_sums[4:5, :]
        extra[121:122, :] = mlp_sums[3:4, :]
        extra[122:126, :] = up_cols[0:4, :]
        w_acc[128:256, :] += extra[...]
        small = jnp.concatenate([w_acc[...].T, jnp.zeros((D, D - 256), F32)], axis=1)
        packed[:, 0:UNIT, :] = small.astype(BF).reshape(GROUPS, UNIT, D)


def mel_kernel(frames, bins, spans, f_even, f_odd, w, out, mel_w, down_buf, up_buf, tall):
    clip = pl.program_id(0)
    rows = f_even.shape[1]

    @pl.when(clip == 0)
    def _():
        first_w = unit_rows(w, 0)[:, 0:256].astype(F32)
        lane = lax.broadcasted_iota(jnp.int32, (D, 128), 1)
        low, high = first_w[:, 0:128], first_w[:, 128:256]
        wrap = 2 * bins - 128
        keep = lane < bins
        zero = jnp.zeros((D, 128), BF)
        taps = (
            jnp.where(keep, low, 0.0).astype(BF),
            jnp.where(
                keep,
                jnp.where(lane < 128 - bins, pltpu.roll(low, 128 - bins, 1), pltpu.roll(high, 128 - bins, 1)),
                0.0,
            ).astype(BF),
            jnp.where(keep, pltpu.roll(high, 128 - wrap, 1), 0.0).astype(BF),
        )
        for at, tap in enumerate((taps[1], taps[2], zero, taps[0])):
            mel_w[0:D, at * 128 : (at + 1) * 128] = tap
        for at, tap in enumerate((taps[0], taps[1], taps[2], zero)):
            mel_w[D : 2 * D, at * 128 : (at + 1) * 128] = tap

    full = nn(f_even[0], mel_w[0:D, :]) + nn(f_odd[0], mel_w[D : 2 * D, :])
    down_buf[0:8, :] = jnp.zeros((8, 128), F32)
    down_buf[8 : 8 + rows, :] = full[:, 256:384]
    up_buf[0:rows, :] = full[:, 384:512]
    up_buf[rows : rows + 8, :] = jnp.zeros((8, 128), F32)
    tall[pl.ds(0, rows, stride=2), :] = full[:, 0:128] + down_buf[7 : 7 + rows, :]
    tall[pl.ds(1, rows, stride=2), :] = full[:, 128:256] + up_buf[1 : rows + 1, :]
    turned = tall[...].T[0:bins, 0:frames]
    place = lax.broadcasted_iota(jnp.int32, (bins, frames), 1)
    bin_at = lax.broadcasted_iota(jnp.int32, (bins, frames), 0)
    time_keep = (place < spans[clip, 0]) | (place >= spans[clip, 0] + spans[clip, 1])
    freq_keep = (bin_at < spans[clip, 2]) | (bin_at >= spans[clip, 2] + spans[clip, 3])
    out[0] = jnp.where(time_keep & freq_keep, turned, 0.0)


def whole(shape):
    return pl.BlockSpec(shape, lambda *_: (0,) * len(shape), pipeline_mode=pl.Buffered(1))


def params(semantics):
    return pltpu.CompilerParams(
        vmem_limit_bytes=VMEM, dimension_semantics=("arbitrary",) * semantics
    )


def cost(flops, moved):
    return pl.CostEstimate(flops=int(flops), bytes_accessed=int(moved), transcendentals=0)


SMEM = pl.BlockSpec(memory_space=pltpu.SMEM)


def ordered(kernel, operands, specs, token):
    if token is None:
        return kernel, operands, specs
    place = len(specs)

    def inner(*refs):
        kernel(*refs[:place], *refs[place + 1 :])

    return inner, list(operands) + [token], list(specs) + [whole(token.shape)]


def call_prepare(spans, mels, padded):
    clips, bins, frames = mels.shape
    row = pl.BlockSpec((1, padded, 256), lambda c: (c, 0, 0))
    return pl.pallas_call(
        functools.partial(prepare_kernel, frames, bins),
        grid=(clips,),
        in_specs=[SMEM, pl.BlockSpec((1, bins, frames), lambda c: (c, 0, 0))],
        out_specs=[row, row],
        out_shape=[jax.ShapeDtypeStruct((clips, padded, 256), BF)] * 2,
        scratch_shapes=[
            pltpu.VMEM((128, 2 * padded), F32),
            pltpu.VMEM((2 * padded + 16, 128), F32),
        ],
        compiler_params=params(1),
        cost_estimate=cost(8e9, clips * padded * 2048),
        name="mel_prepare",
    )(spans, mels)


def call_stem(order, ce, co, pos, mine, other):
    clips, padded, _ = ce.shape
    row = lambda width: pl.BlockSpec((1, ROWS, width), lambda i, c: (c, i, 0))
    out = lambda width, kind: jax.ShapeDtypeStruct((clips, padded, width), kind)
    return pl.pallas_call(
        stem_kernel,
        grid=(padded // ROWS, clips),
        in_specs=[
            SMEM, row(256), row(256), pl.BlockSpec((ROWS, D), lambda i, c: (i, 0)),
            whole(mine.shape), whole(other.shape),
        ],
        out_specs=[row(D)] * 6 + [whole((GROUPS, 4 * UNIT, D)), whole((UNIT, D))],
        out_shape=[out(D, BF)] * 5 + [
            out(D, F32),
            jax.ShapeDtypeStruct((GROUPS, 4 * UNIT, D), BF),
            jax.ShapeDtypeStruct((UNIT, D), F32),
        ],
        scratch_shapes=[pltpu.VMEM((clips, ROWS + 8, D), F32), pltpu.VMEM((256, D), BF)],
        compiler_params=params(2),
        cost_estimate=cost(24e9, clips * padded * 9000),
        name="stem_forward",
    )(order, ce, co, pos, mine, other)


def call_project(stream, w, vec):
    clips, padded, _ = stream.shape
    row = lambda width: pl.BlockSpec((1, ROWS, width), lambda c, i: (c, i, 0))
    return pl.pallas_call(
        project_kernel,
        grid=(clips, padded // ROWS),
        in_specs=[row(D), whole(w.shape), whole(vec.shape)],
        out_specs=row(3 * D),
        out_shape=jax.ShapeDtypeStruct((clips, padded, 3 * D), BF),
        compiler_params=params(2),
        cost_estimate=cost(10e9, clips * padded * 5000),
        name="projection_forward",
    )(stream, w, vec)


def call_attend(qkv, length):
    clips, padded, _ = qkv.shape
    query = pl.BlockSpec((1, ROWS, 128), lambda c, h, i: (c, i, h))
    whole_rows = lambda at: pl.BlockSpec((1, padded, 128), lambda c, h, i: (c, 0, at + h))
    return pl.pallas_call(
        functools.partial(attend_kernel, length),
        grid=(clips, PAIRS, padded // ROWS),
        in_specs=[whole_rows(0), whole_rows(PAIRS), whole_rows(2 * PAIRS)],
        out_specs=[
            pl.BlockSpec((1, 2, ROWS, padded), lambda c, h, i: (c, h, i, 0)),
            query,
            query,
            query,
        ],
        out_shape=[
            jax.ShapeDtypeStruct((clips, HEADS, padded, padded), BF),
            jax.ShapeDtypeStruct((clips, padded, D), BF),
            jax.ShapeDtypeStruct((clips, padded, D), BF),
            jax.ShapeDtypeStruct((clips, padded, D), F32),
        ],
        scratch_shapes=[
            pltpu.VMEM((2, 128, padded), BF),
            pltpu.VMEM((padded, 256), BF),
            pltpu.SMEM((1,), F32),
        ],
        compiler_params=params(3),
        cost_estimate=cost(50e9, clips * padded * padded * 16),
        name="attention_forward",
    )(qkv, qkv, qkv)


def call_attend_back(clip, weights, grad, attended, low_part, inverse, qkv, earlier, token):
    clips, padded, _ = qkv.shape
    query = pl.BlockSpec((1, ROWS, 128), lambda h, i: (clip, i, h))
    keys = lambda at: pl.BlockSpec((1, padded, 128), lambda h, i: (clip, 0, at + h))
    shape = jax.ShapeDtypeStruct((clips, padded, D), BF)
    aliases = {}
    extra = []
    extra_specs = []
    if earlier is not None:
        extra = list(earlier)
        extra_specs = [pl.BlockSpec(memory_space=pl.ANY)] * 3
        aliases = {8: 0, 9: 1, 10: 2}
    kernel, operands, specs = ordered(
        functools.partial(attend_back_kernel, 0 if earlier is None else 1),
        [weights, grad, attended, low_part, inverse, qkv, qkv, qkv] + extra,
        [
            pl.BlockSpec((1, 2, ROWS, padded), lambda h, i: (clip, h, i, 0)),
            query, query, query, query, query, keys(PAIRS), keys(2 * PAIRS),
        ] + extra_specs,
        token,
    )
    return pl.pallas_call(
        kernel,
        grid=(PAIRS, padded // ROWS),
        in_specs=specs,
        out_specs=[query, keys(0), keys(0)],
        out_shape=[shape] * 3,
        scratch_shapes=[pltpu.VMEM((128, padded), F32)] * 2
        + [pltpu.VMEM((2, 256, padded), BF), pltpu.VMEM((2, ROWS, padded), BF)],
        input_output_aliases=aliases,
        compiler_params=params(2),
        cost_estimate=cost(40e9, padded * padded * 16),
        name="attention_backward",
    )(*operands)


def call_mlp(live, attended, stream, cot, w, vec, up_bias):
    clips, padded, _ = attended.shape
    row = pl.BlockSpec((1, ROWS, D), lambda i, c: (c, i, 0))
    return pl.pallas_call(
        functools.partial(mlp_kernel, cot.shape[1]),
        grid=(padded // ROWS, clips),
        in_specs=[SMEM, row, row, row, whole(w.shape), whole(vec.shape), whole(up_bias.shape)],
        out_specs=[
            pl.BlockSpec((ROWS * clips, D), lambda i, c: (i, 0)), row, row,
            whole((GROUPS, 9 * UNIT, D)), whole((8, D)), whole((8, FF)),
        ],
        out_shape=[
            jax.ShapeDtypeStruct((cot.shape[1] * clips, D), BF),
            jax.ShapeDtypeStruct(attended.shape, BF),
            jax.ShapeDtypeStruct(attended.shape, BF),
            jax.ShapeDtypeStruct((GROUPS, 9 * UNIT, D), BF),
            jax.ShapeDtypeStruct((8, D), F32),
            jax.ShapeDtypeStruct((8, FF), F32),
        ],
        scratch_shapes=[
            pltpu.VMEM((D, D), F32),
            pltpu.VMEM((FF // D, D, D), F32),
            pltpu.VMEM((FF // D, D, D), F32),
            pltpu.VMEM((D, D), BF),
            pltpu.VMEM((FF, D), BF),
            pltpu.VMEM((FF // D, D, D), BF),
            pltpu.VMEM((D // 128, ROWS * clips, 128), F32),
            pltpu.VMEM((ROWS, FF), BF),
            pltpu.VMEM((ROWS, FF), BF),
        ],
        compiler_params=params(2),
        cost_estimate=cost(60e9, clips * padded * 8000),
        name="mlp_both_ways",
    )(live, attended, stream, cot, w, vec, up_bias)


def call_qkv_back(grads, stream, state_grad, d_two, w, vec, token):
    clips, padded, _ = stream.shape
    row = pl.BlockSpec((1, ROWS, D), lambda c, i: (c, i, 0))
    kernel, operands, specs = ordered(
        qkv_back_kernel,
        [*grads, stream, state_grad, d_two, w, vec],
        [row] * 6 + [whole(w.shape), whole(vec.shape)],
        token,
    )
    return pl.pallas_call(
        kernel,
        grid=(clips, padded // ROWS),
        in_specs=specs,
        out_specs=[row, whole((GROUPS, 3 * UNIT, D)), whole((8, D))],
        out_shape=[
            jax.ShapeDtypeStruct(stream.shape, BF),
            jax.ShapeDtypeStruct((GROUPS, 3 * UNIT, D), BF),
            jax.ShapeDtypeStruct((8, D), F32),
        ],
        scratch_shapes=[pltpu.VMEM((3, D, D), F32), pltpu.VMEM((3, D, D), BF)],
        compiler_params=params(2),
        cost_estimate=cost(18e9, clips * padded * 9000),
        name="projection_backward",
    )(*operands)


def call_stem_back(second_grad, a_even, a_odd, d_even, d_odd, ce, co, w, sums, qkv_packed, token):
    clips, padded, _ = second_grad.shape
    last = padded // ROWS - 1
    row = lambda width: pl.BlockSpec((1, ROWS, width), lambda c, i: (c, last - i, 0))
    kernel, operands, specs = ordered(
        stem_back_kernel,
        [second_grad, a_even, a_odd, d_even, d_odd, ce, co, w, *sums, qkv_packed],
        [row(D)] * 5 + [row(256)] * 2 + [whole(w.shape)] + [whole((8, D))] * 3
        + [whole(qkv_packed.shape)],
        token,
    )
    return pl.pallas_call(
        kernel,
        grid=(clips, padded // ROWS),
        in_specs=specs,
        out_specs=[row(D), row(D), whole((GROUPS, 7 * UNIT, D))],
        out_shape=[
            jax.ShapeDtypeStruct(second_grad.shape, BF),
            jax.ShapeDtypeStruct(second_grad.shape, BF),
            jax.ShapeDtypeStruct((GROUPS, 7 * UNIT, D), BF),
        ],
        scratch_shapes=[
            pltpu.VMEM((3, D, D), F32),
            pltpu.VMEM((256, D), F32),
            pltpu.VMEM((ROWS + 8, D), F32),
            pltpu.VMEM((128, D), F32),
            pltpu.VMEM((3, D, D), BF),
        ],
        compiler_params=params(2),
        cost_estimate=cost(18e9, clips * padded * 9000),
        name="stem_backward",
    )(*operands)


def call_mel(spans, f_even, f_odd, w, frames, bins, token):
    clips, padded, _ = f_even.shape
    row = pl.BlockSpec((1, padded, D), lambda c: (c, 0, 0))
    kernel, operands, specs = ordered(
        functools.partial(mel_kernel, frames, bins),
        [spans, f_even, f_odd, w],
        [SMEM, row, row, whole(w.shape)],
        token,
    )
    return pl.pallas_call(
        kernel,
        grid=(clips,),
        in_specs=specs,
        out_specs=pl.BlockSpec((1, bins, frames), lambda c: (c, 0, 0)),
        out_shape=jax.ShapeDtypeStruct((clips, bins, frames), F32),
        scratch_shapes=[
            pltpu.VMEM((2 * D, D), BF),
            pltpu.VMEM((padded + 8, 128), F32),
            pltpu.VMEM((padded + 8, 128), F32),
            pltpu.VMEM((2 * padded, 128), F32),
        ],
        compiler_params=params(1),
        cost_estimate=cost(8e9, clips * padded * 4000),
        name="mel_backward",
    )(*operands)


def call_after(x, token):
    hold = pl.BlockSpec(memory_space=pl.ANY)

    def kernel(held, ready, passed):
        del held, ready, passed

    return pl.pallas_call(
        kernel,
        in_specs=[hold, pl.BlockSpec(token.shape, lambda: (0, 0))],
        out_specs=hold,
        out_shape=jax.ShapeDtypeStruct(x.shape, x.dtype),
        input_output_aliases={0: 0},
        name="after_stage",
    )(x, token)


def swap(x, mask, count):
    return lax.ppermute(x, "dp", [(i, i ^ mask) for i in range(count)])


def stages(count):
    bits = count.bit_length() - 1
    return [(0, 1)] + [(at, min(2, bits - at)) for at in range(1, bits, 2)]


def gather_xor(x, count, index, filler):
    held = x[None]
    where = jnp.zeros((count,), jnp.int32)
    apart = jnp.arange(count, dtype=jnp.int32) ^ index
    token = None
    parts = None
    for first, many in reversed(stages(count)):
        if parts is not None:
            if first == 0:
                parts[-1] = parts[-1] + filler
            held = jnp.concatenate(parts)
        where = where + ((apart >> first) & ((1 << many) - 1)) * held.shape[0]
        parts = [held] + [swap(held, rel << first, count) for rel in range(1, 1 << many)]
        if first > 0:
            token = parts[-1]
    return parts, where, token


class Scatter:
    def __init__(self, x, count, index):
        self.held, self.count, self.index = x, count, index
        self.plan = stages(count)

    def step(self):
        if not self.plan:
            return None
        first, many = self.plan.pop(0)
        radix = 1 << many
        held = self.held
        split = held.reshape((held.shape[0] // radix, radix) + held.shape[1:])
        mine = (self.index >> first) & (radix - 1)
        take = lambda at: lax.dynamic_index_in_dim(split, at, 1, keepdims=False)
        got = [swap(take(mine ^ rel), rel << first, self.count) for rel in range(1, radix)]
        total = take(mine).astype(F32)
        for piece in got:
            total = total + piece.astype(F32)
        self.held = total.astype(BF) if self.plan else total
        return total[0, :1, :128]

    def owned(self):
        while self.plan:
            self.step()
        return self.held[0]


def rows_of(gathered, first, parts, unit):
    taken = gathered[:, first * unit : (first + parts) * unit]
    return taken.reshape(GROUPS, parts * UNIT, gathered.shape[2])


def to_groups(gathered, pieces, unit):
    if unit == UNIT:
        return gathered
    out = []
    at = 0
    for parts in pieces:
        out.append(rows_of(gathered, at, parts, unit))
        at += parts
    return jnp.concatenate(out, axis=1)


def from_groups(packed, pieces, count):
    unit = D // count
    if unit == UNIT:
        return packed
    out = []
    at = 0
    for parts in pieces:
        piece = packed[:, at * UNIT : (at + parts) * UNIT]
        out.append(piece.reshape(count, parts * unit, D))
        at += parts
    return jnp.concatenate(out, axis=1)


def position_table(frames):
    half = D // 2
    rate = np.exp(-(math.log(10000.0) / (half - 1)) * np.arange(half, dtype=np.float64))
    angle = np.arange(frames, dtype=np.float64)[:, None] * rate[None, :]
    return np.concatenate([np.sin(angle), np.cos(angle)], axis=1).astype(np.float32)


def per_device(
    count, log_mels, mask_spans, live_slots, first_conv, second_conv, biases, norm_gains,
    qkv_weight, out_weight, up_weight, up_bias, down_weight, cotangent,
):
    clips, frames, bins = log_mels.shape
    length = frames // 2
    padded = -(-length // ROWS) * ROWS
    index = lax.axis_index("dp")
    unit = D // count
    tap_lanes = 3 * bins
    ups = FF // D

    small = jnp.concatenate(
        [
            first_conv.reshape(tap_lanes, unit).T,
            biases.T,
            norm_gains.T,
            up_bias.reshape(unit, ups),
            jnp.zeros((unit, D - tap_lanes - 10 - ups), BF),
        ],
        axis=1,
    )
    near = jnp.concatenate([small, second_conv.reshape(3 * unit, D)])
    col_even, col_odd = call_prepare(mask_spans, log_mels.transpose(0, 2, 1), padded)
    parts, order, token = gather_xor(near, count, index, col_even[0, padded - 1, 255])
    if unit != UNIT:
        near = jnp.take(jnp.concatenate(parts), order, axis=0)
        near = to_groups(near, (1,) * 4, unit)
        parts = (near[: GROUPS // 2], near[GROUPS // 2 :])
        order = jnp.arange(GROUPS, dtype=jnp.int32)
    qkv_w = qkv_weight.transpose(1, 0, 2).reshape(3 * unit, D)
    qkv_w = to_groups(lax.all_gather(qkv_w, "dp", axis=0, tiled=False), (1,) * 3, unit)
    far = jnp.concatenate(
        [
            out_weight,
            up_weight.reshape(unit, ups, D).transpose(1, 0, 2).reshape(ups * unit, D),
            down_weight,
        ]
    )
    far = far + token[0, 0, D - 1]
    far = lax.all_gather(far, "dp", axis=0, tiled=False)
    far = to_groups(far, (1,) * (1 + ups) + (ups,), unit)

    table = jnp.asarray(position_table(padded))
    a_even, a_odd, d_even, d_odd, d_two, stream, near, vec = call_stem(
        order, col_even, col_odd, table, *parts
    )
    qkv = call_project(stream, qkv_w, vec)
    up_row = jnp.pad(vec[10 : 10 + ups].T.reshape(1, FF), ((0, 7), (0, 0)))
    weights, attended, low_part, inverse = call_attend(qkv, length)
    encoded, att_grad, state_grad, mlp_packed, mlp_sums, up_sums = call_mlp(
        live_slots, attended, stream, cotangent, far, vec, up_row
    )
    mlp_packed = from_groups(mlp_packed, (1,) * (1 + ups) + (ups,), count)
    mlp_sum = Scatter(mlp_packed, count, index)
    up_cols = jnp.pad(up_sums[0].reshape(D, ups).T, ((0, 8 - ups), (0, 0)))
    grads = None
    for clip in range(clips):
        token = mlp_sum.step() if clip else None
        grads = call_attend_back(
            clip, weights, att_grad, attended, low_part, inverse, qkv, grads, token
        )
    second_grad, qkv_packed, qkv_sums = call_qkv_back(
        grads, stream, state_grad, d_two, qkv_w, vec, mlp_sum.step()
    )
    f_even, f_odd, stem_packed = call_stem_back(
        second_grad, a_even, a_odd, d_even, d_odd, col_even, col_odd, near,
        (qkv_sums, mlp_sums, up_cols), qkv_packed, mlp_sum.step(),
    )
    stem_sum = Scatter(from_groups(stem_packed, (1,) * 7, count), count, index)
    encoded = call_after(encoded, stem_sum.step())
    encoded = encoded.reshape(length, clips, D).transpose(1, 0, 2)
    token = encoded[0, 0:1, 0:128].astype(F32)
    mel_turned = call_mel(mask_spans, f_even, f_odd, near, frames, bins, token)
    mel_grad = mel_turned.transpose(0, 2, 1)
    mlp_owned, owned = mlp_sum.owned(), stem_sum.owned()
    stem_owned, qkv_owned = owned[: 4 * unit], owned[4 * unit :]

    mixed = stem_owned[:unit]
    bias_grad = mixed[:, tap_lanes : tap_lanes + 8].T
    return (
        encoded,
        mel_grad,
        mixed[:, :tap_lanes].T.reshape(3, bins, unit),
        stem_owned[unit : 4 * unit].reshape(3, unit, D),
        bias_grad,
        mixed[:, tap_lanes + 8 : tap_lanes + 10].T,
        qkv_owned.reshape(3, unit, D).transpose(1, 0, 2),
        mlp_owned[:unit],
        mlp_owned[unit : (1 + ups) * unit]
        .reshape(ups, unit, D)
        .transpose(1, 0, 2)
        .reshape(unit, FF),
        mixed[:, tap_lanes + 10 : tap_lanes + 10 + ups].reshape(ups * unit),
        mlp_owned[(1 + ups) * unit :],
        bias_grad[6],
    )


def solution(mesh):
    return jax.shard_map(
        functools.partial(per_device, mesh.shape["dp"]),
        mesh=mesh,
        in_specs=(
            P("dp", None, None),
            P("dp", None),
            P("dp"),
            P(None, None, "dp"),
            P(None, "dp", None),
            P(None, "dp"),
            P(None, "dp"),
            P("dp", None, None),
            P("dp", None),
            P("dp", None),
            P("dp"),
            P("dp", None),
            P("dp", None, None),
        ),
        out_specs=(
            P("dp", None, None),
            P("dp", None, None),
            P(None, None, "dp"),
            P(None, "dp", None),
            P(None, "dp"),
            P(None, "dp"),
            P("dp", None, None),
            P("dp", None),
            P("dp", None),
            P("dp"),
            P("dp", None),
            P("dp"),
        ),
        check_vma=False,
    )
```
